128 devices in a mesh: dp: 32 (over z, x, core), tensor: 4 (over y).
Axes of the slice: x: 4, y: 4, z: 4, core: 2. Of those that a mesh axis runs over, the one named last changes fastest.
Arguments:
- tokens: bfloat16 [32768, 1024], P(('dp', 'tensor')), may hold values from -6 to 6
- cotangent: bfloat16 [32768, 1024], P(('dp', 'tensor')), may hold values from -6 to 6
- gain_attn: float32 [1024], replicated, may hold values from 0.5 to 1.5
- w_query: bfloat16 [1024, 1024], P(None, 'tensor'), may hold values from -0.1875 to 0.1875
- key_projection_weight: bfloat16 [1024, 512], P(None, 'tensor'), may hold values from -0.1875 to 0.1875
- value_projection_weight: bfloat16 [1024, 512], P(None, 'tensor'), may hold values from -0.1875 to 0.1875
- w_out: bfloat16 [1024, 1024], P('tensor'), may hold values from -1.5 to 1.5
- gain_moe: float32 [1024], replicated, may hold values from 0.5 to 1.5
- w_router: bfloat16 [1024, 32], replicated, may hold values from -0.09375 to 0.09375
- w_gate: bfloat16 [32, 1024, 512], P('dp', None, 'tensor'), may hold values from -0.1875 to 0.1875
- w_up: bfloat16 [32, 1024, 512], P('dp', None, 'tensor'), may hold values from -0.1875 to 0.1875
- w_down: bfloat16 [32, 512, 1024], P('dp', 'tensor'), may hold values from -1.5 to 1.5
- routes: int32 [32768, 8], P(('dp', 'tensor')), may hold values from 0 to 31, all different within a row; in each aligned block of 256 rows (0 to 255, 256 to 511, ...) at most 96 rows name the same one
- owner_map: int32 [32], replicated, may hold values from 0 to 31, each once
Outputs:
- mixed_out: bfloat16 [32768, 1024], P(('dp', 'tensor'))
- d_tokens: float32 [32768, 1024], P(('dp', 'tensor'))
- g_gain_attn: float32 [1024], replicated
- g_query: float32 [1024, 1024], P(None, 'tensor')
- g_key: float32 [1024, 512], P(None, 'tensor')
- g_value: float32 [1024, 512], P(None, 'tensor')
- g_out: float32 [1024, 1024], P('tensor')
- g_gain_moe: float32 [1024], replicated
- g_router: float32 [1024, 32], replicated
- g_gate: float32 [32, 1024, 512], P('dp', None, 'tensor')
- g_up: float32 [32, 1024, 512], P('dp', None, 'tensor')
- g_down: float32 [32, 512, 1024], P('dp', 'tensor')
The draws below stay inside these ranges and needn't reach their ends.
Inputs may be any that keep to these rules, and one draw needn't show every extreme that they name: `routes`: each row names 8 different experts. Within the rows of one device no expert is named more than 96 times, and in some devices' rows one expert is named exactly 96 times. Each value once: expert e uses slot owner_map[e] of w_gate, w_up and w_down.
All inputs are finite; a program needn't handle non-finite values.
Results may differ from the reference program's by a relative error of at most 0.025.
Values may be sent and summed in bfloat16 or wider, within the bound.
No kernel may reach another device: no remote copies, remote signals or barrier semaphores. Data moves between devices by JAX's collectives and lax.ppermute only.
A program may use at most 192 MiB of HBM per device.

```python
import math
import jax
import jax.numpy as jnp
import numpy as np
from jax import lax

MODEL_DIM = 1024
QUERY_HEADS = 16
KEY_VALUE_HEADS = 8
HEAD_DIM = 64
FF = 512
EXPERTS = 32
TOP = 8
SEQUENCE_LENGTH = 1024
TOK_DEV = 256
TOKEN_TOTAL = 32768
CAP = 96
N_DP = 32
N_TENSOR = 4


def block_scale(own_key, dims, shards, least, largest):
    factor_of, own = 1.0, jax.random.fold_in(own_key, 6)
    for dim, parts in shards:
        draws = jnp.exp(jax.random.uniform(jax.random.fold_in(own, dim), (parts,), jnp.float32, least / len(shards), largest / len(shards)))
        factor_of = factor_of * jnp.repeat(draws, dims[dim] // parts).reshape([-1 if axis == dim else 1 for axis in range(len(dims))])
    return factor_of


def assign_block(own_key, own, number, rows, number_of, top, most, skew):
    order = jax.random.permutation(own_key, number_of)
    crowded, usual = shares(number_of, rows * top, most, skew, True), shares(number_of, rows * top, most, skew, False)
    places = jnp.arange(number_of)

    def named(sizes, rotation):
        used = int((sizes > 0).sum())
        fixed = max(1, used // 4)
        shifted = fixed + (places - fixed + rotation * (used - fixed)) % max(1, number_of - fixed)
        return jnp.zeros((number_of,), jnp.int32).at[order[jnp.where(places < fixed, places, shifted)]].set(jnp.asarray(sizes, jnp.int32))

    sizes = jnp.where(number % 4 == 0, named(crowded, number // 4), named(usual, number - number // 4 - 1))
    mixed = jax.random.permutation(jax.random.fold_in(own, 3), number_of)
    donor, sink = mixed[0:number_of // 2 * 2:2], mixed[1:number_of // 2 * 2:2]
    room = jnp.minimum(sizes[donor] - 1, most - sizes[sink]) // 2
    room = jnp.where((donor == order[0]) | (sink == order[0]) | (sizes[sink] == 0), 0, jnp.maximum(room, 0))
    shifted = jax.random.randint(jax.random.fold_in(own, 4), (number_of // 2,), 0, 1 << 20) % (room + 1)
    sizes = sizes.at[donor].add(-shifted).at[sink].add(shifted)
    members = jnp.searchsorted(jnp.cumsum(sizes), jnp.arange(rows * top), side="right").astype(jnp.int32)
    grid = members.reshape(top, rows).T
    grid = grid[jax.random.permutation(jax.random.fold_in(own, 1), rows)]
    rotation = jax.random.randint(jax.random.fold_in(own, 2), (rows, 1), 0, top)
    return jnp.take_along_axis(grid, (jnp.arange(top)[None, :] + rotation) % top, axis=1)


def shares(count, total, bound, skew, full):
    portions = [(1 << 20) // math.isqrt(standing ** skew) + 1 for standing in range(1, count + 1)]
    largest = bound if full else min(bound, max(-(-total // count), total * portions[0] // sum(portions)))
    least = 1 if total - largest >= count - 1 else 0
    given, surplus = [largest] + [least] * (count - 1), total - largest - least * (count - 1)
    while surplus > 0:
        free = [i for i in range(1, count) if given[i] < largest] or [i for i in range(1, count) if given[i] < bound]
        mass, remaining = sum([portions[i] for i in free]), surplus
        for i in free:
            more = min(bound - given[i], max(1, remaining * portions[i] // mass), surplus)
            given[i] = given[i] + more
            surplus = surplus - more
    return np.array(given)


def gaussian(own_key, dims, width, most, cuts=(), held_as=jnp.bfloat16):
    drawn = width * jax.random.normal(own_key, dims, jnp.float32)
    if cuts:
        drawn = drawn * block_scale(own_key, dims, cuts, -0.22, 0.18)
    return jnp.clip(drawn, -most, most).astype(held_as)


def setup_inputs(seed: int = 0) -> dict:
    key_list = jax.random.split(jax.random.key(seed), 15)
    tokens = gaussian(key_list[0], (TOKEN_TOTAL, MODEL_DIM), 1.0, 6.0, ((0, 128),))
    cotangent = gaussian(key_list[1], (TOKEN_TOTAL, MODEL_DIM), 1.0, 6.0, ((0, 128),))
    gain_attn = jnp.clip(1.0 + 0.1 * jax.random.normal(key_list[2], (MODEL_DIM,), jnp.float32), 0.5, 1.5)
    w_query = gaussian(key_list[3], (MODEL_DIM, QUERY_HEADS * HEAD_DIM), MODEL_DIM ** -0.5, 0.1875, ((1, 4),))
    key_projection_weight = gaussian(key_list[4], (MODEL_DIM, KEY_VALUE_HEADS * HEAD_DIM), MODEL_DIM ** -0.5, 0.1875, ((1, 4),))
    value_projection_weight = gaussian(key_list[5], (MODEL_DIM, KEY_VALUE_HEADS * HEAD_DIM), MODEL_DIM ** -0.5, 0.1875, ((1, 4),))
    w_out = gaussian(key_list[6], (QUERY_HEADS * HEAD_DIM, MODEL_DIM), (QUERY_HEADS * HEAD_DIM // 64) ** -0.5, 1.5, ((0, 4),))
    gain_moe = jnp.clip(1.0 + 0.1 * jax.random.normal(key_list[7], (MODEL_DIM,), jnp.float32), 0.5, 1.5)
    w_router = gaussian(key_list[8], (MODEL_DIM, EXPERTS), (4 * MODEL_DIM) ** -0.5, 0.09375)
    w_gate = gaussian(key_list[9], (EXPERTS, MODEL_DIM, FF), MODEL_DIM ** -0.5, 0.1875, ((0, 32), (2, 4)))
    w_up = gaussian(key_list[10], (EXPERTS, MODEL_DIM, FF), MODEL_DIM ** -0.5, 0.1875, ((0, 32), (2, 4)))
    w_down = gaussian(key_list[11], (EXPERTS, FF, MODEL_DIM), (FF // 32) ** -0.5, 1.5, ((0, 32), (1, 4)))
    routes_keys = jax.random.split(jax.random.fold_in(key_list[12], 1), TOKEN_TOTAL // TOK_DEV)
    routes_turns = jax.random.permutation(jax.random.fold_in(key_list[12], 3), TOKEN_TOTAL // TOK_DEV)
    routes = jax.vmap(lambda own, number: assign_block(jax.random.fold_in(key_list[12], 2), own, number, TOK_DEV, EXPERTS, TOP, CAP, 1))(routes_keys, routes_turns).reshape((TOKEN_TOTAL, TOP))
    owner_map = jax.random.permutation(key_list[13], EXPERTS).astype(jnp.int32)
    return dict(tokens=tokens, cotangent=cotangent, gain_attn=gain_attn, w_query=w_query, key_projection_weight=key_projection_weight, value_projection_weight=value_projection_weight, w_out=w_out, gain_moe=gain_moe, w_router=w_router, w_gate=w_gate, w_up=w_up, w_down=w_down, routes=routes, owner_map=owner_map)


@jax.custom_vjp
def lower_precision(v):
    return lax.optimization_barrier(v.astype(jnp.bfloat16)).astype(jnp.float32)

@jax.custom_vjp
def lower_precision_backward(v):
    return v

def low_keep(v):
    return (lower_precision(v), None)

def low_pass(kept, grad):
    return (grad,)

def back_keep(v):
    return (v, None)

def back_low(kept, grad):
    return (lower_precision(grad),)
lower_precision.defvjp(low_keep, low_pass)
lower_precision_backward.defvjp(back_keep, back_low)
norm_eps = 1e-05
highest_precision = lax.Precision.HIGHEST

def rms_norm(values, gain_vec):
    return values * lax.rsqrt(lax.optimization_barrier(jnp.mean(values * values, axis=-1, keepdims=True)) + norm_eps) * gain_vec

def rotary_embedding(values, seq_length):
    row_count, head_count, head_size = values.shape
    half_size = head_size // 2
    steps_f = jnp.arange(half_size).astype(values.dtype)
    inv_freq = jnp.exp(steps_f * (-2.0 * math.log(10000.0) / head_size))
    positions = (jnp.arange(row_count) % seq_length).astype(values.dtype)
    angles = positions[:, None] * inv_freq[None, :]
    cosine = jnp.concatenate([jnp.cos(angles), jnp.cos(angles)], axis=1)[:, None, :]
    sine = jnp.concatenate([jnp.sin(angles), jnp.sin(angles)], axis=1)[:, None, :]
    turned = jnp.concatenate([-values[..., half_size:], values[..., :half_size]], axis=-1)
    return values * cosine + turned * sine

def attend_one_sequence(block_in):
    query_seq, key_seq, value_seq = block_in
    seq_length, query_heads, head_size = query_seq.shape
    kv_heads = key_seq.shape[1]
    grouped = query_seq.reshape(seq_length, kv_heads, query_heads // kv_heads, head_size)
    raw_scores = lower_precision_backward(jnp.einsum('qhgd,khd->hgqk', grouped, key_seq, precision=highest_precision))
    scaled = raw_scores * head_size ** (-0.5)
    causal = jnp.arange(seq_length)[None, :] <= jnp.arange(seq_length)[:, None]
    masked = jnp.where(causal, scaled, -jnp.inf)
    row_peak = lax.optimization_barrier(jnp.max(masked, axis=-1, keepdims=True))
    exp_scores = jnp.exp(masked - row_peak)
    attn_probs = lower_precision(exp_scores / lax.optimization_barrier(jnp.sum(exp_scores, axis=-1, keepdims=True)))
    mixed_heads = jnp.einsum('hgqk,khd->qhgd', attn_probs, value_seq, precision=highest_precision)
    return mixed_heads.reshape(seq_length, query_heads * head_size)

def reference(tokens, cotangent, gain_attn, w_query, key_projection_weight, value_projection_weight, w_out, gain_moe, w_router, w_gate, w_up, w_down, routes, owner_map):
    route_count = TOKEN_TOTAL * TOP
    max_rows = N_DP * N_TENSOR * CAP
    flat_experts = routes.reshape(-1).astype(jnp.int32)
    slot_hits = flat_experts[None, :] == jnp.arange(EXPERTS, dtype=jnp.int32)[:, None]
    slot_ranks = jnp.cumsum(slot_hits.astype(jnp.int32), axis=1) - 1
    targets = jnp.where(slot_hits, slot_ranks, max_rows).astype(jnp.int32)
    route_table = jnp.full((EXPERTS, max_rows + 1), route_count, jnp.int32)
    route_ids_all = jnp.broadcast_to(jnp.arange(route_count, dtype=jnp.int32)[None, :], targets.shape)
    route_table = route_table.at[jnp.arange(EXPERTS, dtype=jnp.int32)[:, None], targets].set(route_ids_all)[:, :max_rows]
    slot_list = owner_map.astype(jnp.int32)

    def forward(tokens_f, gain_a, query_w, key_matrix, value_w, out_w, gain_m, router_w, gate_w, up_w, down_w):
        attention_normed_input = lower_precision(rms_norm(tokens_f, gain_a))
        query_rows_full = lower_precision(rotary_embedding(lower_precision_backward(jnp.dot(attention_normed_input, query_w, precision=highest_precision)).reshape(TOKEN_TOTAL, QUERY_HEADS, HEAD_DIM), SEQUENCE_LENGTH))
        key_rows_full = lower_precision(rotary_embedding(lower_precision_backward(jnp.dot(attention_normed_input, key_matrix, precision=highest_precision)).reshape(TOKEN_TOTAL, KEY_VALUE_HEADS, HEAD_DIM), SEQUENCE_LENGTH))
        value_rows_full = lower_precision(lower_precision_backward(jnp.dot(attention_normed_input, value_w, precision=highest_precision)))
        sequence_total = TOKEN_TOTAL // SEQUENCE_LENGTH
        attention_output = lax.map(jax.checkpoint(attend_one_sequence), (query_rows_full.reshape(sequence_total, SEQUENCE_LENGTH, QUERY_HEADS, HEAD_DIM), key_rows_full.reshape(sequence_total, SEQUENCE_LENGTH, KEY_VALUE_HEADS, HEAD_DIM), value_rows_full.reshape(sequence_total, SEQUENCE_LENGTH, KEY_VALUE_HEADS, HEAD_DIM)))
        attention_output = lower_precision_backward(lower_precision(attention_output.reshape(TOKEN_TOTAL, QUERY_HEADS * HEAD_DIM)))
        hidden = tokens_f + lower_precision_backward(jnp.dot(attention_output, out_w, precision=highest_precision))
        normed_m = lower_precision(rms_norm(hidden, gain_m))
        logits = lower_precision_backward(jnp.dot(normed_m, router_w, precision=highest_precision))
        chosen = jnp.take_along_axis(logits, routes.astype(jnp.int32), axis=1)
        chosen_peak = lax.optimization_barrier(jnp.max(chosen, axis=-1, keepdims=True))
        chosen_exp = jnp.exp(chosen - chosen_peak)
        route_gates = chosen_exp / lax.optimization_barrier(jnp.sum(chosen_exp, axis=-1, keepdims=True))
        gate_flat = jnp.concatenate([route_gates.reshape(-1), jnp.zeros((1,), route_gates.dtype)])
        padded_rows = jnp.concatenate([normed_m, jnp.zeros((1, MODEL_DIM), normed_m.dtype)], axis=0)

        def expert_step(summed_rows, step_in):
            route_ids, slot_id = step_in
            token_ids = route_ids // TOP
            expert_rows = lower_precision_backward(padded_rows[token_ids])
            gate_pre = lower_precision_backward(jnp.dot(expert_rows, gate_w[slot_id], precision=highest_precision))
            up_pre = lower_precision_backward(jnp.dot(expert_rows, up_w[slot_id], precision=highest_precision))
            act_values = lower_precision(gate_pre * jax.nn.sigmoid(gate_pre) * up_pre)
            expert_out = lower_precision_backward(lower_precision(jnp.dot(act_values, down_w[slot_id], precision=highest_precision)))
            summed_rows = summed_rows.at[token_ids].add(expert_out * gate_flat[route_ids][:, None])
            return (summed_rows, None)
        start_rows = jnp.zeros((TOKEN_TOTAL + 1, MODEL_DIM), hidden.dtype)
        moe_rows, unused = lax.scan(jax.checkpoint(expert_step), start_rows, (route_table, slot_list))
        return hidden + moe_rows[:TOKEN_TOTAL]
    float_args = tuple((array_in.astype(jnp.float32) for array_in in (tokens, gain_attn, w_query, key_projection_weight, value_projection_weight, w_out, gain_moe, w_router, w_gate, w_up, w_down)))
    mixed_out, pull_back = jax.vjp(forward, *float_args)
    all_grads = pull_back(cotangent.astype(jnp.float32))
    return (mixed_out.astype(jnp.bfloat16), all_grads[0], all_grads[1], all_grads[2], all_grads[3], all_grads[4], all_grads[5], all_grads[6], all_grads[7], all_grads[8], all_grads[9], all_grads[10])
```

```python
import functools
import math

import jax
import jax.numpy as jnp
from jax import lax
from jax.experimental import pallas as pl
from jax.experimental.pallas import tpu as pltpu
from jax.sharding import PartitionSpec as P

BF = jnp.bfloat16
F32 = jnp.float32
NORM_EPS = 1e-05
HEAD = 64
SEQ = 1024
ROWS = 256
WIDTH = 1024
HALF = 512
FF = 512
SLOTS = 32
CAP = 96
VMEM = 58 * 1024 * 1024

NN = (((1,), (0,)), ((), ()))
NT = (((1,), (1,)), ((), ()))
TN = (((0,), (0,)), ((), ()))


def mm(a, b, dims=NN):
    return lax.dot_general(a, b, dims, preferred_element_type=F32)


def _dp_pairs(dz, dx, dc):
    pairs = []
    for z in range(4):
        for x in range(4):
            for c in range(2):
                src = ((z + dz) % 4) * 8 + ((x + dx) % 4) * 2 + (c + dc) % 2
                pairs.append((src, z * 8 + x * 2 + c))
    return pairs


def from_z(v, d):
    return lax.ppermute(v, "dp", _dp_pairs(d, 0, 0))


def from_x(v, d):
    return lax.ppermute(v, "dp", _dp_pairs(0, d, 0))


def from_core(v):
    return lax.ppermute(v, "dp", _dp_pairs(0, 0, 1))


def from_y(v, d):
    return lax.ppermute(v, "tensor", [((i + d) % 4, i) for i in range(4)])


def low(v):
    return v.astype(BF)


def wide(v):
    return v.astype(F32)


def ring_gather(own, get):
    half = own.shape[0] // 2
    plus, minus = get(own, 1), get(own, -1)
    far = jnp.concatenate([get(plus[:half], 1), get(minus[half:], -1)], axis=0)
    return plus, far, minus


def ring_sum(blocks, get):
    own, plus, far, minus = blocks
    half = own.shape[0] // 2
    far_low, far_high = get(far[:half], -1), get(far[half:], 1)
    to_plus = jnp.concatenate([low(wide(plus[:half]) + wide(far_low)), plus[half:]], axis=0)
    to_minus = jnp.concatenate([minus[:half], low(wide(minus[half:]) + wide(far_high))], axis=0)
    return wide(own) + wide(get(to_plus, -1)) + wide(get(to_minus, 1))


def gather_direct(own, get):
    half = own.shape[0] // 2
    return get(own, 1), get(own[:half], 2), get(own[half:], -2), get(own, -1)


def sum_direct(own, plus, far_low, far_high, minus, get):
    far = jnp.concatenate([get(far_low, 2), get(far_high, -2)], axis=0)
    return wide(own) + wide(get(plus, -1)) + wide(get(minus, 1)) + wide(far)


def plane_gather(rows):
    a, b = rows[None, :, :HALF], rows[None, :, HALF:]

    def ring4(v, get):
        plus, minus = get(v, 1), get(v, -1)
        cut = ROWS // 2
        far = jnp.concatenate([get(plus[:, :cut], 1), get(minus[:, cut:], -1)], axis=1)
        return jnp.concatenate([v, plus, far, minus], axis=0)

    a4, b4 = ring4(a, from_z), ring4(b, from_x)
    return (a4, *ring_gather(a4, from_x)), (b4, *ring_gather(b4, from_z))


def plane_sum(a_blocks, b_blocks):
    sa = low(ring_sum(a_blocks, from_x))
    sb = low(ring_sum(b_blocks, from_z))
    ra = ring_sum([sa[i] for i in range(4)], from_z)
    rb = ring_sum([sb[i] for i in range(4)], from_x)
    return jnp.concatenate([ra, rb], axis=1)


def ring_position(dp):
    return dp // 8, (dp // 2) % 4, dp % 2


def dp_sum(v, dp):
    _, x, c = ring_position(dp)
    half = v.shape[0] // 2
    part = half // 4
    keep = lax.dynamic_slice_in_dim(v, c * half, half, 0)
    send = lax.dynamic_slice_in_dim(v, (1 - c) * half, half, 0)
    s = low(wide(keep) + wide(from_core(send)))
    b = [lax.dynamic_slice_in_dim(s, ((x + r) % 4) * part, part, 0) for r in range(4)]
    s = low(sum_direct(b[0], b[1], b[2][: part // 2], b[2][part // 2 :], b[3], from_x))
    p, fl, fh, m = gather_direct(s, from_z)
    s = low(wide(s) + wide(p) + wide(m) + jnp.concatenate([wide(fl), wide(fh)], axis=0))
    p, fl, fh, m = gather_direct(s, from_x)
    whole = jnp.concatenate([s, p, fl, fh, m], axis=0)
    whole = jnp.concatenate([whole, whole], axis=0)
    whole = lax.dynamic_slice_in_dim(whole, ((4 - x) % 4) * part, half, 0)
    other = from_core(whole)
    return jnp.where(
        c == 0,
        jnp.concatenate([whole, other], axis=0),
        jnp.concatenate([other, whole], axis=0),
    )


def tensor_sum(v):
    return v + from_y(v, 1) + from_y(v, 2) + from_y(v, 3)


def _block_starts(y):
    starts = []
    for r in range(4):
        off = lax.rem(y + r, 4) * ROWS
        if r == 2:
            starts += [off, off + ROWS // 2]
        else:
            starts.append(off)
    return [pl.multiple_of(s, 128) for s in starts]


def attention_forward_kernel(
    y_ref, n0, n1, n2, n3, n4, w_ref, wo_ref, cos_ref, sin_ref,
    qkv_ref, o_ref, lse_ref, p0, p1, p2, p3, p4,
):
    starts = _block_starts(y_ref[0])
    for start, ref in zip(starts, (n0, n1, n2, n3, n4)):
        width = ref.shape[0]
        at = pl.ds(start, width)
        t = mm(w_ref[...], ref[...], NT)
        cos, sin = cos_ref[:, at], sin_ref[:, at]
        for h in range(6):
            a, b = t[64 * h : 64 * h + 32], t[64 * h + 32 : 64 * h + 64]
            ra, rb = a * cos - b * sin, b * cos + a * sin
            if h < 4:
                ra, rb = ra * 0.125, rb * 0.125
            qkv_ref[64 * h : 64 * h + 32, at] = low(ra)
            qkv_ref[64 * h + 32 : 64 * h + 64, at] = low(rb)
        qkv_ref[384:512, at] = low(t[384:])
    key_at = lax.broadcasted_iota(jnp.int32, (ROWS, 2 * ROWS), 0)
    query_at = lax.broadcasted_iota(jnp.int32, (ROWS, 2 * ROWS), 1)
    allowed = key_at <= jnp.bitwise_and(query_at, ROWS - 1)
    for g in range(2):
        keys = qkv_ref[256 + 64 * g : 320 + 64 * g, :].T
        values = qkv_ref[384 + 64 * g : 448 + 64 * g, :]
        for i in range(4):
            here = slice(i * ROWS, (i + 1) * ROWS)
            q2 = jnp.concatenate(
                [qkv_ref[128 * g : 128 * g + 64, here], qkv_ref[128 * g + 64 : 128 * g + 128, here]],
                axis=1,
            )
            tiles = []
            for j in range(i + 1):
                s = mm(keys[j * ROWS : (j + 1) * ROWS], q2)
                if j == i:
                    s = jnp.where(allowed, s, -jnp.inf)
                tiles.append(s)
            peak = tiles[0].max(axis=0, keepdims=True)
            for s in tiles[1:]:
                peak = jnp.maximum(peak, s.max(axis=0, keepdims=True))
            total = jnp.zeros_like(peak)
            mixed = jnp.zeros((HEAD, 2 * ROWS), F32)
            for j, s in enumerate(tiles):
                e = jnp.exp(s - peak)
                total = total + e.sum(axis=0, keepdims=True)
                mixed = mixed + mm(values[:, j * ROWS : (j + 1) * ROWS], low(e))
            mixed = mixed / total
            lse = peak + jnp.log(total)
            o_ref[128 * g : 128 * g + 64, here] = mixed[:, :ROWS]
            o_ref[128 * g + 64 : 128 * g + 128, here] = mixed[:, ROWS:]
            lse_ref[2 * g : 2 * g + 1, here] = lse[:, :ROWS]
            lse_ref[2 * g + 1 : 2 * g + 2, here] = lse[:, ROWS:]
    lse_ref[4:8, :] = jnp.zeros((4, SEQ), F32)
    for start, ref in zip(starts, (p0, p1, p2, p3, p4)):
        att = low(o_ref[:, pl.ds(start, ref.shape[0])])
        ref[...] = low(mm(att.T, wo_ref[...]))


PIECES = (ROWS, ROWS, ROWS // 2, ROWS // 2, ROWS)


def attention_forward(y, blocks, w_t, w_out, cos, sin):
    smem = pl.BlockSpec(memory_space=pltpu.SMEM)
    vmem = pl.BlockSpec(memory_space=pltpu.VMEM)
    return pl.pallas_call(
        attention_forward_kernel,
        out_shape=(
            jax.ShapeDtypeStruct((512, SEQ), BF),
            jax.ShapeDtypeStruct((256, SEQ), F32),
            jax.ShapeDtypeStruct((8, SEQ), F32),
            *[jax.ShapeDtypeStruct((w, WIDTH), BF) for w in PIECES],
        ),
        in_specs=[smem] + [vmem] * 9,
        out_specs=[vmem] * 8,
        compiler_params=pltpu.CompilerParams(vmem_limit_bytes=VMEM),
        cost_estimate=pl.CostEstimate(flops=8_000_000_000, bytes_accessed=10_000_000, transcendentals=3_000_000),
        name="attention_forward",
    )(y, *blocks, w_t, w_out, cos, sin)


def out_gradient_kernel(y_ref, d0, d1, d2, d3, d4, o_ref, g_ref):
    total = jnp.zeros((256, WIDTH), F32)
    for start, ref in zip(_block_starts(y_ref[0]), (d0, d1, d2, d3, d4)):
        total = total + mm(low(o_ref[:, pl.ds(start, ref.shape[0])]), ref[...])
    g_ref[...] = low(total)


def out_gradient(y, blocks, o):
    smem = pl.BlockSpec(memory_space=pltpu.SMEM)
    vmem = pl.BlockSpec(memory_space=pltpu.VMEM)
    return pl.pallas_call(
        out_gradient_kernel,
        out_shape=jax.ShapeDtypeStruct((256, WIDTH), BF),
        in_specs=[smem] + [vmem] * 6,
        out_specs=vmem,
        compiler_params=pltpu.CompilerParams(vmem_limit_bytes=VMEM),
        cost_estimate=pl.CostEstimate(flops=540_000_000, bytes_accessed=4_000_000, transcendentals=0),
        name="out_gradient",
    )(y, *blocks, o)


def attention_backward_kernel(
    g, y_ref, d0, d1, d2, d3, d4, x0, x1, x2, x3, x4, qkv_ref, o_ref, lse_ref, wo_ref, cos_ref, sin_ref,
    dqkv_ref, gw_ref, do_ref, delta_ref, dk_ref, dv_ref,
):
    starts = _block_starts(y_ref[0])
    heads = slice(128 * g, 128 * g + 128)
    for start, ref in zip(starts, (d0, d1, d2, d3, d4)):
        do_ref[:, pl.ds(start, ref.shape[0])] = low(mm(wo_ref[heads, :], ref[...], NT))
    prod = o_ref[heads, :] * wide(do_ref[...])
    delta_ref[0:1, :] = prod[:64].sum(axis=0, keepdims=True)
    delta_ref[1:2, :] = prod[64:].sum(axis=0, keepdims=True)
    keys_t = qkv_ref[256 + 64 * g : 320 + 64 * g, :]
    keys = keys_t.T
    values = qkv_ref[384 + 64 * g : 448 + 64 * g, :].T
    dk_ref[...] = jnp.zeros_like(dk_ref)
    dv_ref[...] = jnp.zeros_like(dv_ref)
    key_at = lax.broadcasted_iota(jnp.int32, (ROWS, 2 * ROWS), 0)
    query_at = lax.broadcasted_iota(jnp.int32, (ROWS, 2 * ROWS), 1)
    allowed = key_at <= jnp.bitwise_and(query_at, ROWS - 1)
    for i in range(4):
        here = slice(i * ROWS, (i + 1) * ROWS)

        def pair(ref, base, step):
            return jnp.concatenate(
                [ref[base : base + step, here], ref[base + step : base + 2 * step, here]], axis=1
            )

        q2 = pair(qkv_ref, 128 * g, 64)
        do2 = pair(do_ref, 0, 64)
        lse2 = pair(lse_ref, 2 * g, 1)
        delta2 = pair(delta_ref, 0, 1)
        dq = jnp.zeros((HEAD, 2 * ROWS), F32)
        for j in range(i + 1):
            at = slice(j * ROWS, (j + 1) * ROWS)
            s = mm(keys[at], q2)
            p = jnp.exp(s - lse2)
            if j == i:
                p = jnp.where(allowed, p, 0.0)
            dp = mm(values[at], do2)
            ds = low(p * (dp - delta2))
            dq = dq + mm(keys_t[:, at], ds)
            dk_ref[:, at] += mm(q2, ds, NT)
            dv_ref[:, at] += mm(do2, low(p), NT)
        cos, sin = cos_ref[:, here], sin_ref[:, here]
        dq = dq * 0.125
        for h in range(2):
            a, b = dq[:32, h * ROWS : (h + 1) * ROWS], dq[32:, h * ROWS : (h + 1) * ROWS]
            dqkv_ref[64 * h : 64 * h + 32, here] = low(a * cos + b * sin)
            dqkv_ref[64 * h + 32 : 64 * h + 64, here] = low(b * cos - a * sin)
    a, b = dk_ref[:32, :], dk_ref[32:, :]
    dqkv_ref[128:160, :] = low(a * cos_ref[...] + b * sin_ref[...])
    dqkv_ref[160:192, :] = low(b * cos_ref[...] - a * sin_ref[...])
    dqkv_ref[192:256, :] = low(dv_ref[...])
    total = jnp.zeros((256, WIDTH), F32)
    for start, ref in zip(starts, (x0, x1, x2, x3, x4)):
        total = total + mm(dqkv_ref[:, pl.ds(start, ref.shape[0])], ref[...])
    gw_ref[...] = low(total)


def attention_backward(g, y, d_blocks, x_blocks, qkv, o, lse, w_out, cos, sin):
    smem = pl.BlockSpec(memory_space=pltpu.SMEM)
    vmem = pl.BlockSpec(memory_space=pltpu.VMEM)
    return pl.pallas_call(
        functools.partial(attention_backward_kernel, g),
        out_shape=(
            jax.ShapeDtypeStruct((256, SEQ), BF),
            jax.ShapeDtypeStruct((256, WIDTH), BF),
        ),
        in_specs=[smem] + [vmem] * 16,
        out_specs=[vmem] * 2,
        scratch_shapes=[
            pltpu.VMEM((128, SEQ), BF),
            pltpu.VMEM((8, SEQ), F32),
            pltpu.VMEM((64, SEQ), F32),
            pltpu.VMEM((64, SEQ), F32),
        ],
        compiler_params=pltpu.CompilerParams(vmem_limit_bytes=VMEM),
        cost_estimate=pl.CostEstimate(flops=9_000_000_000, bytes_accessed=10_000_000, transcendentals=1_500_000),
        name="attention_backward",
    )(y, *d_blocks, *x_blocks, qkv, o, lse, w_out, cos, sin)


def input_gradient_kernel(y_ref, a_ref, b_ref, wa_ref, wb_ref, p0, p1, p2, p3, p4):
    for start, ref in zip(_block_starts(y_ref[0]), (p0, p1, p2, p3, p4)):
        at = pl.ds(start, ref.shape[0])
        ref[...] = low(mm(a_ref[:, at].T, wa_ref[...]) + mm(b_ref[:, at].T, wb_ref[...]))


def input_gradient(y, d0, d1, w0, w1):
    smem = pl.BlockSpec(memory_space=pltpu.SMEM)
    vmem = pl.BlockSpec(memory_space=pltpu.VMEM)
    return pl.pallas_call(
        input_gradient_kernel,
        out_shape=tuple(jax.ShapeDtypeStruct((w, WIDTH), BF) for w in PIECES),
        in_specs=[smem] + [vmem] * 4,
        out_specs=[vmem] * 5,
        compiler_params=pltpu.CompilerParams(vmem_limit_bytes=VMEM),
        cost_estimate=pl.CostEstimate(flops=1_100_000_000, bytes_accessed=5_000_000, transcendentals=0),
        name="input_gradient",
    )(y, d0, d1, w0, w1)


def expert_kernel(
    slot_ref, ta, tb0, tb1, tb2, tb3, ca, cb0, cb1, cb2, cb3, pos_ref, hot_ref, wr_ref, wgu_ref, wd_ref,
    x_ref, dx_ref, act_ref, dgu_ref, dia, dib0, dib1, dib2, dib3, oa, ob0, ob1, ob2, ob3, dr_ref,
    g_scr, m_scr, y_scr, p_scr,
):
    tb, cb, dib, ob = (tb0, tb1, tb2, tb3), (cb0, cb1, cb2, cb3), (dib0, dib1, dib2, dib3), (ob0, ob1, ob2, ob3)
    place = wide(lax.broadcasted_iota(jnp.int32, (CAP, ROWS), 0))
    lane = lax.broadcasted_iota(jnp.int32, (4 * CAP, SLOTS), 1)
    for k in range(4):
        tok = jnp.concatenate([ta[0, k], tb[k][0]], axis=1)
        cot = jnp.concatenate([ca[0, k], cb[k][0]], axis=1)
        pick = jnp.concatenate([low(wide(place == pos_ref[0, k, e : e + 1, :])) for e in range(2)], axis=0)
        p_scr[k] = pick
        xs, gs, ms = low(mm(pick, tok)), low(mm(pick, cot)), mm(pick, hot_ref[0, k], NT)
        for e in range(2):
            rows = slice(k * CAP, (k + 1) * CAP)
            x_ref[e, 0, rows, :] = xs[e * CAP : (e + 1) * CAP]
            g_scr[e, rows, :] = gs[e * CAP : (e + 1) * CAP]
            m_scr[e, rows, :] = ms[e * CAP : (e + 1) * CAP]
    for e in range(2):
        x = x_ref[e, 0]
        grad = wide(g_scr[e])
        named = m_scr[e] > 0.5
        logits = jnp.where(named, mm(x, wr_ref[...]), -1e30)
        powers = jnp.where(named, jnp.exp(logits - logits.max(axis=1, keepdims=True)), 0.0)
        total = powers.sum(axis=1, keepdims=True)
        mine = jnp.where(lane == slot_ref[e], powers, 0.0).sum(axis=1, keepdims=True)
        gate = mine / jnp.where(total > 0.0, total, 1.0)
        gu = mm(x, wgu_ref[e])
        pre, up = gu[:, :FF], gu[:, FF:]
        sig = jax.nn.sigmoid(pre)
        silu = pre * sig
        act = low(silu * up)
        act_ref[e, 0] = act
        out = wide(low(mm(act, wd_ref[e])))
        d_route = (out * grad).sum(axis=1, keepdims=True)
        y_scr[0, e] = low(gate * out)
        dx = low(gate * grad)
        dx_ref[e, 0] = dx
        d_act = mm(dx, wd_ref[e], NT)
        dgu = jnp.concatenate(
            [low(d_act * up * sig * (1.0 + pre * (1.0 - sig))), low(d_act * silu)], axis=1
        )
        dgu_ref[e, 0] = dgu
        y_scr[1, e] = low(mm(dgu, wgu_ref[e], NT))
        for k in range(4):
            pick = wide(p_scr[k, e * CAP : (e + 1) * CAP, :])
            dr_ref[0, k, e : e + 1, :] = (pick * d_route[k * CAP : (k + 1) * CAP]).sum(axis=0, keepdims=True)
    for k in range(4):
        pick_t = p_scr[k].T
        for which, (a_out, b_out) in enumerate(((oa, ob[k]), (dia, dib[k]))):
            rows = jnp.concatenate([y_scr[which, e, k * CAP : (k + 1) * CAP, :] for e in range(2)], axis=0)
            dense = low(mm(pick_t, rows))
            a_out[0, k] = dense[:, :HALF]
            b_out[0] = dense[:, HALF:]


def experts(slots, tok_a, tok_b, cot_a, cot_b, pos, hot, w_router, w_gu, w_d):
    smem = pl.BlockSpec(memory_space=pltpu.SMEM)
    a_spec = pl.BlockSpec((1, 4, ROWS, HALF), lambda j: (j, 0, 0, 0))
    b_spec = pl.BlockSpec((1, ROWS, HALF), lambda j: (j, 0, 0))

    def whole(v):
        return pl.BlockSpec(v.shape, lambda j: (0,) * v.ndim, pipeline_mode=pl.Buffered(1))

    def stack(width):
        return pl.BlockSpec((2, 1, 4 * CAP, width), lambda j: (0, j, 0, 0))

    a_shape = jax.ShapeDtypeStruct((4, 4, ROWS, HALF), BF)
    b_shape = jax.ShapeDtypeStruct((4, ROWS, HALF), BF)
    return pl.pallas_call(
        expert_kernel,
        grid=(4,),
        out_shape=(
            jax.ShapeDtypeStruct((2, 4, 4 * CAP, WIDTH), BF),
            jax.ShapeDtypeStruct((2, 4, 4 * CAP, WIDTH), BF),
            jax.ShapeDtypeStruct((2, 4, 4 * CAP, FF), BF),
            jax.ShapeDtypeStruct((2, 4, 4 * CAP, 2 * FF), BF),
            a_shape, *[b_shape] * 4, a_shape, *[b_shape] * 4,
            jax.ShapeDtypeStruct((4, 4, 2, ROWS), F32),
        ),
        in_specs=[smem, a_spec, *[b_spec] * 4, a_spec, *[b_spec] * 4,
                  pl.BlockSpec((1, 4, 2, ROWS), lambda j: (j, 0, 0, 0)),
                  pl.BlockSpec((1, 4, SLOTS, ROWS), lambda j: (j, 0, 0, 0)),
                  whole(w_router), whole(w_gu), whole(w_d)],
        out_specs=[stack(WIDTH), stack(WIDTH), stack(FF), stack(2 * FF),
                   a_spec, *[b_spec] * 4, a_spec, *[b_spec] * 4,
                   pl.BlockSpec((1, 4, 2, ROWS), lambda j: (j, 0, 0, 0))],
        scratch_shapes=[
            pltpu.VMEM((2, 4 * CAP, WIDTH), BF),
            pltpu.VMEM((2, 4 * CAP, SLOTS), F32),
            pltpu.VMEM((2, 2, 4 * CAP, WIDTH), BF),
            pltpu.VMEM((4, 2 * CAP, ROWS), BF),
        ],
        compiler_params=pltpu.CompilerParams(vmem_limit_bytes=VMEM, dimension_semantics=("arbitrary",)),
        cost_estimate=pl.CostEstimate(flops=30_000_000_000, bytes_accessed=60_000_000, transcendentals=3_000_000),
        name="experts",
    )(slots, tok_a, *tok_b, cot_a, *cot_b, pos, hot, w_router, w_gu, w_d)


def expert_gradient_kernel(x_ref, dx_ref, act_ref, dgu_ref, out_ref):
    x = x_ref[0].reshape(16 * CAP, WIDTH)
    dgu = dgu_ref[0].reshape(16 * CAP, 2 * FF)
    act = act_ref[0].reshape(16 * CAP, FF)
    dx = dx_ref[0].reshape(16 * CAP, WIDTH)
    x_t = x.T
    for part in range(2):
        g = low(mm(x_t, dgu[:, part * FF : (part + 1) * FF]))
        for r in range(4):
            out_ref[r, part] = g[:, 128 * r : 128 * r + 128]
    g = low(mm(act.T, dx))
    for r in range(4):
        for k in range(8):
            out_ref[r, 2, 128 * k : 128 * k + 128, :] = g[128 * r : 128 * r + 128, 128 * k : 128 * k + 128]


def expert_gradient(e, x, dx, act, dgu):
    def stack(width):
        return pl.BlockSpec((1, 4, 4 * CAP, width), lambda i: (e, 0, 0, 0))

    return pl.pallas_call(
        expert_gradient_kernel,
        grid=(1,),
        out_shape=jax.ShapeDtypeStruct((4, 3, WIDTH, 128), BF),
        in_specs=[stack(WIDTH), stack(WIDTH), stack(FF), stack(2 * FF)],
        out_specs=pl.BlockSpec((4, 3, WIDTH, 128), lambda i: (0, 0, 0, 0)),
        compiler_params=pltpu.CompilerParams(vmem_limit_bytes=VMEM),
        cost_estimate=pl.CostEstimate(flops=4_900_000_000, bytes_accessed=14_000_000, transcendentals=0),
        name="expert_gradient",
    )(x, dx, act, dgu)


def after(value, *others):
    return lax.optimization_barrier((value, *others))[0]


def norm_scale(x):
    return lax.rsqrt(jnp.mean(x * x, axis=-1, keepdims=True) + NORM_EPS)


def shards(
    tokens, cotangent, gain_attn, w_query, w_key, w_value, w_out, gain_moe, w_router,
    w_gate, w_up, w_down, routes, owner_map,
):
    dp = lax.axis_index("dp")
    y = lax.axis_index("tensor").astype(jnp.int32).reshape(1)
    z_at, x_at, core = ring_position(dp)

    x_in = wide(tokens)
    scale_a = norm_scale(x_in)
    normed_a = low(x_in * scale_a * gain_attn)
    x_blocks = (normed_a, *gather_direct(normed_a, from_y))

    slot_ids = jnp.arange(SLOTS, dtype=jnp.int32)
    picks = routes[:, :, None] == slot_ids[None, None, :]
    route_slots = jnp.sum(jnp.where(picks, owner_map[None, None, :], 0), axis=-1)
    named = jnp.any(picks, axis=1)
    hot = low(jnp.any(route_slots.T[:, None, :] == slot_ids[None, :, None], axis=0))
    hot_z = jnp.stack([hot, from_z(hot, 1), from_z(hot, 2), from_z(hot, 3)])
    hot_all = jnp.stack([hot_z, from_x(hot_z, 1), from_x(hot_z, 2), from_x(hot_z, 3)])
    slots = jnp.stack([dp, dp + 1 - 2 * core]).astype(jnp.int32)
    mine = jnp.concatenate([lax.dynamic_slice_in_dim(hot_all, slots[e], 1, 2) for e in range(2)], axis=2)
    before = low(jnp.arange(ROWS)[:, None] < jnp.arange(ROWS)[None, :])
    rank = jnp.dot(mine.reshape(-1, ROWS), before, preferred_element_type=F32).reshape(mine.shape)
    pos = jnp.where(mine > 0, rank, -1.0)

    cot_a, cot_b = plane_gather(cotangent)

    half = HEAD // 2
    inv_freq = jnp.exp(jnp.arange(half).astype(F32) * (-2.0 * math.log(10000.0) / HEAD))
    angles = inv_freq[:, None] * jnp.arange(SEQ).astype(F32)[None, :]
    cos, sin = jnp.cos(angles), jnp.sin(angles)
    w_cat_t = jnp.concatenate([w_query, w_key, w_value], axis=1).T

    qkv, o_t, lse, *parts = attention_forward(y, x_blocks, w_cat_t, w_out, cos, sin)
    hidden = x_in + sum_direct(*parts, from_y)
    scale_m = norm_scale(hidden)
    normed_m = low(hidden * scale_m * gain_moe)

    tok_a, tok_b = plane_gather(normed_m)

    gu_own = after(jnp.concatenate([w_gate[0], w_up[0]], axis=1), normed_m)
    d_own = after(w_down[0], normed_m)
    gu_all = (gu_own, *gather_direct(gu_own, from_y))
    gu_all = (gu_all[0], gu_all[1], jnp.concatenate(gu_all[2:4], axis=0), gu_all[4])
    d_all = (d_own, *gather_direct(d_own, from_y))
    gu_full = jnp.concatenate([b[:, :128] for b in gu_all] + [b[:, 128:] for b in gu_all], axis=1)
    d_full = jnp.concatenate(d_all, axis=0)
    gu_two = jnp.stack([gu_full, from_core(gu_full)])
    d_two = jnp.stack([d_full, from_core(d_full)])
    by_slot = low(owner_map[:, None] == slot_ids[None, :])
    router_by_slot = low(jnp.dot(w_router, by_slot, preferred_element_type=F32))

    xs, dxs, acts, dgus, di_a, *rest = experts(
        slots, jnp.stack(tok_a), tok_b, jnp.stack(cot_a), cot_b, pos, hot_all, router_by_slot, gu_two, d_two
    )
    di_b, ou_a, ou_b, d_route = rest[:4], rest[4], rest[5:9], rest[9]

    by_x = [d_route[0], *[from_x(d_route[r], -r) for r in (1, 2, 3)]]
    by_x = jnp.stack(by_x)
    back = jnp.stack([by_x[:, 0], *[from_z(by_x[:, r], -r) for r in (1, 2, 3)]], axis=1)
    rel = jnp.arange(4)
    chip = ((z_at - rel[None, :]) % 4) * 4 + (x_at - rel[:, None]) % 4
    source_slots = jnp.stack([2 * chip + core, 2 * chip + 1 - core], axis=-1).reshape(-1)
    match = wide(source_slots[:, None] == owner_map[None, :])
    d_route = jnp.sum(back.reshape(SLOTS, ROWS)[:, :, None] * match[:, None, :], axis=0)

    logits = jnp.dot(normed_m, w_router, preferred_element_type=F32)
    gates = jax.nn.softmax(jnp.where(named, logits, -jnp.inf), axis=-1)
    d_logits = low(gates * (d_route - jnp.sum(gates * d_route, axis=-1, keepdims=True)))
    router_part = mm(d_logits, normed_m, TN)

    d_in = plane_sum([di_a[r] for r in range(4)], list(di_b))
    d_normed_m = mm(d_logits, w_router, NT) + d_in
    u = d_normed_m * gain_moe
    grad = wide(cotangent)
    d_hidden = grad + scale_m * u - hidden * (scale_m**3) * jnp.mean(u * hidden, axis=-1, keepdims=True)
    gain_moe_part = jnp.sum(d_normed_m * hidden * scale_m, axis=0)
    d_hidden_low = low(d_hidden)
    d_blocks = (d_hidden_low, *gather_direct(d_hidden_low, from_y))

    other = expert_gradient(1, xs, dxs, acts, dgus)
    own = expert_gradient(0, xs, dxs, acts, dgus)
    both = low(wide(own) + wide(from_core(other)))
    both = after(both, *d_blocks)
    far = jnp.concatenate(
        [from_y(both[2][:, : WIDTH // 2], 2), from_y(both[2][:, WIDTH // 2 :], -2)], axis=1
    )
    expert_sum = wide(both[0]) + wide(from_y(both[1], -1)) + wide(from_y(both[3], 1)) + wide(far)

    ou_a, *ou_b = lax.optimization_barrier((ou_a, *ou_b, d_hidden_low))[:5]
    mixed = low(hidden + plane_sum([ou_a[r] for r in range(4)], ou_b))

    out_part = out_gradient(y, d_blocks, o_t)
    dq0, gw0 = attention_backward(0, y, d_blocks, x_blocks, qkv, o_t, lse, w_out, cos, sin)
    dq1, gw1 = attention_backward(1, y, d_blocks, x_blocks, qkv, o_t, lse, w_out, cos, sin)
    w0 = jnp.concatenate([w_cat_t[:128], w_cat_t[256:320], w_cat_t[384:448]], axis=0)
    w1 = jnp.concatenate([w_cat_t[128:256], w_cat_t[320:384], w_cat_t[448:]], axis=0)
    d_parts = input_gradient(y, dq0, dq1, w0, w1)
    d_normed_a = sum_direct(*d_parts, from_y)
    u = d_normed_a * gain_attn
    d_tokens = d_hidden + scale_a * u - x_in * (scale_a**3) * jnp.mean(u * x_in, axis=-1, keepdims=True)

    small = jnp.concatenate([router_part, gain_moe_part[None, :], jnp.zeros((31, WIDTH), F32)], axis=0)
    small = tensor_sum(small)
    bundle = dp_sum(jnp.concatenate([out_part, low(small)], axis=0), dp)
    g_out = wide(bundle[:256])
    g_router = wide(bundle[256:288]).T
    g_gain_moe = wide(bundle[288])
    gw = dp_sum(jnp.concatenate([gw0, gw1], axis=0), dp)
    gw_wide = wide(gw)
    rows = jnp.sum(gw_wide * wide(jnp.concatenate([w0, w1], axis=0)), axis=0)
    g_gain_attn = tensor_sum(rows) / gain_attn
    g_query = jnp.concatenate([gw_wide[:128], gw_wide[256:384]], axis=0).T
    g_key = jnp.concatenate([gw_wide[128:192], gw_wide[384:448]], axis=0).T
    g_value = jnp.concatenate([gw_wide[192:256], gw_wide[448:]], axis=0).T
    g_down = expert_sum[2].reshape(8, 128, 128).transpose(1, 0, 2).reshape(1, 128, WIDTH)
    return (
        mixed, d_tokens, g_gain_attn, g_query, g_key, g_value, g_out, g_gain_moe, g_router,
        expert_sum[0][None], expert_sum[1][None], g_down,
    )


def solution(mesh):
    both = P(("dp", "tensor"), None)
    in_specs = (
        both, both, P(), P(None, "tensor"), P(None, "tensor"), P(None, "tensor"), P("tensor", None), P(), P(),
        P("dp", None, "tensor"), P("dp", None, "tensor"), P("dp", "tensor", None), both, P(),
    )
    out_specs = (
        both, both, P(), P(None, "tensor"), P(None, "tensor"), P(None, "tensor"), P("tensor", None), P(), P(),
        P("dp", None, "tensor"), P("dp", None, "tensor"), P("dp", "tensor", None),
    )
    return jax.shard_map(shards, mesh=mesh, in_specs=in_specs, out_specs=out_specs, check_vma=False)
```

```python
import functools
import math

import jax
import jax.numpy as jnp
from jax import lax
from jax.experimental import pallas as pl
from jax.experimental.pallas import tpu as pltpu
from jax.sharding import PartitionSpec as P

BF = jnp.bfloat16
F32 = jnp.float32
NORM_EPS = 1e-05
HEAD = 64
SEQ = 1024
ROWS = 256
WIDTH = 1024
HALF = 512
FF = 512
SLOTS = 32
CAP = 96
VMEM = 58 * 1024 * 1024

NN = (((1,), (0,)), ((), ()))
NT = (((1,), (1,)), ((), ()))
TN = (((0,), (0,)), ((), ()))


def mm(a, b, dims=NN):
    return lax.dot_general(a, b, dims, preferred_element_type=F32)


def _dp_pairs(dz, dx, dc):
    pairs = []
    for z in range(4):
        for x in range(4):
            for c in range(2):
                src = ((z + dz) % 4) * 8 + ((x + dx) % 4) * 2 + (c + dc) % 2
                pairs.append((src, z * 8 + x * 2 + c))
    return pairs


def from_z(v, d):
    return lax.ppermute(v, "dp", _dp_pairs(d, 0, 0))


def from_x(v, d):
    return lax.ppermute(v, "dp", _dp_pairs(0, d, 0))


def from_core(v):
    return lax.ppermute(v, "dp", _dp_pairs(0, 0, 1))


def from_y(v, d):
    return lax.ppermute(v, "tensor", [((i + d) % 4, i) for i in range(4)])


def low(v):
    return v.astype(BF)


def wide(v):
    return v.astype(F32)


PLANE = [[2 * chip + c for chip in range(16)] for c in range(2)]
EXTRA = ROWS + 16
PART = 112
HALF_ROWS = 4 * PART


def gather_direct(own, get, cut=None):
    cut = own.shape[0] // 2 if cut is None else cut
    return get(own, 1), get(own[:cut], 2), get(own[cut:], -2), get(own, -1)


def sum_direct(own, plus, far_low, far_high, minus, get):
    far = jnp.concatenate([get(far_low, 2), get(far_high, -2)], axis=0)
    return wide(own) + wide(get(plus, -1)) + wide(get(minus, 1)) + wide(far)


def plane_gather_first(rows):
    a, b = rows[None, :, :HALF], rows[None, :, HALF:]
    ap, bp, am, bm = from_z(a, 1), from_x(b, 1), from_z(a, -1), from_x(b, -1)
    return jnp.concatenate([a, ap, from_z(ap, 1), am], axis=0), jnp.concatenate([b, bp, from_x(bp, 1), bm], axis=0)


def plane_gather_second(a, b):
    return from_x(a, 1), from_z(b, 1), from_x(a, -1), from_z(b, -1)


def plane_gather_last(near):
    a_plus, b_plus, a_minus, b_minus = near
    return from_x(a_plus[:2], 1), from_z(b_plus[:2], 1), from_x(a_minus[2:], -1), from_z(b_minus[2:], -1)


def add_low(a, b):
    return low(wide(a) + wide(b))


def relay_kernel(a1, a3, b1, b3, al, ah, bl, bh, a1o, a3o, b1o, b3o):
    for own, got, out in ((a1, al, a1o), (a3, ah, a3o), (b1, bl, b1o), (b3, bh, b3o)):
        out[...] = add_low(own[...], got[...])


def relay(a1, a3, b1, b3, al, ah, bl, bh):
    first = pl.BlockSpec((1, EXTRA, HALF), lambda i: (i, 0, 0))
    second = pl.BlockSpec((1, EXTRA, HALF), lambda i: (2 + i, 0, 0))
    shape = jax.ShapeDtypeStruct(a1.shape, BF)
    return pl.pallas_call(
        relay_kernel,
        grid=(2,),
        out_shape=(shape,) * 4,
        in_specs=[first, second] * 2 + [first] * 4,
        out_specs=[first, second] * 2,
        input_output_aliases={k: k for k in range(4)},
        compiler_params=pltpu.CompilerParams(vmem_limit_bytes=VMEM),
        cost_estimate=pl.CostEstimate(flops=2_000_000, bytes_accessed=7_000_000, transcendentals=0),
        name="relay",
    )(a1, a3, b1, b3, al, ah, bl, bh)


def fold_kernel(a0, qa, ra, b0, qb, rb, *outs):
    for own, q, r, to in ((a0, qa, ra, outs[:4]), (b0, qb, rb, outs[4:])):
        for k in range(4):
            to[k][...] = low(wide(own[k]) + wide(q[k]) + wide(r[k]))


def fold(*terms):
    vmem = pl.BlockSpec(memory_space=pltpu.VMEM)
    return pl.pallas_call(
        fold_kernel,
        out_shape=(jax.ShapeDtypeStruct((EXTRA, HALF), BF),) * 8,
        in_specs=[vmem] * 6,
        out_specs=[vmem] * 8,
        compiler_params=pltpu.CompilerParams(vmem_limit_bytes=VMEM),
        cost_estimate=pl.CostEstimate(flops=3_000_000, bytes_accessed=9_000_000, transcendentals=0),
        name="fold",
    )(*terms)


def first_sums(a, b):
    return from_x(a[2], -1), from_z(b[2], -1), from_x(a[3], 1), from_z(b[3], 1)


def second_sums(a, b, far):
    al, bl, ah, bh = far
    a1, a3, b1, b3 = relay(a[1], a[4], b[1], b[4], al, ah, bl, bh)
    return from_x(a1, -1), from_z(b1, -1), from_x(a3, 1), from_z(b3, 1)


def ring_position(dp):
    return dp // 8, (dp // 2) % 4, dp % 2


def spread_kernel(x_ref, keep, got, *blocks):
    for r, ref in enumerate(blocks):
        at = pl.ds(pl.multiple_of(lax.rem(x_ref[0] + r, 4) * PART, 16), PART)
        ref[...] = low(wide(keep[at, :]) + wide(got[at, :]))


def collect_kernel(x_ref, *refs):
    for r, ref in enumerate(refs[:4]):
        at = pl.ds(pl.multiple_of(lax.rem(x_ref[0] + r, 4) * PART, 16), PART)
        refs[4][at, :] = ref[...]


def dp_spread(x, keep, got):
    vmem = pl.BlockSpec(memory_space=pltpu.VMEM)
    return pl.pallas_call(
        spread_kernel,
        out_shape=(jax.ShapeDtypeStruct((PART, WIDTH), BF),) * 4,
        in_specs=[pl.BlockSpec(memory_space=pltpu.SMEM), vmem, vmem],
        out_specs=[vmem] * 4,
        compiler_params=pltpu.CompilerParams(vmem_limit_bytes=VMEM),
        name="spread",
    )(x, keep, got)


def dp_collect(x, s):
    vmem = pl.BlockSpec(memory_space=pltpu.VMEM)
    s = low(wide(s) + wide(from_z(s, 2)) + wide(from_z(s, 1)) + wide(from_z(s, -1)))
    return pl.pallas_call(
        collect_kernel,
        out_shape=jax.ShapeDtypeStruct((HALF_ROWS, WIDTH), BF),
        in_specs=[pl.BlockSpec(memory_space=pltpu.SMEM)] + [vmem] * 4,
        out_specs=vmem,
        compiler_params=pltpu.CompilerParams(vmem_limit_bytes=VMEM),
        name="collect",
    )(x, s, from_x(s, 1), from_x(s, 2), from_x(s, -1))


def tensor_sum(v):
    return wide(v) + wide(from_y(v, 1)) + wide(from_y(v, 2)) + wide(from_y(v, 3))


def _block_starts(y):
    starts = []
    for r in range(4):
        off = lax.rem(y + r, 4) * ROWS
        if r == 2:
            starts += [off, off + ROWS // 2]
        else:
            starts.append(off)
    return [pl.multiple_of(s, 128) for s in starts]


def attention_forward_kernel(
    y_ref, n0, n1, n2, n3, n4, w_ref, wo_ref, cos_ref, sin_ref,
    qkv_ref, o_ref, lse_ref, p0, p1, p2, p3, p4,
):
    starts = _block_starts(y_ref[0])
    for start, ref in zip(starts, (n0, n1, n2, n3, n4)):
        width = ref.shape[0]
        at = pl.ds(start, width)
        t = mm(w_ref[...], ref[...], NT)
        cos, sin = cos_ref[:, at], sin_ref[:, at]
        for h in range(6):
            a, b = t[64 * h : 64 * h + 32], t[64 * h + 32 : 64 * h + 64]
            ra, rb = a * cos - b * sin, b * cos + a * sin
            if h < 4:
                ra, rb = ra * 0.125, rb * 0.125
            qkv_ref[64 * h : 64 * h + 32, at] = low(ra)
            qkv_ref[64 * h + 32 : 64 * h + 64, at] = low(rb)
        qkv_ref[384:512, at] = low(t[384:])
    key_at = lax.broadcasted_iota(jnp.int32, (ROWS, 2 * ROWS), 0)
    query_at = lax.broadcasted_iota(jnp.int32, (ROWS, 2 * ROWS), 1)
    allowed = key_at <= jnp.bitwise_and(query_at, ROWS - 1)
    for g in range(2):
        keys = qkv_ref[256 + 64 * g : 320 + 64 * g, :].T
        values = qkv_ref[384 + 64 * g : 448 + 64 * g, :]
        for i in range(4):
            here = slice(i * ROWS, (i + 1) * ROWS)
            q2 = jnp.concatenate(
                [qkv_ref[128 * g : 128 * g + 64, here], qkv_ref[128 * g + 64 : 128 * g + 128, here]],
                axis=1,
            )
            tiles = []
            for j in range(i + 1):
                s = mm(keys[j * ROWS : (j + 1) * ROWS], q2)
                if j == i:
                    s = jnp.where(allowed, s, -jnp.inf)
                tiles.append(s)
            peak = tiles[0].max(axis=0, keepdims=True)
            for s in tiles[1:]:
                peak = jnp.maximum(peak, s.max(axis=0, keepdims=True))
            total = jnp.zeros_like(peak)
            mixed = jnp.zeros((HEAD, 2 * ROWS), F32)
            for j, s in enumerate(tiles):
                e = jnp.exp(s - peak)
                total = total + e.sum(axis=0, keepdims=True)
                mixed = mixed + mm(values[:, j * ROWS : (j + 1) * ROWS], low(e))
            mixed = mixed / total
            lse = peak + jnp.log(total)
            o_ref[128 * g : 128 * g + 64, here] = mixed[:, :ROWS]
            o_ref[128 * g + 64 : 128 * g + 128, here] = mixed[:, ROWS:]
            lse_ref[2 * g : 2 * g + 1, here] = lse[:, :ROWS]
            lse_ref[2 * g + 1 : 2 * g + 2, here] = lse[:, ROWS:]
    lse_ref[4:8, :] = jnp.zeros((4, SEQ), F32)
    for start, ref in zip(starts, (p0, p1, p2, p3, p4)):
        att = low(o_ref[:, pl.ds(start, ref.shape[0])])
        ref[...] = low(mm(att.T, wo_ref[...]))


PIECES = (ROWS, ROWS, ROWS // 2, ROWS // 2, ROWS)


def attention_forward(y, blocks, w_t, w_out, cos, sin):
    smem = pl.BlockSpec(memory_space=pltpu.SMEM)
    vmem = pl.BlockSpec(memory_space=pltpu.VMEM)
    return pl.pallas_call(
        attention_forward_kernel,
        out_shape=(
            jax.ShapeDtypeStruct((512, SEQ), BF),
            jax.ShapeDtypeStruct((256, SEQ), F32),
            jax.ShapeDtypeStruct((8, SEQ), F32),
            *[jax.ShapeDtypeStruct((w, WIDTH), BF) for w in PIECES],
        ),
        in_specs=[smem] + [vmem] * 9,
        out_specs=[vmem] * 8,
        compiler_params=pltpu.CompilerParams(vmem_limit_bytes=VMEM),
        cost_estimate=pl.CostEstimate(flops=8_000_000_000, bytes_accessed=10_000_000, transcendentals=3_000_000),
        name="attention_forward",
    )(y, *blocks, w_t, w_out, cos, sin)


def attention_backward_kernel(
    at_ref, d0, d1, d2, d3, d4, x0, x1, x2, x3, x4, qkv_ref, o_ref, lse_ref, wo_ref, wa_ref, wb_ref, cos_ref, sin_ref,
    small_ref, keep_ref, send_ref, p0, p1, p2, p3, p4, do_ref, delta_ref, dk_ref, dv_ref, dqkv_ref,
):
    starts = _block_starts(at_ref[0])
    core = at_ref[1]

    def put(half, first, value):
        rows = slice(first, first + value.shape[0])

        @pl.when(core == half)
        def _():
            keep_ref[rows, :] = value

        @pl.when(core != half)
        def _():
            send_ref[rows, :] = value

    total = jnp.zeros((256, WIDTH), F32)
    for start, ref in zip(starts, (d0, d1, d2, d3, d4)):
        at = pl.ds(start, ref.shape[0])
        do_ref[:, at] = low(mm(wo_ref[...], ref[...], NT))
        total = total + mm(low(o_ref[:, at]), ref[...])
    put(0, 256, low(total[:128]))
    put(1, 256, low(total[128:]))
    put(0, 384, jnp.zeros((64, WIDTH), BF))
    put(1, 384, small_ref[...])
    prod = o_ref[...] * wide(do_ref[...])
    for h in range(4):
        delta_ref[h : h + 1, :] = prod[64 * h : 64 * h + 64].sum(axis=0, keepdims=True)
    key_at = lax.broadcasted_iota(jnp.int32, (ROWS, 2 * ROWS), 0)
    query_at = lax.broadcasted_iota(jnp.int32, (ROWS, 2 * ROWS), 1)
    allowed = key_at <= jnp.bitwise_and(query_at, ROWS - 1)
    for g in range(2):
        keys_t = qkv_ref[256 + 64 * g : 320 + 64 * g, :]
        keys = keys_t.T
        values = qkv_ref[384 + 64 * g : 448 + 64 * g, :].T
        dk_ref[...] = jnp.zeros_like(dk_ref)
        dv_ref[...] = jnp.zeros_like(dv_ref)
        base = 256 * g
        for i in range(4):
            here = slice(i * ROWS, (i + 1) * ROWS)

            def pair(ref, base, step):
                return jnp.concatenate(
                    [ref[base : base + step, here], ref[base + step : base + 2 * step, here]], axis=1
                )

            q2 = pair(qkv_ref, 128 * g, 64)
            do2 = pair(do_ref, 128 * g, 64)
            lse2 = pair(lse_ref, 2 * g, 1)
            delta2 = pair(delta_ref, 2 * g, 1)
            dq = jnp.zeros((HEAD, 2 * ROWS), F32)
            for j in range(i + 1):
                at = slice(j * ROWS, (j + 1) * ROWS)
                s = mm(keys[at], q2)
                p = jnp.exp(s - lse2)
                if j == i:
                    p = jnp.where(allowed, p, 0.0)
                dp = mm(values[at], do2)
                ds = low(p * (dp - delta2))
                dq = dq + mm(keys_t[:, at], ds)
                dk_ref[:, at] += mm(q2, ds, NT)
                dv_ref[:, at] += mm(do2, low(p), NT)
            cos, sin = cos_ref[:, here], sin_ref[:, here]
            dq = dq * 0.125
            for h in range(2):
                a, b = dq[:32, h * ROWS : (h + 1) * ROWS], dq[32:, h * ROWS : (h + 1) * ROWS]
                dqkv_ref[base + 64 * h : base + 64 * h + 32, here] = low(a * cos + b * sin)
                dqkv_ref[base + 64 * h + 32 : base + 64 * h + 64, here] = low(b * cos - a * sin)
        a, b = dk_ref[:32, :], dk_ref[32:, :]
        dqkv_ref[base + 128 : base + 160, :] = low(a * cos_ref[...] + b * sin_ref[...])
        dqkv_ref[base + 160 : base + 192, :] = low(b * cos_ref[...] - a * sin_ref[...])
        dqkv_ref[base + 192 : base + 256, :] = low(dv_ref[...])
        total = jnp.zeros((256, WIDTH), F32)
        for start, ref in zip(starts, (x0, x1, x2, x3, x4)):
            total = total + mm(dqkv_ref[base : base + 256, pl.ds(start, ref.shape[0])], ref[...])
        put(g, 0, low(total))
    for start, ref in zip(starts, (p0, p1, p2, p3, p4)):
        at = pl.ds(start, ref.shape[0])
        ref[...] = low(mm(dqkv_ref[:256, at].T, wa_ref[...]) + mm(dqkv_ref[256:, at].T, wb_ref[...]))


def attention_backward(at, d_blocks, x_blocks, qkv, o, lse, w_out, wa, wb, cos, sin, small):
    smem = pl.BlockSpec(memory_space=pltpu.SMEM)
    vmem = pl.BlockSpec(memory_space=pltpu.VMEM)
    return pl.pallas_call(
        attention_backward_kernel,
        out_shape=(
            *[jax.ShapeDtypeStruct((HALF_ROWS, WIDTH), BF)] * 2,
            *[jax.ShapeDtypeStruct((w, WIDTH), BF) for w in PIECES],
        ),
        in_specs=[smem] + [vmem] * 19,
        out_specs=[vmem] * 7,
        scratch_shapes=[
            pltpu.VMEM((256, SEQ), BF),
            pltpu.VMEM((8, SEQ), F32),
            pltpu.VMEM((64, SEQ), F32),
            pltpu.VMEM((64, SEQ), F32),
            pltpu.VMEM((512, SEQ), BF),
        ],
        compiler_params=pltpu.CompilerParams(vmem_limit_bytes=VMEM),
        cost_estimate=pl.CostEstimate(flops=20_000_000_000, bytes_accessed=15_000_000, transcendentals=3_000_000),
        name="attention_backward",
    )(at, *d_blocks, *x_blocks, qkv, o, lse, w_out, wa, wb, cos, sin, small)


def finish_kernel(core_ref, half, other, wa_ref, wb_ref, gq, gk, gv, go, rest):
    core = core_ref[0]

    def unpack(first, second):
        lines = jnp.zeros((1, WIDTH), F32)
        for g, (ref, w_ref) in enumerate(((first, wa_ref), (second, wb_ref))):
            grads = wide(ref[:256, :])
            lines = lines + (grads * wide(w_ref[...])).sum(axis=0, keepdims=True)
            gq[:, 128 * g : 128 * g + 128] = grads[:128].T
            turned = grads[128:].T
            gk[:, 64 * g : 64 * g + 64] = turned[:, :64]
            gv[:, 64 * g : 64 * g + 64] = turned[:, 64:]
            go[128 * g : 128 * g + 128, :] = wide(ref[256:384, :])
        rest[:32, :] = second[384:416, :]
        gains = wide(second[416:418, :]).sum(axis=0, keepdims=True)
        high, high2 = low(gains), low(lines)
        rows = [wide(high), gains - wide(high), wide(high2), lines - wide(high2), jnp.zeros((12, WIDTH), F32)]
        rest[32:, :] = low(jnp.concatenate(rows, axis=0))

    @pl.when(core == 0)
    def _():
        unpack(half, other)

    @pl.when(core != 0)
    def _():
        unpack(other, half)


def finish(core, half, other, wa, wb):
    smem = pl.BlockSpec(memory_space=pltpu.SMEM)
    vmem = pl.BlockSpec(memory_space=pltpu.VMEM)
    return pl.pallas_call(
        finish_kernel,
        out_shape=(
            jax.ShapeDtypeStruct((WIDTH, 256), F32),
            jax.ShapeDtypeStruct((WIDTH, 128), F32),
            jax.ShapeDtypeStruct((WIDTH, 128), F32),
            jax.ShapeDtypeStruct((256, WIDTH), F32),
            jax.ShapeDtypeStruct((48, WIDTH), BF),
        ),
        in_specs=[smem] + [vmem] * 4,
        out_specs=[vmem] * 5,
        compiler_params=pltpu.CompilerParams(vmem_limit_bytes=VMEM),
        cost_estimate=pl.CostEstimate(flops=3_000_000, bytes_accessed=6_000_000, transcendentals=0),
        name="finish",
    )(core, half, other, wa, wb)


SHARD = WIDTH + 512


def expert_kernel(at_ref, *refs):
    ta, (tb0, tb1, tb2, tb3, tb4), (cot_ref, pos_ref, hot_ref, wr_ref), refs = refs[:5], refs[5:10], refs[10:14], refs[14:]
    weights, (x_ref, dx_ref, act_ref, dgu_ref), refs = refs[:2], refs[2:6], refs[6:]
    da, (db0, db1, db2, db3, db4), out_ref, refs = refs[:5], refs[5:10], refs[10], refs[11:]
    ta_scr, tb_scr, wgu_scr, wd_scr, g_scr, m_scr, y_scr, p_scr, dr_scr, da_scr, db_scr, ta_sem, w_sem, da_sem = refs
    j = pl.program_id(0)
    place = wide(lax.broadcasted_iota(jnp.int32, (CAP, ROWS), 0))
    lane = lax.broadcasted_iota(jnp.int32, (4 * CAP, SLOTS), 1)
    z_of = [lax.rem(at_ref[2] + k, 4) for k in range(4)]

    def token_copies(k):
        if k == 2:
            return [pltpu.make_async_copy(ta[2 + p], ta_scr.at[2, pl.ds(2 * p, 2)], ta_sem.at[2 + p]) for p in range(2)]
        n = (0, 1, None, 4)[k]
        return [pltpu.make_async_copy(ta[n], ta_scr.at[k], ta_sem.at[n])]

    def weight_copies():
        copies = []
        for e in range(2):
            for r in range(4):
                ref = weights[e].at[r]
                cols = pl.ds(128 * r, 128)
                moves = [
                    (ref.at[pl.ds(0, WIDTH), pl.ds(0, 128)], wgu_scr.at[e, :, cols]),
                    (ref.at[pl.ds(0, WIDTH), pl.ds(128, 128)], wgu_scr.at[e, :, pl.ds(FF + 128 * r, 128)]),
                ]
                for c in range(4):
                    moves.append((ref.at[pl.ds(WIDTH + 128 * c, 128), :], wd_scr.at[e, cols, pl.ds(256 * c, 256)]))
                for source, target in moves:
                    copies.append(pltpu.make_async_copy(source, target, w_sem.at[len(copies)]))
        return copies

    def sum_copies(k):
        if k == 2:
            return [pltpu.make_async_copy(da_scr.at[2, pl.ds(2 * p, 2)], da[2 + p], da_sem.at[2 + p]) for p in range(2)]
        n = (0, 1, None, 4)[k]
        return [pltpu.make_async_copy(da_scr.at[k], da[n], da_sem.at[n])]

    @pl.when(j == 0)
    def _():
        for copy in token_copies(0) + weight_copies():
            copy.start()
        for k in range(1, 4):
            for copy in token_copies(k):
                copy.start()

    for k in range(4):

        @pl.when(j == k)
        def _(k=k):
            for copy in token_copies(k):
                copy.wait()

    @pl.when(j < 2)
    def _():
        tb_scr[...] = tb2[0]

    @pl.when(j >= 2)
    def _():
        tb_scr[...] = tb3[0]

    halves = (tb0[0], tb1[0], tb_scr[...], tb4[0])
    for k in range(4):
        tok = jnp.concatenate([ta_scr[j, k], halves[k]], axis=1)
        pos = pos_ref[z_of[k], 0]
        pick = jnp.concatenate([low(wide(place == pos[e : e + 1, :])) for e in range(2)], axis=0)
        p_scr[k] = pick
        xs, gs = low(mm(pick, tok)), low(mm(pick, cot_ref[z_of[k], 0]))
        ms = mm(pick, hot_ref[z_of[k], 0], NT)
        for e in range(2):
            rows = slice(k * CAP, (k + 1) * CAP)
            x_ref[e, 0, rows, :] = xs[e * CAP : (e + 1) * CAP]
            g_scr[e, rows, :] = gs[e * CAP : (e + 1) * CAP]
            m_scr[e, rows, :] = ms[e * CAP : (e + 1) * CAP]

    @pl.when(j == 0)
    def _():
        for copy in weight_copies():
            copy.wait()

    both = range(2)
    gu = [mm(x_ref[e, 0], wgu_scr[e]) for e in both]
    logits = [mm(x_ref[e, 0], wr_ref[...]) for e in both]
    sig = [jax.nn.sigmoid(gu[e][:, :FF]) for e in both]
    for e in both:
        act_ref[e, 0] = low(gu[e][:, :FF] * sig[e] * gu[e][:, FF:])
    out = [low(mm(act_ref[e, 0], wd_scr[e])) for e in both]
    gate = []
    for e in both:
        named = m_scr[e] > 0.5
        kept = jnp.where(named, logits[e], -1e30)
        powers = jnp.where(named, jnp.exp(kept - kept.max(axis=1, keepdims=True)), 0.0)
        total = powers.sum(axis=1, keepdims=True)
        mine = jnp.where(lane == at_ref[e], powers, 0.0).sum(axis=1, keepdims=True)
        gate.append(mine / jnp.where(total > 0.0, total, 1.0))
        dx_ref[e, 0] = low(gate[e] * wide(g_scr[e]))
    d_act = [mm(dx_ref[e, 0], wd_scr[e], NT) for e in both]
    d_route = []
    for e in both:
        d_route.append((wide(out[e]) * wide(g_scr[e])).sum(axis=1, keepdims=True))
        y_scr[0, e] = low(gate[e] * wide(out[e]))
    for e in both:
        pre, up = gu[e][:, :FF], gu[e][:, FF:]
        dgu_ref[e, 0, :, :FF] = low(d_act[e] * up * sig[e] * (1.0 + pre * (1.0 - sig[e])))
        dgu_ref[e, 0, :, FF:] = low(d_act[e] * (pre * sig[e]))
    for e in both:
        y_scr[1, e] = low(mm(dgu_ref[e, 0], wgu_scr[e], NT))
        for k in range(4):
            pick = wide(p_scr[k, e * CAP : (e + 1) * CAP, :])
            dr_scr[k, e : e + 1, :] = (pick * d_route[e][k * CAP : (k + 1) * CAP]).sum(axis=0, keepdims=True)
    chip = at_ref[2] * 4 + at_ref[3]
    first = lax.rem(at_ref[0], 2) == 0
    line = lax.broadcasted_iota(jnp.int32, (16, HALF), 0) == chip
    for k in range(4):
        pick_t = p_scr[k].T
        rows = jnp.concatenate([y_scr[0, e, k * CAP : (k + 1) * CAP, :] for e in range(2)], axis=0)
        out_ref[z_of[k], 0] = low(mm(pick_t, rows))
        rows = jnp.concatenate([y_scr[1, e, k * CAP : (k + 1) * CAP, :] for e in range(2)], axis=0)
        dense = low(mm(pick_t, rows))
        own, other = dr_scr[k, 0:1, :], dr_scr[k, 1:2, :]
        pair = jnp.concatenate([jnp.where(first, own, other), jnp.where(first, other, own)], axis=1)
        high = wide(low(pair))
        da_scr[j, k, :ROWS] = dense[:, :HALF]
        da_scr[j, k, ROWS:] = low(jnp.where(line, high, 0.0))
        to = db_scr if k == 2 else (db0, db1, None, db4)[k].at[0]
        to[:ROWS] = dense[:, HALF:]
        to[ROWS:] = low(jnp.where(line, pair - high, 0.0))

    for k in range(4):

        @pl.when(j == k)
        def _(k=k):
            for copy in sum_copies(k):
                copy.start()

    @pl.when(j == 3)
    def _():
        for k in range(4):
            for copy in sum_copies(k):
                copy.wait()

    @pl.when(j < 2)
    def _():
        db2[0] = db_scr[...]

    @pl.when(j >= 2)
    def _():
        db3[0] = db_scr[...]


def experts(at, tok_a, tok_b, cot, pos, hot, w_router, weights):
    def whole(*shape):
        return pl.BlockSpec(shape, lambda j, at: (0,) * len(shape), pipeline_mode=pl.Buffered(1))

    def early(rows):
        return pl.BlockSpec((1, rows, HALF), lambda j, at: (jnp.minimum(j, 1), 0, 0))

    def late(rows):
        return pl.BlockSpec((1, rows, HALF), lambda j, at: (jnp.maximum(j - 2, 0), 0, 0))

    def by_step(rows):
        step = pl.BlockSpec((1, rows, HALF), lambda j, at: (j, 0, 0))
        return [step, step, early(rows), late(rows), step]

    anywhere = pl.BlockSpec(memory_space=pl.ANY)

    def column(*shape):
        return pl.BlockSpec((4, 1, *shape), lambda j, at: (0, lax.rem(at[3] + j, 4), 0, 0))

    def stack(width):
        return pl.BlockSpec((2, 1, 4 * CAP, width), lambda j, at: (0, j, 0, 0))

    return pl.pallas_call(
        expert_kernel,
        grid_spec=pltpu.PrefetchScalarGridSpec(
            num_scalar_prefetch=1,
            grid=(4,),
            in_specs=[*[anywhere] * 5, *by_step(ROWS), column(ROWS, WIDTH), column(2, ROWS), column(SLOTS, ROWS),
                      whole(*w_router.shape), *[anywhere] * 2],
            out_specs=[stack(WIDTH), stack(WIDTH), stack(FF), stack(2 * FF),
                       *[anywhere] * 5, *by_step(EXTRA), column(ROWS, WIDTH)],
            scratch_shapes=[
                pltpu.VMEM((4, 4, ROWS, HALF), BF),
                pltpu.VMEM((ROWS, HALF), BF),
                pltpu.VMEM((2, WIDTH, 2 * FF), BF),
                pltpu.VMEM((2, FF, WIDTH), BF),
                pltpu.VMEM((2, 4 * CAP, WIDTH), BF),
                pltpu.VMEM((2, 4 * CAP, SLOTS), F32),
                pltpu.VMEM((2, 2, 4 * CAP, WIDTH), BF),
                pltpu.VMEM((4, 2 * CAP, ROWS), BF),
                pltpu.VMEM((4, 2, ROWS), F32),
                pltpu.VMEM((4, 4, EXTRA, HALF), BF),
                pltpu.VMEM((EXTRA, HALF), BF),
                pltpu.SemaphoreType.DMA((5,)),
                pltpu.SemaphoreType.DMA((48,)),
                pltpu.SemaphoreType.DMA((5,)),
            ],
        ),
        out_shape=(
            jax.ShapeDtypeStruct((2, 4, 4 * CAP, WIDTH), BF),
            jax.ShapeDtypeStruct((2, 4, 4 * CAP, WIDTH), BF),
            jax.ShapeDtypeStruct((2, 4, 4 * CAP, FF), BF),
            jax.ShapeDtypeStruct((2, 4, 4 * CAP, 2 * FF), BF),
            *[jax.ShapeDtypeStruct((n, EXTRA, HALF), BF) for n in (4, 4, 2, 2, 4) * 2],
            jax.ShapeDtypeStruct((4, 4, ROWS, WIDTH), BF),
        ),
        compiler_params=pltpu.CompilerParams(vmem_limit_bytes=VMEM, dimension_semantics=("arbitrary",)),
        cost_estimate=pl.CostEstimate(flops=30_000_000_000, bytes_accessed=60_000_000, transcendentals=3_000_000),
        name="experts",
    )(at, *tok_a, *tok_b, cot, pos, hot, w_router, *weights)


def expert_gradient_kernel(x_ref, dx_ref, act_ref, dgu_ref, other_ref, own_ref):
    x_t = x_ref[0].reshape(16 * CAP, WIDTH).T
    dx = dx_ref[0].reshape(16 * CAP, WIDTH)
    gu = low(mm(x_t, dgu_ref[0].reshape(16 * CAP, 2 * FF)))
    gd = low(mm(act_ref[0].reshape(16 * CAP, FF), dx, TN))
    for i, ref in enumerate((other_ref, own_ref)):

        @pl.when(pl.program_id(0) == i)
        def _(ref=ref):
            for r in range(4):
                cols = slice(128 * r, 128 * r + 128)
                ref[r, :WIDTH, :128] = gu[:, cols]
                ref[r, :WIDTH, 128:] = gu[:, FF + 128 * r : FF + 128 * r + 128]
                for c in range(4):
                    ref[r, WIDTH + 128 * c : WIDTH + 128 * c + 128, :] = gd[cols, 256 * c : 256 * c + 256]


def expert_gradients(x, dx, act, dgu):
    def stack(width):
        return pl.BlockSpec((1, 4, 4 * CAP, width), lambda i: (1 - i, 0, 0, 0))

    whole = pl.BlockSpec((4, SHARD, 256), lambda i: (0, 0, 0))
    return pl.pallas_call(
        expert_gradient_kernel,
        grid=(2,),
        out_shape=(jax.ShapeDtypeStruct((4, SHARD, 256), BF),) * 2,
        in_specs=[stack(WIDTH), stack(WIDTH), stack(FF), stack(2 * FF)],
        out_specs=[whole, whole],
        compiler_params=pltpu.CompilerParams(vmem_limit_bytes=VMEM),
        cost_estimate=pl.CostEstimate(flops=18_000_000_000, bytes_accessed=28_000_000, transcendentals=0),
        name="expert_gradients",
    )(x, dx, act, dgu)


def merge_kernel(a_ref, b_ref, out):
    out[...] = add_low(a_ref[...], b_ref[...])


def merge(a, b):
    spec = pl.BlockSpec((1, SHARD, 256), lambda i: (i, 0, 0))
    return pl.pallas_call(
        merge_kernel,
        grid=(4,),
        out_shape=jax.ShapeDtypeStruct(a.shape, BF),
        in_specs=[spec] * 2,
        out_specs=spec,
        compiler_params=pltpu.CompilerParams(vmem_limit_bytes=VMEM),
        cost_estimate=pl.CostEstimate(flops=2_000_000, bytes_accessed=10_000_000, transcendentals=0),
        name="merge",
    )(a, b)


def after(value, *others):
    return lax.optimization_barrier((value, *others))[0]


def norm_scale(x):
    return lax.rsqrt(jnp.mean(x * x, axis=-1, keepdims=True) + NORM_EPS)


def shards(
    tokens, cotangent, gain_attn, w_query, w_key, w_value, w_out, gain_moe, w_router,
    w_gate, w_up, w_down, routes, owner_map,
):
    dp = lax.axis_index("dp")
    y = lax.axis_index("tensor").astype(jnp.int32).reshape(1)
    z_at, x_at, core = ring_position(dp)

    x_in = wide(tokens)
    scale_a = norm_scale(x_in)
    normed_a = low(x_in * scale_a * gain_attn)
    x_blocks = (normed_a, *gather_direct(normed_a, from_y))

    slot_ids = jnp.arange(SLOTS, dtype=jnp.int32)
    picks = routes[:, :, None] == slot_ids[None, None, :]
    route_slots = jnp.sum(jnp.where(picks, owner_map[None, None, :], 0), axis=-1)
    named = jnp.any(picks, axis=1)
    hot = low(jnp.any(route_slots.T[:, None, :] == slot_ids[None, :, None], axis=0))

    sent = jnp.concatenate([cotangent, hot.reshape(8, WIDTH), jnp.zeros((8, WIDTH), BF)], axis=0)
    cot = lax.all_gather(sent, "dp", axis=0, axis_index_groups=PLANE).reshape(4, 4, EXTRA, WIDTH)

    half = HEAD // 2
    inv_freq = jnp.exp(jnp.arange(half).astype(F32) * (-2.0 * math.log(10000.0) / HEAD))
    angles = inv_freq[:, None] * jnp.arange(SEQ).astype(F32)[None, :]
    cos, sin = jnp.cos(angles), jnp.sin(angles)
    w_cat_t = jnp.concatenate([w_query, w_key, w_value], axis=1).T

    qkv, o_t, lse, *parts = attention_forward(y, x_blocks, w_cat_t, w_out, cos, sin)
    hidden = x_in + sum_direct(*parts, from_y)
    scale_m = norm_scale(hidden)
    normed_m = low(hidden * scale_m * gain_moe)

    down = w_down[0].reshape(128, 4, 256).transpose(1, 0, 2).reshape(512, 256)
    shard = jnp.concatenate([jnp.concatenate([w_gate[0], w_up[0]], axis=1), down], axis=0)
    w_own = lax.all_gather(shard, "tensor", axis=0)
    tok_a, tok_b = plane_gather_first(normed_m)
    tok_a, tok_b, cot = lax.optimization_barrier((tok_a, tok_b, cot))
    *near, w_own = lax.optimization_barrier((*plane_gather_second(tok_a, tok_b), w_own))
    far = plane_gather_last(near)
    tok_a, tok_b = (tok_a, near[0], far[0], far[2], near[2]), (tok_b, near[1], far[1], far[3], near[3])
    weights = w_own, from_core(w_own)
    hot_all = cot[:, :, ROWS : ROWS + 8].reshape(4, 4, SLOTS, ROWS)
    at = jnp.stack([dp, dp + 1 - 2 * core, z_at, x_at]).astype(jnp.int32)
    mine = jnp.concatenate([lax.dynamic_slice_in_dim(hot_all, at[e], 1, 2) for e in range(2)], axis=2)
    before = low(jnp.arange(ROWS)[:, None] < jnp.arange(ROWS)[None, :])
    rank = jnp.dot(mine.reshape(-1, ROWS), before, preferred_element_type=F32).reshape(mine.shape)
    pos = jnp.where(mine > 0, rank, -1.0)
    by_slot = low(owner_map[:, None] == slot_ids[None, :])
    router_by_slot = low(jnp.dot(w_router, by_slot, preferred_element_type=F32))

    xs, dxs, acts, dgus, *rest = experts(
        at, tok_a, tok_b, cot, pos, hot_all, router_by_slot, weights
    )
    di_a, di_b, weighted = rest[:5], rest[5:10], rest[10]
    far = first_sums(di_a, di_b)
    *far, xs = lax.optimization_barrier((*far, xs))
    relayed = second_sums(di_a, di_b, far)
    other, own = expert_gradients(xs, dxs, acts, dgus)
    *relayed, other, own = lax.optimization_barrier((*relayed, other, own))
    qa, qb, ra, rb = relayed
    a0, a1, a2, a3, b0, b1, b2, b3 = fold(di_a[0], qa, ra, di_b[0], qb, rb)
    far = from_z(a2, -1), from_x(b2, -1)
    minus = from_z(a3, 1), from_x(b3, 1)
    both = merge(own, from_core(other))
    *far, both = lax.optimization_barrier((*far, both))
    expert_sum = lax.psum_scatter(both.reshape(4 * SHARD, 256), "tensor", scatter_dimension=0, tiled=True)
    in_a = wide(a0) + wide(minus[0]) + wide(from_z(add_low(a1, far[0]), -1))
    in_b = wide(b0) + wide(minus[1]) + wide(from_x(add_low(b1, far[1]), -1))
    by_slot_t = (in_a[ROWS:] + in_b[ROWS:]).reshape(SLOTS, ROWS)
    d_in = jnp.concatenate([in_a[:ROWS], in_b[:ROWS]], axis=1)
    match = wide(slot_ids[:, None] == owner_map[None, :])
    d_route = jnp.sum(by_slot_t[:, :, None] * match[:, None, :], axis=0)

    logits = jnp.dot(normed_m, w_router, preferred_element_type=F32)
    gates = jax.nn.softmax(jnp.where(named, logits, -jnp.inf), axis=-1)
    d_logits = low(gates * (d_route - jnp.sum(gates * d_route, axis=-1, keepdims=True)))
    router_part = mm(d_logits, normed_m, TN)

    d_normed_m = mm(d_logits, w_router, NT) + d_in
    u = d_normed_m * gain_moe
    grad = wide(cotangent)
    d_hidden = grad + scale_m * u - hidden * (scale_m**3) * jnp.mean(u * hidden, axis=-1, keepdims=True)
    gain_moe_part = jnp.sum(d_normed_m * hidden * scale_m, axis=0)
    d_hidden_low = low(d_hidden)
    d_blocks = (d_hidden_low, *gather_direct(d_hidden_low, from_y))

    weighted = after(weighted, a0, b0)
    returned = lax.psum_scatter(
        weighted.reshape(16 * ROWS, WIDTH), "dp", scatter_dimension=0, axis_index_groups=PLANE, tiled=True
    )

    high = low(gain_moe_part)
    small = [low(router_part), high[None], low(gain_moe_part - wide(high))[None], jnp.zeros((30, WIDTH), BF)]
    small = jnp.concatenate(small, axis=0)
    wa = jnp.concatenate([w_cat_t[:128], w_cat_t[256:320], w_cat_t[384:448]], axis=0)
    wb = jnp.concatenate([w_cat_t[128:256], w_cat_t[320:384], w_cat_t[448:]], axis=0)
    core_at = core.astype(jnp.int32).reshape(1)
    keep, send, *d_parts = attention_backward(
        jnp.concatenate([y, core_at]), d_blocks, x_blocks, qkv, o_t, lse, w_out, wa, wb, cos, sin, small
    )

    x_index = x_at.astype(jnp.int32).reshape(1)
    far = from_y(d_parts[2], -1), from_y(d_parts[3], 1)
    blocks = dp_spread(x_index, keep, from_core(send))
    cut = ROWS // 2
    plus = jnp.concatenate([add_low(d_parts[1][:cut], far[0]), d_parts[1][cut:]], axis=0)
    minus = jnp.concatenate([d_parts[4][:cut], add_low(d_parts[4][cut:], far[1])], axis=0)
    plus, minus = from_y(plus, -1), from_y(minus, 1)
    s = wide(blocks[0]) + wide(from_x(blocks[2], 2)) + wide(from_x(blocks[1], -1)) + wide(from_x(blocks[3], 1))
    plus, minus, s = lax.optimization_barrier((plus, minus, low(s)))
    d_normed_a = wide(d_parts[0]) + wide(plus) + wide(minus)
    u = d_normed_a * gain_attn
    d_tokens = d_hidden + scale_a * u - x_in * (scale_a**3) * jnp.mean(u * x_in, axis=-1, keepdims=True)

    half_sum = dp_collect(x_index, s)
    half_sum, returned = lax.optimization_barrier((half_sum, returned))
    g_query, g_key, g_value, g_out, rest = finish(core_at, half_sum, from_core(half_sum), wa, wb)
    rest, expert_sum = lax.optimization_barrier((rest, expert_sum))
    rest = tensor_sum(rest)
    expert_sum = wide(expert_sum)
    mixed = low(hidden + wide(returned))
    g_router, g_gain_moe, g_gain_attn = rest[:32].T, rest[32] + rest[33], (rest[34] + rest[35]) / gain_attn
    g_gate, g_up = expert_sum[:WIDTH, :128][None], expert_sum[:WIDTH, 128:][None]
    g_down = expert_sum[WIDTH:].reshape(4, 128, 256).transpose(1, 0, 2).reshape(1, 128, WIDTH)
    return (
        mixed, d_tokens, g_gain_attn, g_query, g_key, g_value, g_out, g_gain_moe, g_router,
        g_gate, g_up, g_down,
    )


def solution(mesh):
    both = P(("dp", "tensor"), None)
    in_specs = (
        both, both, P(), P(None, "tensor"), P(None, "tensor"), P(None, "tensor"), P("tensor", None), P(), P(),
        P("dp", None, "tensor"), P("dp", None, "tensor"), P("dp", "tensor", None), both, P(),
    )
    out_specs = (
        both, both, P(), P(None, "tensor"), P(None, "tensor"), P(None, "tensor"), P("tensor", None), P(), P(),
        P("dp", None, "tensor"), P("dp", None, "tensor"), P("dp", "tensor", None),
    )
    return jax.shard_map(shards, mesh=mesh, in_specs=in_specs, out_specs=out_specs, check_vma=False)
```

```python
import functools
import math

import jax
import jax.numpy as jnp
from jax import lax
from jax.experimental import pallas as pl
from jax.experimental.pallas import tpu as pltpu
from jax.sharding import PartitionSpec as P

BF = jnp.bfloat16
F32 = jnp.float32
NORM_EPS = 1e-05
HEAD = 64
SEQ = 1024
ROWS = 256
WIDTH = 1024
HALF = 512
FF = 512
SLOTS = 32
CAP = 96
VMEM = 58 * 1024 * 1024

NN = (((1,), (0,)), ((), ()))
NT = (((1,), (1,)), ((), ()))
TN = (((0,), (0,)), ((), ()))


def mm(a, b, dims=NN):
    return lax.dot_general(a, b, dims, preferred_element_type=F32)


def _dp_pairs(dz, dx, dc):
    pairs = []
    for z in range(4):
        for x in range(4):
            for c in range(2):
                src = ((z + dz) % 4) * 8 + ((x + dx) % 4) * 2 + (c + dc) % 2
                pairs.append((src, z * 8 + x * 2 + c))
    return pairs


def from_z(v, d):
    return lax.ppermute(v, "dp", _dp_pairs(d, 0, 0))


def from_x(v, d):
    return lax.ppermute(v, "dp", _dp_pairs(0, d, 0))


def from_core(v):
    return lax.ppermute(v, "dp", _dp_pairs(0, 0, 1))


def from_y(v, d):
    return lax.ppermute(v, "tensor", [((i + d) % 4, i) for i in range(4)])


def low(v):
    return v.astype(BF)


def wide(v):
    return v.astype(F32)


PLANE = [[2 * chip + c for chip in range(16)] for c in range(2)]
EXTRA = ROWS + 16
PART = 112
HALF_ROWS = 4 * PART


def gather_direct(own, get, cut=None):
    cut = own.shape[0] // 2 if cut is None else cut
    return get(own, 1), get(own[:cut], 2), get(own[cut:], -2), get(own, -1)


def sum_direct(own, plus, far_low, far_high, minus, get):
    far = jnp.concatenate([get(far_low, 2), get(far_high, -2)], axis=0)
    return wide(own) + wide(get(plus, -1)) + wide(get(minus, 1)) + wide(far)


def plane_gather_first(rows):
    a, b = rows[None, :, :HALF], rows[None, :, HALF:]
    ap, bp, am, bm = from_z(a, 1), from_x(b, 1), from_z(a, -1), from_x(b, -1)
    return jnp.concatenate([a, ap, from_z(ap, 1), am], axis=0), jnp.concatenate([b, bp, from_x(bp, 1), bm], axis=0)


def plane_gather_second(a, b):
    return from_x(a, 1), from_z(b, 1), from_x(a, -1), from_z(b, -1)


def split_kernel(ap, bp, am, bm, *outs):
    for ref, out in zip((ap, bp, am, bm), outs):
        out[...] = ref[...]


def split(a_plus, b_plus, a_minus, b_minus):
    first = pl.BlockSpec((1, ROWS, HALF), lambda i: (i, 0, 0))
    second = pl.BlockSpec((1, ROWS, HALF), lambda i: (2 + i, 0, 0))
    return pl.pallas_call(
        split_kernel,
        grid=(2,),
        out_shape=(jax.ShapeDtypeStruct((2, ROWS, HALF), BF),) * 4,
        in_specs=[first, first, second, second],
        out_specs=[first] * 4,
        compiler_params=pltpu.CompilerParams(vmem_limit_bytes=VMEM),
        cost_estimate=pl.CostEstimate(flops=0, bytes_accessed=4_000_000, transcendentals=0),
        name="split",
    )(a_plus, b_plus, a_minus, b_minus)


def plane_gather_last(a_low, b_low, a_high, b_high):
    return from_x(a_low, 1), from_z(b_low, 1), from_x(a_high, -1), from_z(b_high, -1)


def add_low(a, b):
    return low(wide(a) + wide(b))


def relay_kernel(a1, a3, b1, b3, al, ah, bl, bh, a1o, a3o, b1o, b3o):
    for own, got, out in ((a1, al, a1o), (a3, ah, a3o), (b1, bl, b1o), (b3, bh, b3o)):
        out[...] = add_low(own[...], got[...])


def relay(a1, a3, b1, b3, al, ah, bl, bh):
    first = pl.BlockSpec((1, EXTRA, HALF), lambda i: (i, 0, 0))
    second = pl.BlockSpec((1, EXTRA, HALF), lambda i: (2 + i, 0, 0))
    shape = jax.ShapeDtypeStruct(a1.shape, BF)
    return pl.pallas_call(
        relay_kernel,
        grid=(2,),
        out_shape=(shape,) * 4,
        in_specs=[first, second] * 2 + [first] * 4,
        out_specs=[first, second] * 2,
        input_output_aliases={k: k for k in range(4)},
        compiler_params=pltpu.CompilerParams(vmem_limit_bytes=VMEM),
        cost_estimate=pl.CostEstimate(flops=2_000_000, bytes_accessed=7_000_000, transcendentals=0),
        name="relay",
    )(a1, a3, b1, b3, al, ah, bl, bh)


def fold_kernel(a0, qa, ra, b0, qb, rb, *outs):
    for own, q, r, to in ((a0, qa, ra, outs[:4]), (b0, qb, rb, outs[4:])):
        for k in range(4):
            to[k][...] = low(wide(own[k]) + wide(q[k]) + wide(r[k]))


def fold(*terms):
    vmem = pl.BlockSpec(memory_space=pltpu.VMEM)
    return pl.pallas_call(
        fold_kernel,
        out_shape=(jax.ShapeDtypeStruct((EXTRA, HALF), BF),) * 8,
        in_specs=[vmem] * 6,
        out_specs=[vmem] * 8,
        compiler_params=pltpu.CompilerParams(vmem_limit_bytes=VMEM),
        cost_estimate=pl.CostEstimate(flops=3_000_000, bytes_accessed=9_000_000, transcendentals=0),
        name="fold",
    )(*terms)


def first_sums(a, b):
    return from_x(a[2], -1), from_z(b[2], -1), from_x(a[3], 1), from_z(b[3], 1)


def second_sums(a, b, far):
    al, bl, ah, bh = far
    a1, a3, b1, b3 = relay(a[1], a[4], b[1], b[4], al, ah, bl, bh)
    return from_x(a1, -1), from_z(b1, -1), from_x(a3, 1), from_z(b3, 1)


def ring_position(dp):
    return dp // 8, (dp // 2) % 4, dp % 2


def spread_kernel(x_ref, keep, got, *blocks):
    for r, ref in enumerate(blocks):
        at = pl.ds(pl.multiple_of(lax.rem(x_ref[0] + r, 4) * PART, 16), PART)
        ref[...] = low(wide(keep[at, :]) + wide(got[at, :]))


def collect_kernel(x_ref, *refs):
    for r, ref in enumerate(refs[:4]):
        at = pl.ds(pl.multiple_of(lax.rem(x_ref[0] + r, 4) * PART, 16), PART)
        refs[4][at, :] = ref[...]


def dp_spread(x, keep, got):
    vmem = pl.BlockSpec(memory_space=pltpu.VMEM)
    return pl.pallas_call(
        spread_kernel,
        out_shape=(jax.ShapeDtypeStruct((PART, WIDTH), BF),) * 4,
        in_specs=[pl.BlockSpec(memory_space=pltpu.SMEM), vmem, vmem],
        out_specs=[vmem] * 4,
        compiler_params=pltpu.CompilerParams(vmem_limit_bytes=VMEM),
        name="spread",
    )(x, keep, got)


def plane_exchange(s):
    return low(wide(s) + wide(from_z(s, 2)) + wide(from_z(s, 1)) + wide(from_z(s, -1)))


def dp_collect(x, s):
    vmem = pl.BlockSpec(memory_space=pltpu.VMEM)
    return pl.pallas_call(
        collect_kernel,
        out_shape=jax.ShapeDtypeStruct((HALF_ROWS, WIDTH), BF),
        in_specs=[pl.BlockSpec(memory_space=pltpu.SMEM)] + [vmem] * 4,
        out_specs=vmem,
        compiler_params=pltpu.CompilerParams(vmem_limit_bytes=VMEM),
        name="collect",
    )(x, s, from_x(s, 1), from_x(s, 2), from_x(s, -1))


def totals_kernel(a, b, c, d, gain, router, moe, attn):
    total = wide(a[...]) + wide(b[...]) + wide(c[...]) + wide(d[...])
    router[...] = total[:32]
    moe[...] = total[32:33] + total[33:34]
    attn[...] = (total[34:35] + total[35:36]) / gain[...]


def totals(ins):
    vmem = pl.BlockSpec(memory_space=pltpu.VMEM)
    return pl.pallas_call(
        totals_kernel,
        out_shape=(
            jax.ShapeDtypeStruct((32, WIDTH), F32),
            jax.ShapeDtypeStruct((1, WIDTH), F32),
            jax.ShapeDtypeStruct((1, WIDTH), F32),
        ),
        in_specs=[vmem] * 5,
        out_specs=[vmem] * 3,
        compiler_params=pltpu.CompilerParams(vmem_limit_bytes=VMEM),
        name="totals",
    )(*ins)


def _block_starts(y):
    starts = []
    for r in range(4):
        off = lax.rem(y + r, 4) * ROWS
        if r == 2:
            starts += [off, off + ROWS // 2]
        else:
            starts.append(off)
    return [pl.multiple_of(s, 128) for s in starts]


def attention_forward_kernel(
    y_ref, n0, n1, n2, n3, n4, w_ref, wo_ref, cos_ref, sin_ref,
    qkv_ref, o_ref, lse_ref, p0, p1, p2, p3, p4,
):
    starts = _block_starts(y_ref[0])
    for start, ref in zip(starts, (n0, n1, n2, n3, n4)):
        width = ref.shape[0]
        at = pl.ds(start, width)
        t = mm(w_ref[...], ref[...], NT)
        cos, sin = cos_ref[:, at], sin_ref[:, at]
        for h in range(6):
            a, b = t[64 * h : 64 * h + 32], t[64 * h + 32 : 64 * h + 64]
            ra, rb = a * cos - b * sin, b * cos + a * sin
            if h < 4:
                ra, rb = ra * 0.125, rb * 0.125
            qkv_ref[64 * h : 64 * h + 32, at] = low(ra)
            qkv_ref[64 * h + 32 : 64 * h + 64, at] = low(rb)
        qkv_ref[384:512, at] = low(t[384:])
    key_at = lax.broadcasted_iota(jnp.int32, (ROWS, 2 * ROWS), 0)
    query_at = lax.broadcasted_iota(jnp.int32, (ROWS, 2 * ROWS), 1)
    allowed = key_at <= jnp.bitwise_and(query_at, ROWS - 1)
    for g in range(2):
        keys = qkv_ref[256 + 64 * g : 320 + 64 * g, :].T
        values = qkv_ref[384 + 64 * g : 448 + 64 * g, :]
        for i in range(4):
            here = slice(i * ROWS, (i + 1) * ROWS)
            q2 = jnp.concatenate(
                [qkv_ref[128 * g : 128 * g + 64, here], qkv_ref[128 * g + 64 : 128 * g + 128, here]],
                axis=1,
            )
            tiles = []
            for j in range(i + 1):
                s = mm(keys[j * ROWS : (j + 1) * ROWS], q2)
                if j == i:
                    s = jnp.where(allowed, s, -jnp.inf)
                tiles.append(s)
            peak = tiles[0].max(axis=0, keepdims=True)
            for s in tiles[1:]:
                peak = jnp.maximum(peak, s.max(axis=0, keepdims=True))
            total = jnp.zeros_like(peak)
            mixed = jnp.zeros((HEAD, 2 * ROWS), F32)
            for j, s in enumerate(tiles):
                e = jnp.exp(s - peak)
                total = total + e.sum(axis=0, keepdims=True)
                mixed = mixed + mm(values[:, j * ROWS : (j + 1) * ROWS], low(e))
            mixed = mixed / total
            lse = peak + jnp.log(total)
            o_ref[128 * g : 128 * g + 64, here] = mixed[:, :ROWS]
            o_ref[128 * g + 64 : 128 * g + 128, here] = mixed[:, ROWS:]
            lse_ref[2 * g : 2 * g + 1, here] = lse[:, :ROWS]
            lse_ref[2 * g + 1 : 2 * g + 2, here] = lse[:, ROWS:]
    lse_ref[4:8, :] = jnp.zeros((4, SEQ), F32)
    for start, ref in zip(starts, (p0, p1, p2, p3, p4)):
        att = low(o_ref[:, pl.ds(start, ref.shape[0])])
        ref[...] = low(mm(att.T, wo_ref[...]))


PIECES = (ROWS, ROWS, ROWS // 2, ROWS // 2, ROWS)


def attention_forward(y, blocks, w_t, w_out, cos, sin):
    smem = pl.BlockSpec(memory_space=pltpu.SMEM)
    vmem = pl.BlockSpec(memory_space=pltpu.VMEM)
    return pl.pallas_call(
        attention_forward_kernel,
        out_shape=(
            jax.ShapeDtypeStruct((512, SEQ), BF),
            jax.ShapeDtypeStruct((256, SEQ), F32),
            jax.ShapeDtypeStruct((8, SEQ), F32),
            *[jax.ShapeDtypeStruct((w, WIDTH), BF) for w in PIECES],
        ),
        in_specs=[smem] + [vmem] * 9,
        out_specs=[vmem] * 8,
        compiler_params=pltpu.CompilerParams(vmem_limit_bytes=VMEM),
        cost_estimate=pl.CostEstimate(flops=8_000_000_000, bytes_accessed=10_000_000, transcendentals=3_000_000),
        name="attention_forward",
    )(y, *blocks, w_t, w_out, cos, sin)


def attention_backward_kernel(
    at_ref, d0, d1, d2, d3, d4, x0, x1, x2, x3, x4, qkv_ref, o_ref, lse_ref, wo_ref, wa_ref, wb_ref, cos_ref, sin_ref,
    small_ref, keep_ref, send_ref, p0, p1, p2, p3, p4, do_ref, delta_ref, dk_ref, dv_ref, dqkv_ref,
):
    starts = _block_starts(at_ref[0])
    core = at_ref[1]

    def put(half, first, value):
        rows = slice(first, first + value.shape[0])

        @pl.when(core == half)
        def _():
            keep_ref[rows, :] = value

        @pl.when(core != half)
        def _():
            send_ref[rows, :] = value

    total = jnp.zeros((256, WIDTH), F32)
    for start, ref in zip(starts, (d0, d1, d2, d3, d4)):
        at = pl.ds(start, ref.shape[0])
        do_ref[:, at] = low(mm(wo_ref[...], ref[...], NT))
        total = total + mm(low(o_ref[:, at]), ref[...])
    put(0, 256, low(total[:128]))
    put(1, 256, low(total[128:]))
    put(0, 384, jnp.zeros((64, WIDTH), BF))
    put(1, 384, small_ref[...])
    prod = o_ref[...] * wide(do_ref[...])
    for h in range(4):
        delta_ref[h : h + 1, :] = prod[64 * h : 64 * h + 64].sum(axis=0, keepdims=True)
    key_at = lax.broadcasted_iota(jnp.int32, (ROWS, 2 * ROWS), 0)
    query_at = lax.broadcasted_iota(jnp.int32, (ROWS, 2 * ROWS), 1)
    allowed = key_at <= jnp.bitwise_and(query_at, ROWS - 1)
    for g in range(2):
        keys_t = qkv_ref[256 + 64 * g : 320 + 64 * g, :]
        keys = keys_t.T
        values = qkv_ref[384 + 64 * g : 448 + 64 * g, :].T
        dk_ref[...] = jnp.zeros_like(dk_ref)
        dv_ref[...] = jnp.zeros_like(dv_ref)
        base = 256 * g
        for i in range(4):
            here = slice(i * ROWS, (i + 1) * ROWS)

            def pair(ref, base, step):
                return jnp.concatenate(
                    [ref[base : base + step, here], ref[base + step : base + 2 * step, here]], axis=1
                )

            q2 = pair(qkv_ref, 128 * g, 64)
            do2 = pair(do_ref, 128 * g, 64)
            lse2 = pair(lse_ref, 2 * g, 1)
            delta2 = pair(delta_ref, 2 * g, 1)
            dq = jnp.zeros((HEAD, 2 * ROWS), F32)
            for j in range(i + 1):
                at = slice(j * ROWS, (j + 1) * ROWS)
                s = mm(keys[at], q2)
                p = jnp.exp(s - lse2)
                if j == i:
                    p = jnp.where(allowed, p, 0.0)
                dp = mm(values[at], do2)
                ds = low(p * (dp - delta2))
                dq = dq + mm(keys_t[:, at], ds)
                dk_ref[:, at] += mm(q2, ds, NT)
                dv_ref[:, at] += mm(do2, low(p), NT)
            cos, sin = cos_ref[:, here], sin_ref[:, here]
            dq = dq * 0.125
            for h in range(2):
                a, b = dq[:32, h * ROWS : (h + 1) * ROWS], dq[32:, h * ROWS : (h + 1) * ROWS]
                dqkv_ref[base + 64 * h : base + 64 * h + 32, here] = low(a * cos + b * sin)
                dqkv_ref[base + 64 * h + 32 : base + 64 * h + 64, here] = low(b * cos - a * sin)
        a, b = dk_ref[:32, :], dk_ref[32:, :]
        dqkv_ref[base + 128 : base + 160, :] = low(a * cos_ref[...] + b * sin_ref[...])
        dqkv_ref[base + 160 : base + 192, :] = low(b * cos_ref[...] - a * sin_ref[...])
        dqkv_ref[base + 192 : base + 256, :] = low(dv_ref[...])
        total = jnp.zeros((256, WIDTH), F32)
        for start, ref in zip(starts, (x0, x1, x2, x3, x4)):
            total = total + mm(dqkv_ref[base : base + 256, pl.ds(start, ref.shape[0])], ref[...])
        put(g, 0, low(total))
    for start, ref in zip(starts, (p0, p1, p2, p3, p4)):
        at = pl.ds(start, ref.shape[0])
        ref[...] = low(mm(dqkv_ref[:256, at].T, wa_ref[...]) + mm(dqkv_ref[256:, at].T, wb_ref[...]))


def attention_backward(at, d_blocks, x_blocks, qkv, o, lse, w_out, wa, wb, cos, sin, small):
    smem = pl.BlockSpec(memory_space=pltpu.SMEM)
    vmem = pl.BlockSpec(memory_space=pltpu.VMEM)
    return pl.pallas_call(
        attention_backward_kernel,
        out_shape=(
            *[jax.ShapeDtypeStruct((HALF_ROWS, WIDTH), BF)] * 2,
            *[jax.ShapeDtypeStruct((w, WIDTH), BF) for w in PIECES],
        ),
        in_specs=[smem] + [vmem] * 19,
        out_specs=[vmem] * 7,
        scratch_shapes=[
            pltpu.VMEM((256, SEQ), BF),
            pltpu.VMEM((8, SEQ), F32),
            pltpu.VMEM((64, SEQ), F32),
            pltpu.VMEM((64, SEQ), F32),
            pltpu.VMEM((512, SEQ), BF),
        ],
        compiler_params=pltpu.CompilerParams(vmem_limit_bytes=VMEM),
        cost_estimate=pl.CostEstimate(flops=20_000_000_000, bytes_accessed=15_000_000, transcendentals=3_000_000),
        name="attention_backward",
    )(at, *d_blocks, *x_blocks, qkv, o, lse, w_out, wa, wb, cos, sin, small)


def finish_kernel(core_ref, half, other, wa_ref, wb_ref, gq, gk, gv, go, rest):
    core = core_ref[0]

    def unpack(first, second):
        lines = jnp.zeros((1, WIDTH), F32)
        for g, (ref, w_ref) in enumerate(((first, wa_ref), (second, wb_ref))):
            grads = wide(ref[:256, :])
            lines = lines + (grads * wide(w_ref[...])).sum(axis=0, keepdims=True)
            gq[:, 128 * g : 128 * g + 128] = grads[:128].T
            turned = grads[128:].T
            gk[:, 64 * g : 64 * g + 64] = turned[:, :64]
            gv[:, 64 * g : 64 * g + 64] = turned[:, 64:]
            go[128 * g : 128 * g + 128, :] = wide(ref[256:384, :])
        rest[:32, :] = second[384:416, :]
        gains = wide(second[416:418, :]).sum(axis=0, keepdims=True)
        high, high2 = low(gains), low(lines)
        rows = [wide(high), gains - wide(high), wide(high2), lines - wide(high2), jnp.zeros((12, WIDTH), F32)]
        rest[32:, :] = low(jnp.concatenate(rows, axis=0))

    @pl.when(core == 0)
    def _():
        unpack(half, other)

    @pl.when(core != 0)
    def _():
        unpack(other, half)


def finish(core, half, other, wa, wb):
    smem = pl.BlockSpec(memory_space=pltpu.SMEM)
    vmem = pl.BlockSpec(memory_space=pltpu.VMEM)
    return pl.pallas_call(
        finish_kernel,
        out_shape=(
            jax.ShapeDtypeStruct((WIDTH, 256), F32),
            jax.ShapeDtypeStruct((WIDTH, 128), F32),
            jax.ShapeDtypeStruct((WIDTH, 128), F32),
            jax.ShapeDtypeStruct((256, WIDTH), F32),
            jax.ShapeDtypeStruct((48, WIDTH), BF),
        ),
        in_specs=[smem] + [vmem] * 4,
        out_specs=[vmem] * 5,
        compiler_params=pltpu.CompilerParams(vmem_limit_bytes=VMEM),
        cost_estimate=pl.CostEstimate(flops=3_000_000, bytes_accessed=6_000_000, transcendentals=0),
        name="finish",
    )(core, half, other, wa, wb)


def hidden_gradient_kernel(
    a0, a1, a2, b0, b1, b2, normed, hidden, gain, cot, named, w_ref, expert_ref, d_ref, low_ref, small_ref
):
    in_a = wide(a0[...]) + wide(a1[...]) + wide(a2[...])
    in_b = wide(b0[...]) + wide(b1[...]) + wide(b2[...])
    routed = in_a[ROWS:] + in_b[ROWS:]
    d_route = jnp.concatenate([routed[:, :ROWS], routed[:, ROWS:]], axis=0)
    picked = named[...] > 0.5
    logits = jnp.where(picked, mm(w_ref[...], normed[...], NT), -jnp.inf)
    powers = jnp.where(picked, jnp.exp(logits - logits.max(axis=0, keepdims=True)), 0.0)
    gates = powers / powers.sum(axis=0, keepdims=True)
    d_logits = low(gates * (d_route - (gates * d_route).sum(axis=0, keepdims=True)))
    d_normed = mm(d_logits, w_ref[...], TN) + jnp.concatenate([in_a[:ROWS], in_b[:ROWS]], axis=1)
    x = hidden[...]
    r = norm_scale(x)
    u = d_normed * gain[...]
    d = wide(cot[...]) + r * u - x * (r * r * r * jnp.mean(u * x, axis=1, keepdims=True))
    d_ref[...] = d
    low_ref[...] = low(d)
    small_ref[:32, :] = low(mm(expert_ref[...], low(mm(d_logits, normed[...]))))
    gains = (d_normed * (x * r)).sum(axis=0, keepdims=True)
    high = wide(low(gains))
    small_ref[32:, :] = low(jnp.concatenate([high, gains - high, jnp.zeros((30, WIDTH), F32)], axis=0))


def hidden_gradient(*ins):
    vmem = pl.BlockSpec(memory_space=pltpu.VMEM)
    return pl.pallas_call(
        hidden_gradient_kernel,
        out_shape=(
            jax.ShapeDtypeStruct((ROWS, WIDTH), F32),
            jax.ShapeDtypeStruct((ROWS, WIDTH), BF),
            jax.ShapeDtypeStruct((64, WIDTH), BF),
        ),
        in_specs=[vmem] * 13,
        out_specs=[vmem] * 3,
        compiler_params=pltpu.CompilerParams(vmem_limit_bytes=VMEM),
        cost_estimate=pl.CostEstimate(flops=60_000_000, bytes_accessed=6_000_000, transcendentals=10_000),
        name="hidden_gradient",
    )(*ins)


def relay_rows_kernel(plus, minus, first, second, plus_out, minus_out):
    plus_out[...] = add_low(plus[...], first[...])
    minus_out[...] = add_low(minus[...], second[...])


def relay_rows(plus, minus, first, second):
    lower = pl.BlockSpec((ROWS // 2, WIDTH), lambda i: (0, 0))
    upper = pl.BlockSpec((ROWS // 2, WIDTH), lambda i: (1, 0))
    return pl.pallas_call(
        relay_rows_kernel,
        grid=(1,),
        out_shape=(jax.ShapeDtypeStruct((ROWS, WIDTH), BF),) * 2,
        in_specs=[lower, upper, lower, lower],
        out_specs=[lower, upper],
        input_output_aliases={0: 0, 1: 1},
        compiler_params=pltpu.CompilerParams(vmem_limit_bytes=VMEM),
        cost_estimate=pl.CostEstimate(flops=300_000, bytes_accessed=1_500_000, transcendentals=0),
        name="relay_rows",
    )(plus, minus, first, second)


SHARD = WIDTH + 512


FAR_STEPS = (((2, 0), (2, 1), (2, 2), (2, 3)), ((0, 2), (1, 2), (3, 2)))
NEAR_STEPS = tuple(tuple((x, z) for z in (0, 1, 3)) for x in (0, 1, 3))
EARLY_STEPS, NEAR_STEPS = NEAR_STEPS[:1], NEAR_STEPS[1:]


def member(pieces, outer, inner):
    if outer == 2:
        return pieces[2 + inner // 2].at[inner % 2]
    return pieces[(0, 1, None, 4)[outer]].at[inner]


def expert_kernel(steps, kept, far, at_ref, *refs):
    ta, tb, (cot_ref, pos_ref, hot_ref, wr_ref), weights, refs = refs[:5], refs[5:10], refs[10:14], refs[14:16], refs[16:]
    refs = refs[kept:]
    stacks, (a0, a1, a4, b0, b1, b4, out_ref), refs = refs[:4], refs[4:11], refs[11:]
    (a2, a3, b2, b3), refs = (refs[:4], refs[4:]) if far else ((None,) * 4, refs)
    da, db = (a0, a1, a2, a3, a4), (b0, b1, b2, b3, b4)
    (tok_scr, cot_scr, wgu_scr, wd_scr, x_scr, dx_scr, act_scr, dgu_scr, g_scr, m_scr, y_scr, p_scr, out_scr), refs = (
        refs[:13], refs[13:],
    )
    w_sem, in_sem, stack_sem, out_sem = refs
    place = wide(lax.broadcasted_iota(jnp.int32, (CAP, ROWS), 0))
    z_of = [lax.rem(at_ref[2] + k, 4) for k in range(4)]
    x_of = [lax.rem(at_ref[3] + k, 4) for k in range(4)]
    chip = at_ref[2] * 4 + at_ref[3]
    first = lax.rem(at_ref[0], 2) == 0
    line = lax.broadcasted_iota(jnp.int32, (16, HALF), 0) == chip
    both = range(2)

    def weight_copies():
        copies = []
        for e, whole in enumerate(weights):
            for r in range(4):
                ref = whole.at[r]
                cols = pl.ds(128 * r, 128)
                moves = [
                    (ref.at[pl.ds(0, WIDTH), pl.ds(0, 128)], wgu_scr.at[e, :, cols]),
                    (ref.at[pl.ds(0, WIDTH), pl.ds(128, 128)], wgu_scr.at[e, :, pl.ds(FF + 128 * r, 128)]),
                ]
                for c in range(4):
                    moves.append((ref.at[pl.ds(WIDTH + 128 * c, 128), :], wd_scr.at[e, cols, pl.ds(256 * c, 256)]))
                for source, target in moves:
                    copies.append(pltpu.make_async_copy(source, target, w_sem.at[len(copies)]))
        return copies

    def in_copies(n):
        copies = []
        for k, (x, z) in enumerate(steps[n]):
            to = tok_scr.at[n % 2, k]
            for source, target in (
                (member(ta, x, z), to.at[:, pl.ds(0, HALF)]),
                (member(tb, z, x), to.at[:, pl.ds(HALF, HALF)]),
                (cot_ref.at[z_of[z], x_of[x], pl.ds(0, ROWS)], cot_scr.at[n % 2, k]),
            ):
                copies.append(pltpu.make_async_copy(source, target, in_sem.at[n % 2, len(copies)]))
        return copies

    def stack_copies(n):
        rows, base = len(steps[n]) * CAP, sum(len(step) for step in steps[:n]) * CAP
        return [
            pltpu.make_async_copy(
                scr.at[n % 2, :, pl.ds(0, rows)], ref.at[:, pl.ds(base, rows)], stack_sem.at[n % 2, i]
            )
            for i, (scr, ref) in enumerate(zip((x_scr, dx_scr, act_scr, dgu_scr), stacks))
        ]

    def out_copies(n):
        copies = []
        for k, (x, z) in enumerate(steps[n]):
            dense = out_scr.at[n % 2, k]
            for source, target in (
                (dense.at[pl.ds(0, EXTRA), pl.ds(0, HALF)], member(da, x, z)),
                (dense.at[pl.ds(0, EXTRA), pl.ds(HALF, HALF)], member(db, z, x)),
                (dense.at[pl.ds(EXTRA, ROWS)], out_ref.at[z_of[z], x_of[x]]),
            ):
                copies.append(pltpu.make_async_copy(source, target, out_sem.at[n % 2, len(copies)]))
        return copies

    for copy in in_copies(0) + weight_copies():
        copy.start()
    for n, step in enumerate(steps):
        slot, count = n % 2, len(step)
        rows = count * CAP
        lane = lax.broadcasted_iota(jnp.int32, (rows, SLOTS), 1)
        for copy in in_copies(n):
            copy.wait()
        if n + 1 < len(steps):
            for copy in in_copies(n + 1):
                copy.start()
        if n >= 2:
            for copy in stack_copies(n - 2) + out_copies(n - 2):
                copy.wait()
        for k, (x, z) in enumerate(step):
            pos = pos_ref[z_of[z], x_of[x]]
            pick = jnp.concatenate([low(wide(place == pos[e : e + 1, :])) for e in both], axis=0)
            p_scr[k] = pick
            xs, gs = low(mm(pick, tok_scr[slot, k])), low(mm(pick, cot_scr[slot, k]))
            ms = mm(pick, hot_ref[z_of[z], x_of[x]], NT)
            for e in both:
                at = slice(k * CAP, (k + 1) * CAP)
                x_scr[slot, e, at, :] = xs[e * CAP : (e + 1) * CAP]
                g_scr[e, at, :] = gs[e * CAP : (e + 1) * CAP]
                m_scr[e, at, :] = ms[e * CAP : (e + 1) * CAP]
        if n == 0:
            for copy in weight_copies():
                copy.wait()
        gu = [mm(x_scr[slot, e, :rows], wgu_scr[e]) for e in both]
        logits = [mm(x_scr[slot, e, :rows], wr_ref[...]) for e in both]
        sig = [jax.nn.sigmoid(gu[e][:, :FF]) for e in both]
        for e in both:
            act_scr[slot, e, :rows] = low(gu[e][:, :FF] * sig[e] * gu[e][:, FF:])
        out = [low(mm(act_scr[slot, e, :rows], wd_scr[e])) for e in both]
        gate = []
        for e in both:
            named = m_scr[e, :rows] > 0.5
            found = jnp.where(named, logits[e], -1e30)
            powers = jnp.where(named, jnp.exp(found - found.max(axis=1, keepdims=True)), 0.0)
            total = powers.sum(axis=1, keepdims=True)
            mine = jnp.where(lane == at_ref[e], powers, 0.0).sum(axis=1, keepdims=True)
            gate.append(mine / jnp.where(total > 0.0, total, 1.0))
            dx_scr[slot, e, :rows] = low(gate[e] * wide(g_scr[e, :rows]))
        d_act = [mm(dx_scr[slot, e, :rows], wd_scr[e], NT) for e in both]
        d_route = []
        for e in both:
            d_route.append((wide(out[e]) * wide(g_scr[e, :rows])).sum(axis=1, keepdims=True))
            y_scr[0, e, :rows] = low(gate[e] * wide(out[e]))
        for e in both:
            pre, up = gu[e][:, :FF], gu[e][:, FF:]
            dgu_scr[slot, e, :rows, :FF] = low(d_act[e] * up * sig[e] * (1.0 + pre * (1.0 - sig[e])))
            dgu_scr[slot, e, :rows, FF:] = low(d_act[e] * (pre * sig[e]))
        for copy in stack_copies(n):
            copy.start()
        for e in both:
            y_scr[1, e, :rows] = low(mm(dgu_scr[slot, e, :rows], wgu_scr[e], NT))
        for k in range(count):
            at = slice(k * CAP, (k + 1) * CAP)
            pick_t = p_scr[k].T
            dense = low(mm(pick_t, jnp.concatenate([y_scr[1, e, at, :] for e in both], axis=0)))
            out_scr[slot, k, :ROWS] = dense
            own, other = [
                (wide(p_scr[k, e * CAP : (e + 1) * CAP, :]) * d_route[e][at]).sum(axis=0, keepdims=True) for e in both
            ]
            pair = jnp.concatenate([jnp.where(first, own, other), jnp.where(first, other, own)], axis=1)
            high = wide(low(pair))
            out_scr[slot, k, ROWS:EXTRA, :HALF] = low(jnp.where(line, high, 0.0))
            out_scr[slot, k, ROWS:EXTRA, HALF:] = low(jnp.where(line, pair - high, 0.0))
            dense = low(mm(pick_t, jnp.concatenate([y_scr[0, e, at, :] for e in both], axis=0)))
            out_scr[slot, k, EXTRA:] = dense
        for copy in out_copies(n):
            copy.start()
    for n in range(max(0, len(steps) - 2), len(steps)):
        for copy in stack_copies(n) + out_copies(n):
            copy.wait()


def experts(steps, at, tok_a, tok_b, cot, pos, hot, w_router, weights, partial=()):
    far = any(2 in member for step in steps for member in step)
    smem = pl.BlockSpec(memory_space=pltpu.SMEM)
    vmem = pl.BlockSpec(memory_space=pltpu.VMEM)
    anywhere = pl.BlockSpec(memory_space=pl.ANY)
    rows, most = sum(len(step) for step in steps) * CAP, max(len(step) for step in steps)
    widths = (WIDTH, WIDTH, FF, 2 * FF)
    ins = (at, *tok_a, *tok_b, cot, pos, hot, w_router, *weights, *partial)
    return pl.pallas_call(
        functools.partial(expert_kernel, steps, len(partial), far),
        out_shape=(
            *[jax.ShapeDtypeStruct((2, rows, width), BF) for width in widths],
            *[jax.ShapeDtypeStruct((4, EXTRA, HALF), BF)] * 6,
            jax.ShapeDtypeStruct((4, 4, ROWS, WIDTH), BF),
            *[jax.ShapeDtypeStruct((2, EXTRA, HALF), BF)] * (4 * far),
        ),
        in_specs=[smem, *[anywhere] * 11, vmem, vmem, vmem, *[anywhere] * (2 + len(partial))],
        out_specs=[anywhere] * (11 + 4 * far),
        scratch_shapes=[
            pltpu.VMEM((2, most, ROWS, WIDTH), BF),
            pltpu.VMEM((2, most, ROWS, WIDTH), BF),
            pltpu.VMEM((2, WIDTH, 2 * FF), BF),
            pltpu.VMEM((2, FF, WIDTH), BF),
            *[pltpu.VMEM((2, 2, most * CAP, width), BF) for width in widths],
            pltpu.VMEM((2, most * CAP, WIDTH), BF),
            pltpu.VMEM((2, most * CAP, SLOTS), F32),
            pltpu.VMEM((2, 2, most * CAP, WIDTH), BF),
            pltpu.VMEM((most, 2 * CAP, ROWS), BF),
            pltpu.VMEM((2, most, EXTRA + ROWS, WIDTH), BF),
            pltpu.SemaphoreType.DMA((48,)),
            pltpu.SemaphoreType.DMA((2, 3 * most)),
            pltpu.SemaphoreType.DMA((2, 4)),
            pltpu.SemaphoreType.DMA((2, 3 * most)),
        ],
        input_output_aliases={17 + k: 4 + k for k in range(len(partial))},
        compiler_params=pltpu.CompilerParams(vmem_limit_bytes=VMEM),
        cost_estimate=pl.CostEstimate(flops=rows * 10_000_000, bytes_accessed=rows * 20_000, transcendentals=rows * 1_000),
        name="experts",
    )(*ins)


def expert_gradient_kernel(*refs):
    (x, dx, act, dgu), outs = [
        jnp.concatenate([refs[4 * k + i][0] for k in range(3)], axis=0) for i in range(4)
    ], refs[12:]
    gu = low(mm(x.T, dgu))
    gd = low(mm(act, dx, TN))
    for i, ref in enumerate(outs):

        @pl.when(pl.program_id(0) == i)
        def _(ref=ref):
            for r in range(4):
                cols = slice(128 * r, 128 * r + 128)
                ref[r, :WIDTH, :128] = gu[:, cols]
                ref[r, :WIDTH, 128:] = gu[:, FF + 128 * r : FF + 128 * r + 128]
                for c in range(4):
                    ref[r, WIDTH + 128 * c : WIDTH + 128 * c + 128, :] = gd[cols, 256 * c : 256 * c + 256]


def expert_gradients(*sets):
    stacks = [v for one in sets for v in one]
    whole = pl.BlockSpec((4, SHARD, 256), lambda i: (0, 0, 0))
    return pl.pallas_call(
        expert_gradient_kernel,
        grid=(2,),
        out_shape=(jax.ShapeDtypeStruct((4, SHARD, 256), BF),) * 2,
        in_specs=[pl.BlockSpec((1, *v.shape[1:]), lambda i: (1 - i, 0, 0)) for v in stacks],
        out_specs=[whole, whole],
        compiler_params=pltpu.CompilerParams(vmem_limit_bytes=VMEM),
        cost_estimate=pl.CostEstimate(flops=18_000_000_000, bytes_accessed=28_000_000, transcendentals=0),
        name="expert_gradients",
    )(*stacks)


def merge_kernel(a_ref, b_ref, out):
    out[...] = add_low(a_ref[...], b_ref[...])


def merge(a, b):
    spec = pl.BlockSpec((1, SHARD, 256), lambda i: (i, 0, 0))
    return pl.pallas_call(
        merge_kernel,
        grid=(4,),
        out_shape=jax.ShapeDtypeStruct(a.shape, BF),
        in_specs=[spec] * 2,
        out_specs=spec,
        compiler_params=pltpu.CompilerParams(vmem_limit_bytes=VMEM),
        cost_estimate=pl.CostEstimate(flops=2_000_000, bytes_accessed=10_000_000, transcendentals=0),
        name="merge",
    )(a, b)


def after(value, *others):
    return lax.optimization_barrier((value, *others))[0]


def norm_scale(x):
    return lax.rsqrt(jnp.mean(x * x, axis=-1, keepdims=True) + NORM_EPS)


def shards(
    tokens, cotangent, gain_attn, w_query, w_key, w_value, w_out, gain_moe, w_router,
    w_gate, w_up, w_down, routes, owner_map,
):
    dp = lax.axis_index("dp")
    y = lax.axis_index("tensor").astype(jnp.int32).reshape(1)
    z_at, x_at, core = ring_position(dp)

    x_in = wide(tokens)
    scale_a = norm_scale(x_in)
    normed_a = low(x_in * scale_a * gain_attn)
    x_blocks = (normed_a, *gather_direct(normed_a, from_y))

    slot_ids = jnp.arange(SLOTS, dtype=jnp.int32)
    picks = routes[:, :, None] == slot_ids[None, None, :]
    route_slots = jnp.sum(jnp.where(picks, owner_map[None, None, :], 0), axis=-1)
    hot = low(jnp.any(route_slots.T[:, None, :] == slot_ids[None, :, None], axis=0))
    row_slots = jnp.concatenate([slot_ids[0::2], slot_ids[1::2]])
    named = wide(jnp.any(route_slots.T[:, None, :] == row_slots[None, :, None], axis=0))
    row_experts = low(row_slots[:, None] == owner_map[None, :])
    router_by_row = low(mm(row_experts, w_router, NT))

    sent = jnp.concatenate([cotangent, hot.reshape(8, WIDTH), jnp.zeros((8, WIDTH), BF)], axis=0)
    cot = lax.all_gather(sent, "dp", axis=0, axis_index_groups=PLANE).reshape(4, 4, EXTRA, WIDTH)

    half = HEAD // 2
    inv_freq = jnp.exp(jnp.arange(half).astype(F32) * (-2.0 * math.log(10000.0) / HEAD))
    angles = inv_freq[:, None] * jnp.arange(SEQ).astype(F32)[None, :]
    cos, sin = jnp.cos(angles), jnp.sin(angles)
    w_cat_t = jnp.concatenate([w_query, w_key, w_value], axis=1).T

    qkv, o_t, lse, *parts = attention_forward(y, x_blocks, w_cat_t, w_out, cos, sin)
    hidden = x_in + sum_direct(*parts, from_y)
    normed_m = low(hidden * norm_scale(hidden) * gain_moe)

    down = w_down[0].reshape(128, 4, 256).transpose(1, 0, 2).reshape(512, 256)
    shard = jnp.concatenate([jnp.concatenate([w_gate[0], w_up[0]], axis=1), down], axis=0)
    w_own = lax.all_gather(shard, "tensor", axis=0)
    tok_a, tok_b = plane_gather_first(normed_m)
    row_experts_t = row_experts.T
    tok_a, tok_b, cot, named, router_by_row, row_experts_t = lax.optimization_barrier(
        (tok_a, tok_b, cot, named, router_by_row, row_experts_t)
    )
    hot_all = cot[:, :, ROWS : ROWS + 8].reshape(4, 4, SLOTS, ROWS)
    at = jnp.stack([dp, dp + 1 - 2 * core, z_at, x_at]).astype(jnp.int32)
    mine = jnp.concatenate([lax.dynamic_slice_in_dim(hot_all, at[e], 1, 2) for e in range(2)], axis=2)
    before = low(jnp.arange(ROWS)[:, None] < jnp.arange(ROWS)[None, :])
    rank = jnp.dot(mine.reshape(-1, ROWS), before, preferred_element_type=F32).reshape(mine.shape)
    pos = jnp.where(mine > 0, rank, -1.0)
    by_slot = low(owner_map[:, None] == slot_ids[None, :])
    router_by_slot = low(jnp.dot(w_router, by_slot, preferred_element_type=F32))
    *near, hot_all, at, pos, router_by_slot = lax.optimization_barrier(
        (*plane_gather_second(tok_a, tok_b), hot_all, at, pos, router_by_slot)
    )
    pieces = split(*near)
    far = plane_gather_last(*pieces)
    w_own = after(w_own, *pieces)
    weights = w_own, from_core(w_own)
    table = (cot, pos, hot_all, router_by_slot, weights)
    feeds_early = (at, (tok_a, near[0], *pieces[:2], near[2]), (tok_b, near[1], *pieces[:2], near[3]), *table)
    feeds = (at, (tok_a, near[0], far[0], far[2], near[2]), (tok_b, near[1], far[1], far[3], near[3]), *table)
    early = experts(EARLY_STEPS, *feeds_early)
    outer = experts(FAR_STEPS, *feeds, early[4:])
    a2, a3, b2, b3 = outer[11:]
    far = first_sums((None, None, a2, a3), (None, None, b2, b3))
    near = experts(NEAR_STEPS, *feeds, outer[4:11])
    a0, a1, a4, b0, b1, b4, weighted = near[4:]
    di_a, di_b = (a0, a1, a2, a3, a4), (b0, b1, b2, b3, b4)
    *far, first_stack = lax.optimization_barrier((*far, near[0]))
    relayed = second_sums(di_a, di_b, far)
    other, own = expert_gradients(early[:4], outer[:4], (first_stack, *near[1:4]))
    *relayed, other, own = lax.optimization_barrier((*relayed, other, own))
    qa, qb, ra, rb = relayed
    a0, a1, a2, a3, b0, b1, b2, b3 = fold(di_a[0], qa, ra, di_b[0], qb, rb)
    far = from_z(a2, -1), from_x(b2, -1)
    minus = from_z(a3, 1), from_x(b3, 1)
    both = merge(own, from_core(other))
    *far, both = lax.optimization_barrier((*far, *minus, both))
    far, minus = far[:2], far[2:]
    expert_sum = lax.psum_scatter(both.reshape(4 * SHARD, 256), "tensor", scatter_dimension=0, tiled=True)
    last = from_z(add_low(a1, far[0]), -1), from_x(add_low(b1, far[1]), -1)
    expert_sum = lax.psum_scatter(both.reshape(4 * SHARD, 256), "tensor", scatter_dimension=0, tiled=True)
    terms = (a0, minus[0], last[0], b0, minus[1], last[1])
    d_hidden, d_hidden_low, small = hidden_gradient(
        *terms, normed_m, hidden, gain_moe[None], cotangent, named, router_by_row, row_experts_t
    )
    d_blocks = (d_hidden_low, *gather_direct(d_hidden_low, from_y))

    weighted = after(weighted, *last)
    returned = lax.psum_scatter(
        weighted.reshape(16 * ROWS, WIDTH), "dp", scatter_dimension=0, axis_index_groups=PLANE, tiled=True
    )

    wa = jnp.concatenate([w_cat_t[:128], w_cat_t[256:320], w_cat_t[384:448]], axis=0)
    wb = jnp.concatenate([w_cat_t[128:256], w_cat_t[320:384], w_cat_t[448:]], axis=0)
    core_at = core.astype(jnp.int32).reshape(1)
    keep, send, *d_parts = attention_backward(
        jnp.concatenate([y, core_at]), d_blocks, x_blocks, qkv, o_t, lse, w_out, wa, wb, cos, sin, small
    )

    x_index = x_at.astype(jnp.int32).reshape(1)
    far = from_y(d_parts[2], -1), from_y(d_parts[3], 1)
    blocks = dp_spread(x_index, keep, from_core(send))
    *far, b0, b1, b2, b3 = lax.optimization_barrier((*far, *blocks))
    blocks = b0, b1, b2, b3
    plus, minus = relay_rows(d_parts[1], d_parts[4], *far)
    plus, minus = from_y(plus, -1), from_y(minus, 1)
    s = wide(blocks[0]) + wide(from_x(blocks[2], 2)) + wide(from_x(blocks[1], -1)) + wide(from_x(blocks[3], 1))
    s = plane_exchange(low(s))
    plus, minus, s = lax.optimization_barrier((plus, minus, s))
    d_normed_a = wide(d_parts[0]) + wide(plus) + wide(minus)
    u = d_normed_a * gain_attn
    d_tokens = d_hidden + scale_a * u - x_in * (scale_a**3) * jnp.mean(u * x_in, axis=-1, keepdims=True)

    half_sum = dp_collect(x_index, s)
    half_sum, returned = lax.optimization_barrier((half_sum, returned))
    g_query, g_key, g_value, g_out, rest = finish(core_at, half_sum, from_core(half_sum), wa, wb)
    *rest, expert_sum = lax.optimization_barrier((rest, *[from_y(rest, d) for d in (1, 2, 3)], expert_sum))
    g_router, g_gain_moe, g_gain_attn = totals((*rest, gain_attn[None]))
    expert_sum = wide(expert_sum)
    mixed = low(hidden + wide(returned))
    g_gate, g_up = expert_sum[:WIDTH, :128][None], expert_sum[:WIDTH, 128:][None]
    g_down = expert_sum[WIDTH:].reshape(4, 128, 256).transpose(1, 0, 2).reshape(1, 128, WIDTH)
    return (
        mixed, d_tokens, g_gain_attn[0], g_query, g_key, g_value, g_out, g_gain_moe[0], g_router.T,
        g_gate, g_up, g_down,
    )


def solution(mesh):
    both = P(("dp", "tensor"), None)
    in_specs = (
        both, both, P(), P(None, "tensor"), P(None, "tensor"), P(None, "tensor"), P("tensor", None), P(), P(),
        P("dp", None, "tensor"), P("dp", None, "tensor"), P("dp", "tensor", None), both, P(),
    )
    out_specs = (
        both, both, P(), P(None, "tensor"), P(None, "tensor"), P(None, "tensor"), P("tensor", None), P(), P(),
        P("dp", None, "tensor"), P("dp", None, "tensor"), P("dp", "tensor", None),
    )
    return jax.shard_map(shards, mesh=mesh, in_specs=in_specs, out_specs=out_specs, check_vma=False)
```

```python
import functools
import math

import jax
import jax.numpy as jnp
from jax import lax
from jax.experimental import pallas as pl
from jax.experimental.pallas import tpu as pltpu
from jax.sharding import PartitionSpec as P

BF = jnp.bfloat16
F32 = jnp.float32
NORM_EPS = 1e-05
HEAD = 64
SEQ = 1024
ROWS = 256
WIDTH = 1024
HALF = 512
FF = 512
SLOTS = 32
CAP = 96
MIB = 1024 * 1024
VMEM = 58 * MIB

NN = (((1,), (0,)), ((), ()))
NT = (((1,), (1,)), ((), ()))
TN = (((0,), (0,)), ((), ()))


def mm(a, b, dims=NN):
    return lax.dot_general(a, b, dims, preferred_element_type=F32)


def _dp_pairs(dz, dx, dc):
    pairs = []
    for z in range(4):
        for x in range(4):
            for c in range(2):
                src = ((z + dz) % 4) * 8 + ((x + dx) % 4) * 2 + (c + dc) % 2
                pairs.append((src, z * 8 + x * 2 + c))
    return pairs


def from_z(v, d):
    return lax.ppermute(v, "dp", _dp_pairs(d, 0, 0))


def from_x(v, d):
    return lax.ppermute(v, "dp", _dp_pairs(0, d, 0))


def from_core(v):
    return lax.ppermute(v, "dp", _dp_pairs(0, 0, 1))


def from_y(v, d):
    return lax.ppermute(v, "tensor", [((i + d) % 4, i) for i in range(4)])


def low(v):
    return v.astype(BF)


def wide(v):
    return v.astype(F32)


PLANE = [[2 * chip + c for chip in range(16)] for c in range(2)]
EXTRA = ROWS + 16
PART = 112
HALF_ROWS = 4 * PART


def gather_direct(own, get, cut=None):
    cut = own.shape[0] // 2 if cut is None else cut
    return get(own, 1), get(own[:cut], 2), get(own[cut:], -2), get(own, -1)


def sum_direct(own, plus, far_low, far_high, minus, get):
    far = jnp.concatenate([get(far_low, 2), get(far_high, -2)], axis=0)
    return wide(own) + wide(get(plus, -1)) + wide(get(minus, 1)) + wide(far)


def plane_gather_first(rows):
    a, b = rows[None, :, :HALF], rows[None, :, HALF:]
    ap, bp, am, bm = from_z(a, 1), from_x(b, 1), from_z(a, -1), from_x(b, -1)
    return jnp.concatenate([a, ap, from_z(ap, 1), am], axis=0), jnp.concatenate([b, bp, from_x(bp, 1), bm], axis=0)


def plane_gather_second(a, b):
    return from_x(a, 1), from_z(b, 1), from_x(a, -1), from_z(b, -1)


def split_kernel(ap, bp, am, bm, *outs):
    for ref, out in zip((ap, bp, am, bm), outs):
        out[...] = ref[...]


def split(a_plus, b_plus, a_minus, b_minus):
    first = pl.BlockSpec((1, ROWS, HALF), lambda i: (i, 0, 0))
    second = pl.BlockSpec((1, ROWS, HALF), lambda i: (2 + i, 0, 0))
    return pl.pallas_call(
        split_kernel,
        grid=(2,),
        out_shape=(jax.ShapeDtypeStruct((2, ROWS, HALF), BF),) * 4,
        in_specs=[first, first, second, second],
        out_specs=[first] * 4,
        compiler_params=pltpu.CompilerParams(vmem_limit_bytes=8 * MIB),
        cost_estimate=pl.CostEstimate(flops=0, bytes_accessed=4_000_000, transcendentals=0),
        name="split",
    )(a_plus, b_plus, a_minus, b_minus)


def plane_gather_last(a_low, b_low, a_high, b_high):
    return from_x(a_low, 1), from_z(b_low, 1), from_x(a_high, -1), from_z(b_high, -1)


def add_low(a, b):
    return low(wide(a) + wide(b))


def relay_kernel(a1, a3, b1, b3, al, ah, bl, bh, a1o, a3o, b1o, b3o):
    for own, got, out in ((a1, al, a1o), (a3, ah, a3o), (b1, bl, b1o), (b3, bh, b3o)):
        out[...] = add_low(own[...], got[...])


def relay(a1, a3, b1, b3, al, ah, bl, bh):
    first = pl.BlockSpec((1, EXTRA, HALF), lambda i: (i, 0, 0))
    second = pl.BlockSpec((1, EXTRA, HALF), lambda i: (2 + i, 0, 0))
    shape = jax.ShapeDtypeStruct(a1.shape, BF)
    return pl.pallas_call(
        relay_kernel,
        grid=(2,),
        out_shape=(shape,) * 4,
        in_specs=[first, second] * 2 + [first] * 4,
        out_specs=[first, second] * 2,
        input_output_aliases={k: k for k in range(4)},
        compiler_params=pltpu.CompilerParams(vmem_limit_bytes=12 * MIB),
        cost_estimate=pl.CostEstimate(flops=2_000_000, bytes_accessed=7_000_000, transcendentals=0),
        name="relay",
    )(a1, a3, b1, b3, al, ah, bl, bh)


def fold_kernel(a0, qa, ra, b0, qb, rb, *outs):
    for own, q, r, to in ((a0, qa, ra, outs[:2]), (b0, qb, rb, outs[2:])):
        for k in range(2):
            to[k][...] = low(wide(own[k]) + wide(q[k]) + wide(r[k]))


def fold(half, *terms):
    spec = pl.BlockSpec((2, EXTRA, HALF), lambda i: (half, 0, 0))
    return pl.pallas_call(
        fold_kernel,
        grid=(1,),
        out_shape=(jax.ShapeDtypeStruct((EXTRA, HALF), BF),) * 4,
        in_specs=[spec] * 6,
        out_specs=[pl.BlockSpec((EXTRA, HALF), lambda i: (0, 0))] * 4,
        compiler_params=pltpu.CompilerParams(vmem_limit_bytes=16 * MIB),
        cost_estimate=pl.CostEstimate(flops=1_500_000, bytes_accessed=4_500_000, transcendentals=0),
        name="fold",
    )(*terms)


def first_sums(a, b):
    return from_x(a[2], -1), from_z(b[2], -1), from_x(a[3], 1), from_z(b[3], 1)


def second_sums(a, b, far):
    al, bl, ah, bh = far
    a1, a3, b1, b3 = relay(a[1], a[4], b[1], b[4], al, ah, bl, bh)
    return from_x(a1, -1), from_z(b1, -1), from_x(a3, 1), from_z(b3, 1)


def ring_position(dp):
    return dp // 8, (dp // 2) % 4, dp % 2


def spread_kernel(x_ref, keep, got, *blocks):
    for r, ref in enumerate(blocks):
        at = pl.ds(pl.multiple_of(lax.rem(x_ref[0] + r, 4) * PART, 16), PART)
        ref[...] = low(wide(keep[at, :]) + wide(got[at, :]))


def collect_kernel(x_ref, *refs):
    for r, ref in enumerate(refs[:4]):
        at = pl.ds(pl.multiple_of(lax.rem(x_ref[0] + r, 4) * PART, 16), PART)
        refs[4][at, :] = ref[...]


def dp_spread(x, keep, got):
    vmem = pl.BlockSpec(memory_space=pltpu.VMEM)
    return pl.pallas_call(
        spread_kernel,
        out_shape=(jax.ShapeDtypeStruct((PART, WIDTH), BF),) * 4,
        in_specs=[pl.BlockSpec(memory_space=pltpu.SMEM), vmem, vmem],
        out_specs=[vmem] * 4,
        compiler_params=pltpu.CompilerParams(vmem_limit_bytes=8 * MIB),
        name="spread",
    )(x, keep, got)


def plane_exchange(s):
    return low(wide(s) + wide(from_z(s, 2)) + wide(from_z(s, 1)) + wide(from_z(s, -1)))


def dp_collect(x, s, others):
    vmem = pl.BlockSpec(memory_space=pltpu.VMEM)
    p, f, m, *others = lax.optimization_barrier((from_x(s, 1), from_x(s, 2), from_x(s, -1), *others))
    return pl.pallas_call(
        collect_kernel,
        out_shape=jax.ShapeDtypeStruct((HALF_ROWS, WIDTH), BF),
        in_specs=[pl.BlockSpec(memory_space=pltpu.SMEM)] + [vmem] * 4,
        out_specs=vmem,
        compiler_params=pltpu.CompilerParams(vmem_limit_bytes=8 * MIB),
        name="collect",
    )(x, s, p, f, m), others


def totals_kernel(a, b, c, d, gain, router, moe, attn):
    total = wide(a[...]) + wide(b[...]) + wide(c[...]) + wide(d[...])
    router[...] = total[:32]
    moe[...] = total[32:33] + total[33:34]
    attn[...] = (total[34:35] + total[35:36]) / gain[...]


def totals(*ins):
    vmem = pl.BlockSpec(memory_space=pltpu.VMEM)
    return pl.pallas_call(
        totals_kernel,
        out_shape=tuple(jax.ShapeDtypeStruct((n, WIDTH), F32) for n in (32, 1, 1)),
        in_specs=[vmem] * 5,
        out_specs=[vmem] * 3,
        compiler_params=pltpu.CompilerParams(vmem_limit_bytes=8 * MIB),
        cost_estimate=pl.CostEstimate(flops=1_000_000, bytes_accessed=1_000_000, transcendentals=0),
        name="totals",
    )(*ins)


def _block_starts(y):
    starts = []
    for r in range(4):
        off = lax.rem(y + r, 4) * ROWS
        if r == 2:
            starts += [off, off + ROWS // 2]
        else:
            starts.append(off)
    return [pl.multiple_of(s, 128) for s in starts]


def attention_forward_kernel(
    y_ref, n0, n1, n2, n3, n4, w_ref, wo_ref, cos_ref, sin_ref,
    qkv_ref, o_ref, lse_ref, p0, p1, p2, p3, p4,
):
    starts = _block_starts(y_ref[0])
    for start, ref in zip(starts, (n0, n1, n2, n3, n4)):
        width = ref.shape[0]
        at = pl.ds(start, width)
        t = mm(w_ref[...], ref[...], NT)
        cos, sin = cos_ref[:, at], sin_ref[:, at]
        for h in range(6):
            a, b = t[64 * h : 64 * h + 32], t[64 * h + 32 : 64 * h + 64]
            ra, rb = a * cos - b * sin, b * cos + a * sin
            if h < 4:
                ra, rb = ra * 0.125, rb * 0.125
            qkv_ref[64 * h : 64 * h + 32, at] = low(ra)
            qkv_ref[64 * h + 32 : 64 * h + 64, at] = low(rb)
        qkv_ref[384:512, at] = low(t[384:])
    key_at = lax.broadcasted_iota(jnp.int32, (ROWS, 2 * ROWS), 0)
    query_at = lax.broadcasted_iota(jnp.int32, (ROWS, 2 * ROWS), 1)
    allowed = key_at <= jnp.bitwise_and(query_at, ROWS - 1)
    for g in range(2):
        keys = qkv_ref[256 + 64 * g : 320 + 64 * g, :].T
        values = qkv_ref[384 + 64 * g : 448 + 64 * g, :]
        for i in range(4):
            here = slice(i * ROWS, (i + 1) * ROWS)
            q2 = jnp.concatenate(
                [qkv_ref[128 * g : 128 * g + 64, here], qkv_ref[128 * g + 64 : 128 * g + 128, here]],
                axis=1,
            )
            tiles = []
            for j in range(i + 1):
                s = mm(keys[j * ROWS : (j + 1) * ROWS], q2)
                if j == i:
                    s = jnp.where(allowed, s, -jnp.inf)
                tiles.append(s)
            peak = tiles[0].max(axis=0, keepdims=True)
            for s in tiles[1:]:
                peak = jnp.maximum(peak, s.max(axis=0, keepdims=True))
            total = jnp.zeros_like(peak)
            mixed = jnp.zeros((HEAD, 2 * ROWS), F32)
            for j, s in enumerate(tiles):
                e = jnp.exp(s - peak)
                total = total + e.sum(axis=0, keepdims=True)
                mixed = mixed + mm(values[:, j * ROWS : (j + 1) * ROWS], low(e))
            mixed = mixed / total
            lse = peak + jnp.log(total)
            o_ref[128 * g : 128 * g + 64, here] = mixed[:, :ROWS]
            o_ref[128 * g + 64 : 128 * g + 128, here] = mixed[:, ROWS:]
            lse_ref[2 * g : 2 * g + 1, here] = lse[:, :ROWS]
            lse_ref[2 * g + 1 : 2 * g + 2, here] = lse[:, ROWS:]
    lse_ref[4:8, :] = jnp.zeros((4, SEQ), F32)
    for start, ref in zip(starts, (p0, p1, p2, p3, p4)):
        att = low(o_ref[:, pl.ds(start, ref.shape[0])])
        ref[...] = low(mm(att.T, wo_ref[...]))


PIECES = (ROWS, ROWS, ROWS // 2, ROWS // 2, ROWS)


def attention_forward(y, blocks, w_t, w_out, cos, sin):
    smem = pl.BlockSpec(memory_space=pltpu.SMEM)
    vmem = pl.BlockSpec(memory_space=pltpu.VMEM)
    return pl.pallas_call(
        attention_forward_kernel,
        out_shape=(
            jax.ShapeDtypeStruct((512, SEQ), BF),
            jax.ShapeDtypeStruct((256, SEQ), F32),
            jax.ShapeDtypeStruct((8, SEQ), F32),
            *[jax.ShapeDtypeStruct((w, WIDTH), BF) for w in PIECES],
        ),
        in_specs=[smem] + [vmem] * 9,
        out_specs=[vmem] * 8,
        compiler_params=pltpu.CompilerParams(vmem_limit_bytes=24 * MIB),
        cost_estimate=pl.CostEstimate(flops=8_000_000_000, bytes_accessed=10_000_000, transcendentals=3_000_000),
        name="attention_forward",
    )(y, *blocks, w_t, w_out, cos, sin)


TILES = tuple((g, i, j) for g in range(2) for i in range(4) for j in range(i + 1))


def probabilities_kernel(qkv_ref, lse_ref, out):
    key_at = lax.broadcasted_iota(jnp.int32, (ROWS, 2 * ROWS), 0)
    query_at = lax.broadcasted_iota(jnp.int32, (ROWS, 2 * ROWS), 1)
    allowed = key_at <= jnp.bitwise_and(query_at, ROWS - 1)
    for g in range(2):
        keys = qkv_ref[256 + 64 * g : 320 + 64 * g, :].T
        for i in range(4):
            here = slice(i * ROWS, (i + 1) * ROWS)
            q2 = jnp.concatenate(
                [qkv_ref[128 * g : 128 * g + 64, here], qkv_ref[128 * g + 64 : 128 * g + 128, here]], axis=1
            )
            lse2 = jnp.concatenate([lse_ref[2 * g : 2 * g + 1, here], lse_ref[2 * g + 1 : 2 * g + 2, here]], axis=1)
            for j in range(i + 1):
                p = jnp.exp(mm(keys[j * ROWS : (j + 1) * ROWS], q2) - lse2)
                out[TILES.index((g, i, j))] = low(jnp.where(allowed, p, 0.0) if j == i else p)


def probabilities(qkv, lse):
    vmem = pl.BlockSpec(memory_space=pltpu.VMEM)
    return pl.pallas_call(
        probabilities_kernel,
        out_shape=jax.ShapeDtypeStruct((len(TILES), ROWS, 2 * ROWS), BF),
        in_specs=[vmem] * 2,
        out_specs=vmem,
        compiler_params=pltpu.CompilerParams(vmem_limit_bytes=16 * MIB),
        cost_estimate=pl.CostEstimate(flops=5_000_000_000, bytes_accessed=7_000_000, transcendentals=3_000_000),
        name="probabilities",
    )(qkv, lse)


def attention_backward_kernel(
    at_ref, d0, d1, d2, d3, d4, x0, x1, x2, x3, x4, qkv_ref, o_ref, prob_any, wo_ref, wa_any, wb_any, cos_ref, sin_ref,
    small_ref, more, keep_ref, send_ref, p0, p1, p2, p3, p4, do_ref, delta_ref, dk_ref, dv_ref, dqkv_ref,
    xs0, xs1, xs2, xs3, xs4, prob_ref, wa_ref, wb_ref, part_ref, in_sem, out_sem, more_sem,
):
    sources = (prob_any, x0, x1, x2, x3, x4, wa_any, wb_any)
    targets = (prob_ref, xs0, xs1, xs2, xs3, xs4, wa_ref, wb_ref)
    loads = [
        pltpu.make_async_copy(source, target, in_sem.at[k]) for k, (source, target) in enumerate(zip(sources, targets))
    ]
    own = pl.ds(0, ROWS)
    stores = [
        pltpu.make_async_copy(part_ref.at[r], target.at[own], out_sem.at[r]) for r, target in enumerate((p0, p1, p2, p4))
    ]
    rest, cut = pl.ds(ROWS, PACK), PIECE // 2 - ROWS
    moves = [
        (more.at[0], p0.at[rest]), (more.at[1], p1.at[rest]), (more.at[3], p4.at[rest]),
        (more.at[2, pl.ds(0, cut)], p2.at[pl.ds(ROWS, cut)]), (more.at[2, pl.ds(cut, PACK - cut)], p3),
    ]
    moves = [pltpu.make_async_copy(source, target, more_sem.at[k]) for k, (source, target) in enumerate(moves)]
    for copy in loads:
        copy.start()
    starts = _block_starts(at_ref[0])
    core = at_ref[1]

    def put(half, first, value):
        rows = slice(first, first + value.shape[0])

        @pl.when(core == half)
        def _():
            keep_ref[rows, :] = value

        @pl.when(core != half)
        def _():
            send_ref[rows, :] = value

    total = jnp.zeros((256, WIDTH), F32)
    for start, ref in zip(starts, (d0, d1, d2, d3, d4)):
        at = pl.ds(start, ref.shape[0])
        do_ref[:, at] = low(mm(wo_ref[...], ref[...], NT))
        total = total + mm(low(o_ref[:, at]), ref[...])
    put(0, 256, low(total[:128]))
    put(1, 256, low(total[128:]))
    put(0, 384, jnp.zeros((64, WIDTH), BF))
    put(1, 384, small_ref[...])
    prod = o_ref[...] * wide(do_ref[...])
    for h in range(4):
        delta_ref[h : h + 1, :] = prod[64 * h : 64 * h + 64].sum(axis=0, keepdims=True)
    loads[0].wait()
    for g in range(2):
        keys_t = qkv_ref[256 + 64 * g : 320 + 64 * g, :]
        values = qkv_ref[384 + 64 * g : 448 + 64 * g, :].T
        dk_ref[...] = jnp.zeros_like(dk_ref)
        dv_ref[...] = jnp.zeros_like(dv_ref)
        base = 256 * g
        for i in range(4):
            here = slice(i * ROWS, (i + 1) * ROWS)

            def pair(ref, base, step):
                return jnp.concatenate(
                    [ref[base : base + step, here], ref[base + step : base + 2 * step, here]], axis=1
                )

            q2 = pair(qkv_ref, 128 * g, 64)
            do2 = pair(do_ref, 128 * g, 64)
            delta2 = pair(delta_ref, 2 * g, 1)
            dq = jnp.zeros((HEAD, 2 * ROWS), F32)
            for j in range(i + 1):
                at = slice(j * ROWS, (j + 1) * ROWS)
                p = prob_ref[TILES.index((g, i, j))]
                ds = low(wide(p) * (mm(values[at], do2) - delta2))
                dq = dq + mm(keys_t[:, at], ds)
                dk_ref[:, at] += mm(q2, ds, NT)
                dv_ref[:, at] += mm(do2, p, NT)
            cos, sin = cos_ref[:, here], sin_ref[:, here]
            dq = dq * 0.125
            for h in range(2):
                a, b = dq[:32, h * ROWS : (h + 1) * ROWS], dq[32:, h * ROWS : (h + 1) * ROWS]
                dqkv_ref[base + 64 * h : base + 64 * h + 32, here] = low(a * cos + b * sin)
                dqkv_ref[base + 64 * h + 32 : base + 64 * h + 64, here] = low(b * cos - a * sin)
        a, b = dk_ref[:32, :], dk_ref[32:, :]
        dqkv_ref[base + 128 : base + 160, :] = low(a * cos_ref[...] + b * sin_ref[...])
        dqkv_ref[base + 160 : base + 192, :] = low(b * cos_ref[...] - a * sin_ref[...])
        dqkv_ref[base + 192 : base + 256, :] = low(dv_ref[...])
        if g == 0:
            for copy in loads[1:6]:
                copy.wait()
        total = jnp.zeros((256, WIDTH), F32)
        for start, ref in zip(starts, (xs0, xs1, xs2, xs3, xs4)):
            total = total + mm(dqkv_ref[base : base + 256, pl.ds(start, ref.shape[0])], ref[...])
        put(g, 0, low(total))
    for copy in loads[6:]:
        copy.wait()
    for copy in moves:
        copy.start()
    for r, copy in enumerate(stores):
        at = pl.ds(pl.multiple_of(lax.rem(at_ref[0] + r, 4) * ROWS, 128), ROWS)
        part_ref[r] = low(mm(dqkv_ref[:256, at].T, wa_ref[...]) + mm(dqkv_ref[256:, at].T, wb_ref[...]))
        copy.start()
    for copy in stores + moves:
        copy.wait()


def attention_backward(at, d_blocks, x_blocks, qkv, o, probs, w_out, wa, wb, cos, sin, small, more):
    smem = pl.BlockSpec(memory_space=pltpu.SMEM)
    vmem = pl.BlockSpec(memory_space=pltpu.VMEM)
    anywhere = pl.BlockSpec(memory_space=pl.ANY)
    return pl.pallas_call(
        attention_backward_kernel,
        out_shape=(
            *[jax.ShapeDtypeStruct((HALF_ROWS, WIDTH), BF)] * 2,
            *[jax.ShapeDtypeStruct((n, WIDTH), BF) for n in (PIECE, PIECE, PIECE // 2, PIECE // 2, PIECE)],
        ),
        in_specs=[smem] + [vmem] * 5 + [anywhere] * 5 + [vmem] * 2 + [anywhere, vmem] + [anywhere] * 2 + [vmem] * 3 + [anywhere],
        out_specs=[vmem] * 2 + [anywhere] * 5,
        scratch_shapes=[
            pltpu.VMEM((256, SEQ), BF),
            pltpu.VMEM((8, SEQ), F32),
            pltpu.VMEM((64, SEQ), F32),
            pltpu.VMEM((64, SEQ), F32),
            pltpu.VMEM((512, SEQ), BF),
            *[pltpu.VMEM((w, WIDTH), BF) for w in PIECES],
            pltpu.VMEM(probs.shape, BF),
            pltpu.VMEM(wa.shape, BF),
            pltpu.VMEM(wb.shape, BF),
            pltpu.VMEM((4, ROWS, WIDTH), BF),
            pltpu.SemaphoreType.DMA((8,)),
            pltpu.SemaphoreType.DMA((4,)),
            pltpu.SemaphoreType.DMA((5,)),
        ],
        compiler_params=pltpu.CompilerParams(vmem_limit_bytes=32 * MIB),
        cost_estimate=pl.CostEstimate(flops=20_000_000_000, bytes_accessed=15_000_000, transcendentals=3_000_000),
        name="attention_backward",
    )(at, *d_blocks, *x_blocks, qkv, o, probs, w_out, wa, wb, cos, sin, small, more)


def finish_kernel(core_ref, half, other, wa_ref, wb_ref, gq, gk, gv, go, rest):
    core = core_ref[0]

    def unpack(first, second):
        lines = jnp.zeros((1, WIDTH), F32)
        for g, (ref, w_ref) in enumerate(((first, wa_ref), (second, wb_ref))):
            grads = wide(ref[:256, :])
            lines = lines + (grads * wide(w_ref[...])).sum(axis=0, keepdims=True)
            gq[:, 128 * g : 128 * g + 128] = grads[:128].T
            turned = grads[128:].T
            gk[:, 64 * g : 64 * g + 64] = turned[:, :64]
            gv[:, 64 * g : 64 * g + 64] = turned[:, 64:]
            go[128 * g : 128 * g + 128, :] = wide(ref[256:384, :])
        rest[:32, :] = second[384:416, :]
        gains = wide(second[416:418, :]).sum(axis=0, keepdims=True)
        high, high2 = low(gains), low(lines)
        rows = [wide(high), gains - wide(high), wide(high2), lines - wide(high2), jnp.zeros((12, WIDTH), F32)]
        rest[32:, :] = low(jnp.concatenate(rows, axis=0))

    @pl.when(core == 0)
    def _():
        unpack(half, other)

    @pl.when(core != 0)
    def _():
        unpack(other, half)


def finish(core, half, other, wa, wb):
    smem = pl.BlockSpec(memory_space=pltpu.SMEM)
    vmem = pl.BlockSpec(memory_space=pltpu.VMEM)
    return pl.pallas_call(
        finish_kernel,
        out_shape=(
            jax.ShapeDtypeStruct((WIDTH, 256), F32),
            jax.ShapeDtypeStruct((WIDTH, 128), F32),
            jax.ShapeDtypeStruct((WIDTH, 128), F32),
            jax.ShapeDtypeStruct((256, WIDTH), F32),
            jax.ShapeDtypeStruct((48, WIDTH), BF),
        ),
        in_specs=[smem] + [vmem] * 4,
        out_specs=[vmem] * 5,
        compiler_params=pltpu.CompilerParams(vmem_limit_bytes=16 * MIB),
        cost_estimate=pl.CostEstimate(flops=3_000_000, bytes_accessed=6_000_000, transcendentals=0),
        name="finish",
    )(core, half, other, wa, wb)


def hidden_gradient_kernel(
    a0, a1, a2, b0, b1, b2, normed, hidden, gain, cot, named, w_ref, expert_ref, d_ref, low_ref, small_ref
):
    in_a = wide(a0[...]) + wide(a1[...]) + wide(a2[...])
    in_b = wide(b0[...]) + wide(b1[...]) + wide(b2[...])
    routed = in_a[ROWS:] + in_b[ROWS:]
    d_route = jnp.concatenate([routed[:, :ROWS], routed[:, ROWS:]], axis=0)
    picked = named[...] > 0.5
    logits = jnp.where(picked, mm(w_ref[...], normed[...], NT), -jnp.inf)
    powers = jnp.where(picked, jnp.exp(logits - logits.max(axis=0, keepdims=True)), 0.0)
    gates = powers / powers.sum(axis=0, keepdims=True)
    d_logits = low(gates * (d_route - (gates * d_route).sum(axis=0, keepdims=True)))
    d_normed = mm(d_logits, w_ref[...], TN) + jnp.concatenate([in_a[:ROWS], in_b[:ROWS]], axis=1)
    x = hidden[...]
    r = norm_scale(x)
    u = d_normed * gain[...]
    d = wide(cot[...]) + r * u - x * (r * r * r * jnp.mean(u * x, axis=1, keepdims=True))
    d_ref[...] = d
    low_ref[...] = low(d)
    small_ref[:32, :] = low(mm(expert_ref[...], low(mm(d_logits, normed[...]))))
    gains = (d_normed * (x * r)).sum(axis=0, keepdims=True)
    high = wide(low(gains))
    small_ref[32:, :] = low(jnp.concatenate([high, gains - high, jnp.zeros((30, WIDTH), F32)], axis=0))


def hidden_gradient(*ins):
    vmem = pl.BlockSpec(memory_space=pltpu.VMEM)
    return pl.pallas_call(
        hidden_gradient_kernel,
        out_shape=(
            jax.ShapeDtypeStruct((ROWS, WIDTH), F32),
            jax.ShapeDtypeStruct((ROWS, WIDTH), BF),
            jax.ShapeDtypeStruct((64, WIDTH), BF),
        ),
        in_specs=[vmem] * 13,
        out_specs=[vmem] * 3,
        compiler_params=pltpu.CompilerParams(vmem_limit_bytes=20 * MIB),
        cost_estimate=pl.CostEstimate(flops=60_000_000, bytes_accessed=6_000_000, transcendentals=10_000),
        name="hidden_gradient",
    )(*ins)


def relay_rows_kernel(plus, minus, first, second, plus_out, minus_out):
    plus_out[...] = add_low(plus[...], first[...])
    minus_out[...] = add_low(minus[...], second[...])


def relay_rows(plus, minus, first, second):
    lower = pl.BlockSpec((PIECE // 2, WIDTH), lambda i: (0, 0))
    upper = pl.BlockSpec((PIECE // 2, WIDTH), lambda i: (1, 0))
    return pl.pallas_call(
        relay_rows_kernel,
        grid=(1,),
        out_shape=(jax.ShapeDtypeStruct((PIECE, WIDTH), BF),) * 2,
        in_specs=[lower, upper, lower, lower],
        out_specs=[lower, upper],
        input_output_aliases={0: 0, 1: 1},
        compiler_params=pltpu.CompilerParams(vmem_limit_bytes=10 * MIB),
        cost_estimate=pl.CostEstimate(flops=300_000, bytes_accessed=1_500_000, transcendentals=0),
        name="relay_rows",
    )(plus, minus, first, second)


SHARD = WIDTH + 512
PACK = 384
PIECE = ROWS + PACK


FAR_STEPS = (((2, 0), (2, 1), (2, 2), (2, 3)), ((0, 2), (1, 2), (3, 2)))
NEAR_STEPS = tuple(tuple((x, z) for z in (0, 1, 3)) for x in (0, 1, 3))
EARLY_STEPS, NEAR_STEPS = NEAR_STEPS[:1], NEAR_STEPS[1:]


def member(pieces, outer, inner):
    if outer == 2:
        return pieces[2 + inner // 2].at[inner % 2]
    return pieces[(0, 1, None, 4)[outer]].at[inner]


def expert_kernel(steps, kept, far, at_ref, *refs):
    ta, tb, (cot_ref, pos_ref, hot_ref, wr_ref), weights, refs = refs[:5], refs[5:10], refs[10:14], refs[14:16], refs[16:]
    refs = refs[kept:]
    stacks, (a0, a1, a4, b0, b1, b4, out_ref), refs = refs[:4], refs[4:11], refs[11:]
    (a2, a3, b2, b3), refs = (refs[:4], refs[4:]) if far else ((None,) * 4, refs)
    da, db = (a0, a1, a2, a3, a4), (b0, b1, b2, b3, b4)
    (tok_scr, cot_scr, wgu_scr, wd_scr, x_scr, dx_scr, act_scr, dgu_scr, g_scr, m_scr, y_scr, p_scr, out_scr), refs = (
        refs[:13], refs[13:],
    )
    w_sem, in_sem, stack_sem, out_sem = refs
    place = wide(lax.broadcasted_iota(jnp.int32, (CAP, ROWS), 0))
    z_of = [lax.rem(at_ref[2] + k, 4) for k in range(4)]
    x_of = [lax.rem(at_ref[3] + k, 4) for k in range(4)]
    chip = at_ref[2] * 4 + at_ref[3]
    first = lax.rem(at_ref[0], 2) == 0
    line = lax.broadcasted_iota(jnp.int32, (16, HALF), 0) == chip
    both = range(2)

    def weight_copies():
        copies = []
        for e, whole in enumerate(weights):
            for r in range(4):
                ref = whole.at[r]
                cols = pl.ds(128 * r, 128)
                moves = [
                    (ref.at[pl.ds(0, WIDTH), pl.ds(0, 128)], wgu_scr.at[e, :, cols]),
                    (ref.at[pl.ds(0, WIDTH), pl.ds(128, 128)], wgu_scr.at[e, :, pl.ds(FF + 128 * r, 128)]),
                ]
                for c in range(4):
                    moves.append((ref.at[pl.ds(WIDTH + 128 * c, 128), :], wd_scr.at[e, cols, pl.ds(256 * c, 256)]))
                for source, target in moves:
                    copies.append(pltpu.make_async_copy(source, target, w_sem.at[len(copies)]))
        return copies

    def in_copies(n):
        copies = []
        for k, (x, z) in enumerate(steps[n]):
            to = tok_scr.at[n % 2, k]
            for source, target in (
                (member(ta, x, z), to.at[:, pl.ds(0, HALF)]),
                (member(tb, z, x), to.at[:, pl.ds(HALF, HALF)]),
                (cot_ref.at[z_of[z], x_of[x], pl.ds(0, ROWS)], cot_scr.at[n % 2, k]),
            ):
                copies.append(pltpu.make_async_copy(source, target, in_sem.at[n % 2, len(copies)]))
        return copies

    def stack_copies(n):
        rows, base = len(steps[n]) * CAP, sum(len(step) for step in steps[:n]) * CAP
        return [
            pltpu.make_async_copy(
                scr.at[n % 2, :, pl.ds(0, rows)], ref.at[:, pl.ds(base, rows)], stack_sem.at[n % 2, i]
            )
            for i, (scr, ref) in enumerate(zip((x_scr, dx_scr, act_scr, dgu_scr), stacks))
        ]

    def out_copies(n):
        copies = []
        for k, (x, z) in enumerate(steps[n]):
            dense = out_scr.at[n % 2, k]
            for source, target in (
                (dense.at[pl.ds(0, EXTRA), pl.ds(0, HALF)], member(da, x, z)),
                (dense.at[pl.ds(0, EXTRA), pl.ds(HALF, HALF)], member(db, z, x)),
                (dense.at[pl.ds(EXTRA, ROWS)], out_ref.at[z_of[z], x_of[x]]),
            ):
                copies.append(pltpu.make_async_copy(source, target, out_sem.at[n % 2, len(copies)]))
        return copies

    for copy in in_copies(0) + weight_copies():
        copy.start()
    for n, step in enumerate(steps):
        slot, count = n % 2, len(step)
        rows = count * CAP
        lane = lax.broadcasted_iota(jnp.int32, (rows, SLOTS), 1)
        for copy in in_copies(n):
            copy.wait()
        if n + 1 < len(steps):
            for copy in in_copies(n + 1):
                copy.start()
        if n >= 2:
            for copy in stack_copies(n - 2) + out_copies(n - 2):
                copy.wait()
        for k, (x, z) in enumerate(step):
            pos = pos_ref[z_of[z], x_of[x]]
            pick = jnp.concatenate([low(wide(place == pos[e : e + 1, :])) for e in both], axis=0)
            p_scr[k] = pick
            xs, gs = low(mm(pick, tok_scr[slot, k])), low(mm(pick, cot_scr[slot, k]))
            ms = mm(pick, hot_ref[z_of[z], x_of[x]], NT)
            for e in both:
                at = slice(k * CAP, (k + 1) * CAP)
                x_scr[slot, e, at, :] = xs[e * CAP : (e + 1) * CAP]
                g_scr[e, at, :] = gs[e * CAP : (e + 1) * CAP]
                m_scr[e, at, :] = ms[e * CAP : (e + 1) * CAP]
        if n == 0:
            for copy in weight_copies():
                copy.wait()
        gu = [mm(x_scr[slot, e, :rows], wgu_scr[e]) for e in both]
        logits = [mm(x_scr[slot, e, :rows], wr_ref[...]) for e in both]
        sig = [jax.nn.sigmoid(gu[e][:, :FF]) for e in both]
        for e in both:
            act_scr[slot, e, :rows] = low(gu[e][:, :FF] * sig[e] * gu[e][:, FF:])
        out = [low(mm(act_scr[slot, e, :rows], wd_scr[e])) for e in both]
        gate = []
        for e in both:
            named = m_scr[e, :rows] > 0.5
            found = jnp.where(named, logits[e], -1e30)
            powers = jnp.where(named, jnp.exp(found - found.max(axis=1, keepdims=True)), 0.0)
            total = powers.sum(axis=1, keepdims=True)
            mine = jnp.where(lane == at_ref[e], powers, 0.0).sum(axis=1, keepdims=True)
            gate.append(mine / jnp.where(total > 0.0, total, 1.0))
            dx_scr[slot, e, :rows] = low(gate[e] * wide(g_scr[e, :rows]))
        d_act = [mm(dx_scr[slot, e, :rows], wd_scr[e], NT) for e in both]
        d_route = []
        for e in both:
            d_route.append((wide(out[e]) * wide(g_scr[e, :rows])).sum(axis=1, keepdims=True))
            y_scr[0, e, :rows] = low(gate[e] * wide(out[e]))
        for e in both:
            pre, up = gu[e][:, :FF], gu[e][:, FF:]
            dgu_scr[slot, e, :rows, :FF] = low(d_act[e] * up * sig[e] * (1.0 + pre * (1.0 - sig[e])))
            dgu_scr[slot, e, :rows, FF:] = low(d_act[e] * (pre * sig[e]))
        for copy in stack_copies(n):
            copy.start()
        for e in both:
            y_scr[1, e, :rows] = low(mm(dgu_scr[slot, e, :rows], wgu_scr[e], NT))
        for k in range(count):
            at = slice(k * CAP, (k + 1) * CAP)
            pick_t = p_scr[k].T
            dense = low(mm(pick_t, jnp.concatenate([y_scr[1, e, at, :] for e in both], axis=0)))
            out_scr[slot, k, :ROWS] = dense
            own, other = [
                (wide(p_scr[k, e * CAP : (e + 1) * CAP, :]) * d_route[e][at]).sum(axis=0, keepdims=True) for e in both
            ]
            pair = jnp.concatenate([jnp.where(first, own, other), jnp.where(first, other, own)], axis=1)
            high = wide(low(pair))
            out_scr[slot, k, ROWS:EXTRA, :HALF] = low(jnp.where(line, high, 0.0))
            out_scr[slot, k, ROWS:EXTRA, HALF:] = low(jnp.where(line, pair - high, 0.0))
            dense = low(mm(pick_t, jnp.concatenate([y_scr[0, e, at, :] for e in both], axis=0)))
            out_scr[slot, k, EXTRA:] = dense
        for copy in out_copies(n):
            copy.start()
    for n in range(max(0, len(steps) - 2), len(steps)):
        for copy in stack_copies(n) + out_copies(n):
            copy.wait()


def experts(steps, at, tok_a, tok_b, cot, pos, hot, w_router, weights, partial=()):
    far = any(2 in member for step in steps for member in step)
    smem = pl.BlockSpec(memory_space=pltpu.SMEM)
    vmem = pl.BlockSpec(memory_space=pltpu.VMEM)
    anywhere = pl.BlockSpec(memory_space=pl.ANY)
    rows, most = sum(len(step) for step in steps) * CAP, max(len(step) for step in steps)
    widths = (WIDTH, WIDTH, FF, 2 * FF)
    ins = (at, *tok_a, *tok_b, cot, pos, hot, w_router, *weights, *partial)
    return pl.pallas_call(
        functools.partial(expert_kernel, steps, len(partial), far),
        out_shape=(
            *[jax.ShapeDtypeStruct((2, rows, width), BF) for width in widths],
            *[jax.ShapeDtypeStruct((4, EXTRA, HALF), BF)] * 6,
            jax.ShapeDtypeStruct((4, 4, ROWS, WIDTH), BF),
            *[jax.ShapeDtypeStruct((2, EXTRA, HALF), BF)] * (4 * far),
        ),
        in_specs=[smem, *[anywhere] * 11, vmem, vmem, vmem, *[anywhere] * (2 + len(partial))],
        out_specs=[anywhere] * (11 + 4 * far),
        scratch_shapes=[
            pltpu.VMEM((2, most, ROWS, WIDTH), BF),
            pltpu.VMEM((2, most, ROWS, WIDTH), BF),
            pltpu.VMEM((2, WIDTH, 2 * FF), BF),
            pltpu.VMEM((2, FF, WIDTH), BF),
            *[pltpu.VMEM((2, 2, most * CAP, width), BF) for width in widths],
            pltpu.VMEM((2, most * CAP, WIDTH), BF),
            pltpu.VMEM((2, most * CAP, SLOTS), F32),
            pltpu.VMEM((2, 2, most * CAP, WIDTH), BF),
            pltpu.VMEM((most, 2 * CAP, ROWS), BF),
            pltpu.VMEM((2, most, EXTRA + ROWS, WIDTH), BF),
            pltpu.SemaphoreType.DMA((48,)),
            pltpu.SemaphoreType.DMA((2, 3 * most)),
            pltpu.SemaphoreType.DMA((2, 4)),
            pltpu.SemaphoreType.DMA((2, 3 * most)),
        ],
        input_output_aliases={17 + k: 4 + k for k in range(len(partial))},
        compiler_params=pltpu.CompilerParams(vmem_limit_bytes=VMEM),
        cost_estimate=pl.CostEstimate(flops=rows * 10_000_000, bytes_accessed=rows * 20_000, transcendentals=rows * 1_000),
        name="experts",
    )(*ins)


def expert_gradient_kernel(y_ref, *refs):
    (x, dx, act, dgu), outs = [
        jnp.concatenate([refs[4 * k + i][0] for k in range(3)], axis=0) for i in range(4)
    ], refs[12:]
    gu = low(mm(x.T, dgu))
    gd = low(mm(act, dx, TN))
    for i, ref in enumerate(outs):

        @pl.when(pl.program_id(0) == i)
        def _(ref=ref):
            for r in range(4):
                to = lax.rem(r - y_ref[0] + 4, 4)
                cols = slice(128 * r, 128 * r + 128)
                ref[to, :128, :] = gd[cols, :]
                for k in range(4):
                    part = slice(256 * k, 256 * k + 256)
                    ref[to, 128:, 256 * k : 256 * k + 128] = gu[part, cols]
                    ref[to, 128:, 256 * k + 128 : 256 * k + 256] = gu[part, FF + 128 * r : FF + 128 * r + 128]


def expert_gradients(y, *sets):
    stacks = [v for one in sets for v in one]
    whole = pl.BlockSpec((4, PACK, WIDTH), lambda i: (0, 0, 0))
    return pl.pallas_call(
        expert_gradient_kernel,
        grid=(2,),
        out_shape=(jax.ShapeDtypeStruct((4, PACK, WIDTH), BF),) * 2,
        in_specs=[
            pl.BlockSpec(memory_space=pltpu.SMEM),
            *[pl.BlockSpec((1, *v.shape[1:]), lambda i: (1 - i, 0, 0)) for v in stacks],
        ],
        out_specs=[whole, whole],
        compiler_params=pltpu.CompilerParams(vmem_limit_bytes=VMEM),
        cost_estimate=pl.CostEstimate(flops=18_000_000_000, bytes_accessed=28_000_000, transcendentals=0),
        name="expert_gradients",
    )(y, *stacks)


def merge_kernel(a_ref, b_ref, out):
    out[...] = add_low(a_ref[...], b_ref[...])


def merge(a, b):
    spec = pl.BlockSpec((1, PACK, WIDTH), lambda i: (i, 0, 0))
    return pl.pallas_call(
        merge_kernel,
        grid=(4,),
        out_shape=jax.ShapeDtypeStruct(a.shape, BF),
        in_specs=[spec] * 2,
        out_specs=spec,
        compiler_params=pltpu.CompilerParams(vmem_limit_bytes=10 * MIB),
        cost_estimate=pl.CostEstimate(flops=2_000_000, bytes_accessed=10_000_000, transcendentals=0),
        name="merge",
    )(a, b)


def token_gradient_kernel(own, plus, minus, tokens, gain, d_hidden, d_tokens, gate, up, down):
    def total(first, last):
        return wide(own[first:last]) + wide(plus[first:last]) + wide(minus[first:last])

    x = wide(tokens[...])
    r = norm_scale(x)
    u = total(0, ROWS) * gain[...]
    d_tokens[...] = d_hidden[...] + r * u - x * (r * r * r * jnp.mean(u * x, axis=1, keepdims=True))
    down[0] = total(ROWS, ROWS + 128)
    packed = total(ROWS + 128, PIECE)
    for k in range(4):
        gate[0, 256 * k : 256 * k + 256, :] = packed[:, 256 * k : 256 * k + 128]
        up[0, 256 * k : 256 * k + 256, :] = packed[:, 256 * k + 128 : 256 * k + 256]


def token_gradient(*ins):
    vmem = pl.BlockSpec(memory_space=pltpu.VMEM)
    return pl.pallas_call(
        token_gradient_kernel,
        out_shape=(
            jax.ShapeDtypeStruct((ROWS, WIDTH), F32),
            jax.ShapeDtypeStruct((1, WIDTH, 128), F32),
            jax.ShapeDtypeStruct((1, WIDTH, 128), F32),
            jax.ShapeDtypeStruct((1, 128, WIDTH), F32),
        ),
        in_specs=[vmem] * 6,
        out_specs=[vmem] * 4,
        compiler_params=pltpu.CompilerParams(vmem_limit_bytes=20 * MIB),
        cost_estimate=pl.CostEstimate(flops=6_000_000, bytes_accessed=9_000_000, transcendentals=0),
        name="token_gradient",
    )(*ins)


def after(value, *others):
    return lax.optimization_barrier((value, *others))[0]


def norm_scale(x):
    return lax.rsqrt(jnp.mean(x * x, axis=-1, keepdims=True) + NORM_EPS)


def shards(
    tokens, cotangent, gain_attn, w_query, w_key, w_value, w_out, gain_moe, w_router,
    w_gate, w_up, w_down, routes, owner_map,
):
    dp = lax.axis_index("dp")
    y = lax.axis_index("tensor").astype(jnp.int32).reshape(1)
    z_at, x_at, core = ring_position(dp)

    x_in = wide(tokens)
    scale_a = norm_scale(x_in)
    normed_a = low(x_in * scale_a * gain_attn)
    x_blocks = (normed_a, *gather_direct(normed_a, from_y))

    slot_ids = jnp.arange(SLOTS, dtype=jnp.int32)
    picks = routes[:, :, None] == slot_ids[None, None, :]
    route_slots = jnp.sum(jnp.where(picks, owner_map[None, None, :], 0), axis=-1)
    hot = low(jnp.any(route_slots.T[:, None, :] == slot_ids[None, :, None], axis=0))
    row_slots = jnp.concatenate([slot_ids[0::2], slot_ids[1::2]])
    named = wide(jnp.any(route_slots.T[:, None, :] == row_slots[None, :, None], axis=0))
    row_experts = low(row_slots[:, None] == owner_map[None, :])
    router_by_row = low(mm(row_experts, w_router, NT))

    sent = jnp.concatenate([cotangent, hot.reshape(8, WIDTH), jnp.zeros((8, WIDTH), BF)], axis=0)
    cot = lax.all_gather(sent, "dp", axis=0, axis_index_groups=PLANE).reshape(4, 4, EXTRA, WIDTH)

    half = HEAD // 2
    inv_freq = jnp.exp(jnp.arange(half).astype(F32) * (-2.0 * math.log(10000.0) / HEAD))
    angles = inv_freq[:, None] * jnp.arange(SEQ).astype(F32)[None, :]
    cos, sin = jnp.cos(angles), jnp.sin(angles)
    w_cat_t = jnp.concatenate([w_query, w_key, w_value], axis=1).T

    qkv, o_t, lse, *parts = attention_forward(y, x_blocks, w_cat_t, w_out, cos, sin)
    hidden = x_in + sum_direct(*parts, from_y)
    normed_m = low(hidden * norm_scale(hidden) * gain_moe)

    down = w_down[0].reshape(128, 4, 256).transpose(1, 0, 2).reshape(512, 256)
    shard = jnp.concatenate([jnp.concatenate([w_gate[0], w_up[0]], axis=1), down], axis=0)
    w_own = lax.all_gather(shard, "tensor", axis=0)
    tok_a, tok_b = plane_gather_first(normed_m)
    row_experts_t = row_experts.T
    tok_a, tok_b, cot, named, router_by_row, row_experts_t = lax.optimization_barrier(
        (tok_a, tok_b, cot, named, router_by_row, row_experts_t)
    )
    hot_all = cot[:, :, ROWS : ROWS + 8].reshape(4, 4, SLOTS, ROWS)
    at = jnp.stack([dp, dp + 1 - 2 * core, z_at, x_at]).astype(jnp.int32)
    mine = jnp.concatenate([lax.dynamic_slice_in_dim(hot_all, at[e], 1, 2) for e in range(2)], axis=2)
    before = low(jnp.arange(ROWS)[:, None] < jnp.arange(ROWS)[None, :])
    rank = jnp.dot(mine.reshape(-1, ROWS), before, preferred_element_type=F32).reshape(mine.shape)
    pos = jnp.where(mine > 0, rank, -1.0)
    by_slot = low(owner_map[:, None] == slot_ids[None, :])
    router_by_slot = low(jnp.dot(w_router, by_slot, preferred_element_type=F32))
    *near, hot_all, at, pos, router_by_slot = lax.optimization_barrier(
        (*plane_gather_second(tok_a, tok_b), hot_all, at, pos, router_by_slot)
    )
    pieces = split(*near)
    far = plane_gather_last(*pieces)
    w_own = after(w_own, *pieces)
    weights = w_own, from_core(w_own)
    table = (cot, pos, hot_all, router_by_slot, weights)
    feeds_early = (at, (tok_a, near[0], *pieces[:2], near[2]), (tok_b, near[1], *pieces[:2], near[3]), *table)
    feeds = (at, (tok_a, near[0], far[0], far[2], near[2]), (tok_b, near[1], far[1], far[3], near[3]), *table)
    early = experts(EARLY_STEPS, *feeds_early)
    outer = experts(FAR_STEPS, *feeds, early[4:])
    a2, a3, b2, b3 = outer[11:]
    far = first_sums((None, None, a2, a3), (None, None, b2, b3))
    near = experts(NEAR_STEPS, *feeds, outer[4:11])
    a0, a1, a4, b0, b1, b4, weighted = near[4:]
    di_a, di_b = (a0, a1, a2, a3, a4), (b0, b1, b2, b3, b4)
    *far, first_stack = lax.optimization_barrier((*far, near[0]))
    relayed = second_sums(di_a, di_b, far)
    other, own = expert_gradients(y, early[:4], outer[:4], (first_stack, *near[1:4]))
    *relayed, other, own = lax.optimization_barrier((*relayed, other, own))
    qa, qb, ra, rb = relayed
    terms = di_a[0], qa, ra, di_b[0], qb, rb
    a2, a3, b2, b3 = fold(1, *terms)
    far = from_z(a2, -1), from_x(b2, -1)
    minus = from_z(a3, 1), from_x(b3, 1)
    a0, a1, b0, b1 = fold(0, *terms)
    both = merge(own, from_core(other))
    *far, both = lax.optimization_barrier((*far, *minus, both))
    far, minus = far[:2], far[2:]
    last = from_z(add_low(a1, far[0]), -1), from_x(add_low(b1, far[1]), -1)
    terms = (a0, minus[0], last[0], b0, minus[1], last[1])
    d_hidden, d_hidden_low, small = hidden_gradient(
        *terms, normed_m, hidden, gain_moe[None], cotangent, named, router_by_row, row_experts_t
    )
    d_blocks = (d_hidden_low, *gather_direct(d_hidden_low, from_y))

    weighted = after(weighted, *last)
    returned = lax.psum_scatter(
        weighted.reshape(16 * ROWS, WIDTH), "dp", scatter_dimension=0, axis_index_groups=PLANE, tiled=True
    )

    wa = jnp.concatenate([w_cat_t[:128], w_cat_t[256:320], w_cat_t[384:448]], axis=0)
    wb = jnp.concatenate([w_cat_t[128:256], w_cat_t[320:384], w_cat_t[448:]], axis=0)
    core_at = core.astype(jnp.int32).reshape(1)
    probs = probabilities(after(qkv, d_hidden_low), lse)
    keep, send, *d_parts = attention_backward(
        jnp.concatenate([y, core_at]), d_blocks, x_blocks, qkv, o_t, probs, w_out, wa, wb, cos, sin, small, both
    )

    x_index = x_at.astype(jnp.int32).reshape(1)
    far = from_y(d_parts[2], -1), from_y(d_parts[3], 1)
    blocks = dp_spread(x_index, keep, from_core(send))
    s = wide(blocks[0]) + wide(from_x(blocks[2], 2)) + wide(from_x(blocks[1], -1)) + wide(from_x(blocks[3], 1))
    *far, s = lax.optimization_barrier((*far, low(s)))
    plus, minus = relay_rows(d_parts[1], d_parts[4], *far)
    plus, minus = from_y(plus, -1), from_y(minus, 1)
    s = plane_exchange(s)
    half_sum, (plus, minus) = dp_collect(x_index, s, (plus, minus))
    half_sum, returned = lax.optimization_barrier((half_sum, returned))
    g_query, g_key, g_value, g_out, rest = finish(core_at, half_sum, from_core(half_sum), wa, wb)
    plus, minus = lax.optimization_barrier((plus, minus, rest))[:2]
    grads = token_gradient(d_parts[0], plus, minus, tokens, gain_attn[None], d_hidden)
    rest = (rest, *[from_y(rest, d) for d in (1, 2, 3)])
    *rest, d_tokens, g_gate, g_up, g_down = lax.optimization_barrier((*rest, *grads))
    g_router, g_gain_moe, g_gain_attn = totals(*rest, gain_attn[None])
    mixed = low(hidden + wide(returned))
    return (
        mixed, d_tokens, g_gain_attn[0], g_query, g_key, g_value, g_out, g_gain_moe[0], g_router.T,
        g_gate, g_up, g_down,
    )


def solution(mesh):
    both = P(("dp", "tensor"), None)
    in_specs = (
        both, both, P(), P(None, "tensor"), P(None, "tensor"), P(None, "tensor"), P("tensor", None), P(), P(),
        P("dp", None, "tensor"), P("dp", None, "tensor"), P("dp", "tensor", None), both, P(),
    )
    out_specs = (
        both, both, P(), P(None, "tensor"), P(None, "tensor"), P(None, "tensor"), P("tensor", None), P(), P(),
        P("dp", None, "tensor"), P("dp", None, "tensor"), P("dp", "tensor", None),
    )
    return jax.shard_map(shards, mesh=mesh, in_specs=in_specs, out_specs=out_specs, check_vma=False)
```

```python
import functools
import math

import jax
import jax.numpy as jnp
from jax import lax
from jax.experimental import pallas as pl
from jax.experimental.pallas import tpu as pltpu
from jax.sharding import PartitionSpec as P

BF = jnp.bfloat16
F32 = jnp.float32
NORM_EPS = 1e-05
HEAD = 64
SEQ = 1024
ROWS = 256
WIDTH = 1024
HALF = 512
FF = 512
SLOTS = 32
CAP = 96
MIB = 1024 * 1024
VMEM = 58 * MIB

NN = (((1,), (0,)), ((), ()))
NT = (((1,), (1,)), ((), ()))
TN = (((0,), (0,)), ((), ()))


def mm(a, b, dims=NN):
    return lax.dot_general(a, b, dims, preferred_element_type=F32)


def _dp_pairs(dz, dx, dc):
    pairs = []
    for z in range(4):
        for x in range(4):
            for c in range(2):
                src = ((z + dz) % 4) * 8 + ((x + dx) % 4) * 2 + (c + dc) % 2
                pairs.append((src, z * 8 + x * 2 + c))
    return pairs


def from_z(v, d):
    return lax.ppermute(v, "dp", _dp_pairs(d, 0, 0))


def from_x(v, d):
    return lax.ppermute(v, "dp", _dp_pairs(0, d, 0))


def from_core(v):
    return lax.ppermute(v, "dp", _dp_pairs(0, 0, 1))


def from_y(v, d):
    return lax.ppermute(v, "tensor", [((i + d) % 4, i) for i in range(4)])


def low(v):
    return v.astype(BF)


def wide(v):
    return v.astype(F32)


PLANE = [[2 * chip + c for chip in range(16)] for c in range(2)]
EXTRA = ROWS + 16
PART = 112
HALF_ROWS = 4 * PART


def gather_direct(own, get, cut=None):
    cut = own.shape[0] // 2 if cut is None else cut
    return get(own, 1), get(own[:cut], 2), get(own[cut:], -2), get(own, -1)


def gather_halves(first, second):
    plus_first, minus_second = from_y(first, 1), from_y(second, -1)
    minus_first, plus_second = from_y(first, -1), from_y(second, 1)
    far = from_y(plus_first, 1), from_y(minus_second, -1)
    return first, second, plus_first, plus_second, *far, minus_first, minus_second


def sum_direct(own, plus, far_low, far_high, minus, get):
    far = jnp.concatenate([get(far_low, 2), get(far_high, -2)], axis=0)
    return wide(own) + wide(get(plus, -1)) + wide(get(minus, 1)) + wide(far)


def plane_gather_first(rows):
    a, b = rows[None, :, :HALF], rows[None, :, HALF:]
    ap, bp, am, bm = from_z(a, 1), from_x(b, 1), from_z(a, -1), from_x(b, -1)
    return jnp.concatenate([a, ap, from_z(ap, 1), am], axis=0), jnp.concatenate([b, bp, from_x(bp, 1), bm], axis=0)


def plane_gather_second(a, b):
    return from_x(a, 1), from_z(b, 1), from_x(a, -1), from_z(b, -1)


def split_kernel(ap, bp, am, bm, *outs):
    for ref, out in zip((ap, bp, am, bm), outs):
        out[...] = ref[...]


def split(a_plus, b_plus, a_minus, b_minus):
    first = pl.BlockSpec((1, ROWS, HALF), lambda i: (i, 0, 0))
    second = pl.BlockSpec((1, ROWS, HALF), lambda i: (2 + i, 0, 0))
    return pl.pallas_call(
        split_kernel,
        grid=(2,),
        out_shape=(jax.ShapeDtypeStruct((2, ROWS, HALF), BF),) * 4,
        in_specs=[first, first, second, second],
        out_specs=[first] * 4,
        compiler_params=pltpu.CompilerParams(vmem_limit_bytes=8 * MIB),
        cost_estimate=pl.CostEstimate(flops=0, bytes_accessed=4_000_000, transcendentals=0),
        name="split",
    )(a_plus, b_plus, a_minus, b_minus)


def plane_gather_last(a_low, b_low, a_high, b_high):
    return from_x(a_low, 1), from_z(b_low, 1), from_x(a_high, -1), from_z(b_high, -1)


def add_low(a, b):
    return low(wide(a) + wide(b))


def relay_kernel(a1, a3, b1, b3, al, ah, bl, bh, a1o, a3o, b1o, b3o):
    for own, got, out in ((a1, al, a1o), (a3, ah, a3o), (b1, bl, b1o), (b3, bh, b3o)):
        out[...] = add_low(own[...], got[...])


def relay(a1, a3, b1, b3, al, ah, bl, bh):
    first = pl.BlockSpec((1, EXTRA, HALF), lambda i: (i, 0, 0))
    second = pl.BlockSpec((1, EXTRA, HALF), lambda i: (2 + i, 0, 0))
    shape = jax.ShapeDtypeStruct(a1.shape, BF)
    return pl.pallas_call(
        relay_kernel,
        grid=(2,),
        out_shape=(shape,) * 4,
        in_specs=[first, second] * 2 + [first] * 4,
        out_specs=[first, second] * 2,
        input_output_aliases={k: k for k in range(4)},
        compiler_params=pltpu.CompilerParams(vmem_limit_bytes=12 * MIB),
        cost_estimate=pl.CostEstimate(flops=2_000_000, bytes_accessed=7_000_000, transcendentals=0),
        name="relay",
    )(a1, a3, b1, b3, al, ah, bl, bh)


def fold_kernel(a0, qa, ra, b0, qb, rb, *outs):
    for own, q, r, to in ((a0, qa, ra, outs[:2]), (b0, qb, rb, outs[2:])):
        for k in range(2):
            to[k][...] = low(wide(own[k]) + wide(q[k]) + wide(r[k]))


def fold(half, *terms):
    spec = pl.BlockSpec((2, EXTRA, HALF), lambda i: (half, 0, 0))
    return pl.pallas_call(
        fold_kernel,
        grid=(1,),
        out_shape=(jax.ShapeDtypeStruct((EXTRA, HALF), BF),) * 4,
        in_specs=[spec] * 6,
        out_specs=[pl.BlockSpec((EXTRA, HALF), lambda i: (0, 0))] * 4,
        compiler_params=pltpu.CompilerParams(vmem_limit_bytes=16 * MIB),
        cost_estimate=pl.CostEstimate(flops=1_500_000, bytes_accessed=4_500_000, transcendentals=0),
        name="fold",
    )(*terms)


def first_sums(a, b):
    return from_x(a[2], -1), from_z(b[2], -1), from_x(a[3], 1), from_z(b[3], 1)


def second_sums(a, b, far):
    al, bl, ah, bh = far
    a1, a3, b1, b3 = relay(a[1], a[4], b[1], b[4], al, ah, bl, bh)
    return from_x(a1, -1), from_z(b1, -1), from_x(a3, 1), from_z(b3, 1)


def ring_position(dp):
    return dp // 8, (dp // 2) % 4, dp % 2


def spread_kernel(x_ref, keep, got, *blocks):
    for r, ref in enumerate(blocks):
        at = pl.ds(pl.multiple_of(lax.rem(x_ref[0] + r, 4) * PART, 16), PART)
        ref[...] = low(wide(keep[at, :]) + wide(got[at, :]))


def collect_kernel(x_ref, *refs):
    for r, ref in enumerate(refs[:4]):
        at = pl.ds(pl.multiple_of(lax.rem(x_ref[0] + r, 4) * PART, 16), PART)
        refs[4][at, :] = ref[...]


def dp_spread(x, keep, got):
    vmem = pl.BlockSpec(memory_space=pltpu.VMEM)
    return pl.pallas_call(
        spread_kernel,
        out_shape=(jax.ShapeDtypeStruct((PART, WIDTH), BF),) * 4,
        in_specs=[pl.BlockSpec(memory_space=pltpu.SMEM), vmem, vmem],
        out_specs=[vmem] * 4,
        compiler_params=pltpu.CompilerParams(vmem_limit_bytes=8 * MIB),
        name="spread",
    )(x, keep, got)


def plane_exchange(s):
    return low(wide(s) + wide(from_z(s, 2)) + wide(from_z(s, 1)) + wide(from_z(s, -1)))


def dp_collect(x, s, others):
    vmem = pl.BlockSpec(memory_space=pltpu.VMEM)
    p, f, m, *others = lax.optimization_barrier((from_x(s, 1), from_x(s, 2), from_x(s, -1), *others))
    return pl.pallas_call(
        collect_kernel,
        out_shape=jax.ShapeDtypeStruct((HALF_ROWS, WIDTH), BF),
        in_specs=[pl.BlockSpec(memory_space=pltpu.SMEM)] + [vmem] * 4,
        out_specs=vmem,
        compiler_params=pltpu.CompilerParams(vmem_limit_bytes=8 * MIB),
        name="collect",
    )(x, s, p, f, m), others


def totals_kernel(a, b, c, d, gain, router, moe, attn):
    total = wide(a[...]) + wide(b[...]) + wide(c[...]) + wide(d[...])
    router[...] = total[:32]
    moe[...] = total[32:33] + total[33:34]
    attn[...] = (total[34:35] + total[35:36]) / gain[...]


def totals(*ins):
    vmem = pl.BlockSpec(memory_space=pltpu.VMEM)
    return pl.pallas_call(
        totals_kernel,
        out_shape=tuple(jax.ShapeDtypeStruct((n, WIDTH), F32) for n in (32, 1, 1)),
        in_specs=[vmem] * 5,
        out_specs=[vmem] * 3,
        compiler_params=pltpu.CompilerParams(vmem_limit_bytes=8 * MIB),
        cost_estimate=pl.CostEstimate(flops=1_000_000, bytes_accessed=1_000_000, transcendentals=0),
        name="totals",
    )(*ins)


def _block_starts(y):
    starts = []
    for r in range(4):
        off = lax.rem(y + r, 4) * ROWS
        if r == 2:
            starts += [off, off + ROWS // 2]
        else:
            starts.append(off)
    return [pl.multiple_of(s, 128) for s in starts]


def whole_blocks(y, halves):
    for r in range(4):
        at = pl.ds(pl.multiple_of(lax.rem(y + r, 4) * ROWS, 128), ROWS)
        yield at, jnp.concatenate([halves[2 * r][...], halves[2 * r + 1][...]], axis=0)


def attention_forward_kernel(
    y_ref, n0, n1, n2, n3, n4, w_ref, wo_ref, cos_ref, sin_ref,
    qkv_ref, o_ref, lse_ref, p0, p1, p2, p3, p4,
):
    starts = _block_starts(y_ref[0])
    for start, ref in zip(starts, (n0, n1, n2, n3, n4)):
        width = ref.shape[0]
        at = pl.ds(start, width)
        t = mm(w_ref[...], ref[...], NT)
        cos, sin = cos_ref[:, at], sin_ref[:, at]
        for h in range(6):
            a, b = t[64 * h : 64 * h + 32], t[64 * h + 32 : 64 * h + 64]
            ra, rb = a * cos - b * sin, b * cos + a * sin
            if h < 4:
                ra, rb = ra * 0.125, rb * 0.125
            qkv_ref[64 * h : 64 * h + 32, at] = low(ra)
            qkv_ref[64 * h + 32 : 64 * h + 64, at] = low(rb)
        qkv_ref[384:512, at] = low(t[384:])
    key_at = lax.broadcasted_iota(jnp.int32, (ROWS, 2 * ROWS), 0)
    query_at = lax.broadcasted_iota(jnp.int32, (ROWS, 2 * ROWS), 1)
    allowed = key_at <= jnp.bitwise_and(query_at, ROWS - 1)
    for g in range(2):
        keys = qkv_ref[256 + 64 * g : 320 + 64 * g, :].T
        values = qkv_ref[384 + 64 * g : 448 + 64 * g, :]
        for i in range(4):
            here = slice(i * ROWS, (i + 1) * ROWS)
            q2 = jnp.concatenate(
                [qkv_ref[128 * g : 128 * g + 64, here], qkv_ref[128 * g + 64 : 128 * g + 128, here]],
                axis=1,
            )
            tiles = []
            for j in range(i + 1):
                s = mm(keys[j * ROWS : (j + 1) * ROWS], q2)
                if j == i:
                    s = jnp.where(allowed, s, -jnp.inf)
                tiles.append(s)
            peak = tiles[0].max(axis=0, keepdims=True)
            for s in tiles[1:]:
                peak = jnp.maximum(peak, s.max(axis=0, keepdims=True))
            total = jnp.zeros_like(peak)
            mixed = jnp.zeros((HEAD, 2 * ROWS), F32)
            for j, s in enumerate(tiles):
                e = jnp.exp(s - peak)
                total = total + e.sum(axis=0, keepdims=True)
                mixed = mixed + mm(values[:, j * ROWS : (j + 1) * ROWS], low(e))
            mixed = mixed / total
            lse = peak + jnp.log(total)
            o_ref[128 * g : 128 * g + 64, here] = mixed[:, :ROWS]
            o_ref[128 * g + 64 : 128 * g + 128, here] = mixed[:, ROWS:]
            lse_ref[2 * g : 2 * g + 1, here] = lse[:, :ROWS]
            lse_ref[2 * g + 1 : 2 * g + 2, here] = lse[:, ROWS:]
    lse_ref[4:8, :] = jnp.zeros((4, SEQ), F32)
    for start, ref in zip(starts, (p0, p1, p2, p3, p4)):
        att = low(o_ref[:, pl.ds(start, ref.shape[0])])
        ref[...] = low(mm(att.T, wo_ref[...]))


PIECES = (ROWS, ROWS, ROWS // 2, ROWS // 2, ROWS)


def attention_forward(y, blocks, w_t, w_out, cos, sin):
    smem = pl.BlockSpec(memory_space=pltpu.SMEM)
    vmem = pl.BlockSpec(memory_space=pltpu.VMEM)
    return pl.pallas_call(
        attention_forward_kernel,
        out_shape=(
            jax.ShapeDtypeStruct((512, SEQ), BF),
            jax.ShapeDtypeStruct((256, SEQ), F32),
            jax.ShapeDtypeStruct((8, SEQ), F32),
            *[jax.ShapeDtypeStruct((w, WIDTH), BF) for w in PIECES],
        ),
        in_specs=[smem] + [vmem] * 9,
        out_specs=[vmem] * 8,
        compiler_params=pltpu.CompilerParams(vmem_limit_bytes=24 * MIB),
        cost_estimate=pl.CostEstimate(flops=8_000_000_000, bytes_accessed=10_000_000, transcendentals=3_000_000),
        name="attention_forward",
    )(y, *blocks, w_t, w_out, cos, sin)


TILES = tuple((g, i, j) for g in range(2) for i in range(4) for j in range(i + 1))


def probabilities_kernel(qkv_ref, lse_ref, out):
    key_at = lax.broadcasted_iota(jnp.int32, (ROWS, 2 * ROWS), 0)
    query_at = lax.broadcasted_iota(jnp.int32, (ROWS, 2 * ROWS), 1)
    allowed = key_at <= jnp.bitwise_and(query_at, ROWS - 1)
    for g in range(2):
        keys = qkv_ref[256 + 64 * g : 320 + 64 * g, :].T
        for i in range(4):
            here = slice(i * ROWS, (i + 1) * ROWS)
            q2 = jnp.concatenate(
                [qkv_ref[128 * g : 128 * g + 64, here], qkv_ref[128 * g + 64 : 128 * g + 128, here]], axis=1
            )
            lse2 = jnp.concatenate([lse_ref[2 * g : 2 * g + 1, here], lse_ref[2 * g + 1 : 2 * g + 2, here]], axis=1)
            for j in range(i + 1):
                p = jnp.exp(mm(keys[j * ROWS : (j + 1) * ROWS], q2) - lse2)
                out[TILES.index((g, i, j))] = low(jnp.where(allowed, p, 0.0) if j == i else p)


def probabilities(qkv, lse):
    vmem = pl.BlockSpec(memory_space=pltpu.VMEM)
    return pl.pallas_call(
        probabilities_kernel,
        out_shape=jax.ShapeDtypeStruct((len(TILES), ROWS, 2 * ROWS), BF),
        in_specs=[vmem] * 2,
        out_specs=vmem,
        compiler_params=pltpu.CompilerParams(vmem_limit_bytes=16 * MIB),
        cost_estimate=pl.CostEstimate(flops=5_000_000_000, bytes_accessed=7_000_000, transcendentals=3_000_000),
        name="probabilities",
    )(qkv, lse)


def attention_backward_kernel(
    at_ref, d0, d1, d2, d3, d4, d5, d6, d7, x0, x1, x2, x3, x4, qkv_ref, o_ref, prob_any, wo_ref, wa_any, wb_any, cos_ref, sin_ref,
    small_ref, more, keep_ref, send_ref, p0, p1, p2, p3, p4, do_ref, delta_ref, dk_ref, dv_ref, dqkv_ref,
    x_ref, prob_ref, wa_ref, wb_ref, part_ref, in_sem, out_sem, more_sem,
):
    sources = (prob_any, x0, x1, x2, x3, x4, wa_any, wb_any)
    x_parts = [x_ref.at[2, pl.ds(half * (ROWS // 2), ROWS // 2)] for half in range(2)]
    targets = (prob_ref, x_ref.at[0], x_ref.at[1], *x_parts, x_ref.at[3], wa_ref, wb_ref)
    loads = [
        pltpu.make_async_copy(source, target, in_sem.at[k]) for k, (source, target) in enumerate(zip(sources, targets))
    ]
    own = pl.ds(0, ROWS)
    stores = [
        pltpu.make_async_copy(part_ref.at[r], target.at[own], out_sem.at[r]) for r, target in enumerate((p0, p1, p2, p4))
    ]
    rest, cut = pl.ds(ROWS, PACK), PIECE // 2 - ROWS
    moves = [
        (more.at[0], p0.at[rest]), (more.at[1], p1.at[rest]), (more.at[3], p4.at[rest]),
        (more.at[2, pl.ds(0, cut)], p2.at[pl.ds(ROWS, cut)]), (more.at[2, pl.ds(cut, PACK - cut)], p3),
    ]
    moves = [pltpu.make_async_copy(source, target, more_sem.at[k]) for k, (source, target) in enumerate(moves)]
    for copy in loads:
        copy.start()
    core = at_ref[1]

    def put(half, first, value):
        rows = slice(first, first + value.shape[0])

        @pl.when(core == half)
        def _():
            keep_ref[rows, :] = value

        @pl.when(core != half)
        def _():
            send_ref[rows, :] = value

    total = jnp.zeros((256, WIDTH), F32)
    for at, d in whole_blocks(at_ref[0], (d0, d1, d2, d3, d4, d5, d6, d7)):
        do_ref[:, at] = low(mm(wo_ref[...], d, NT))
        total = total + mm(low(o_ref[:, at]), d)
    put(0, 256, low(total[:128]))
    put(1, 256, low(total[128:]))
    put(0, 384, jnp.zeros((64, WIDTH), BF))
    put(1, 384, small_ref[...])
    prod = o_ref[...] * wide(do_ref[...])
    for h in range(4):
        delta_ref[h : h + 1, :] = prod[64 * h : 64 * h + 64].sum(axis=0, keepdims=True)
    loads[0].wait()
    for g in range(2):
        keys_t = qkv_ref[256 + 64 * g : 320 + 64 * g, :]
        values = qkv_ref[384 + 64 * g : 448 + 64 * g, :].T
        dk_ref[...] = jnp.zeros_like(dk_ref)
        dv_ref[...] = jnp.zeros_like(dv_ref)
        base = 256 * g
        for i in range(4):
            here = slice(i * ROWS, (i + 1) * ROWS)

            def pair(ref, base, step):
                return jnp.concatenate(
                    [ref[base : base + step, here], ref[base + step : base + 2 * step, here]], axis=1
                )

            q2 = pair(qkv_ref, 128 * g, 64)
            do2 = pair(do_ref, 128 * g, 64)
            delta2 = pair(delta_ref, 2 * g, 1)
            dq = jnp.zeros((HEAD, 2 * ROWS), F32)
            for j in range(i + 1):
                at = slice(j * ROWS, (j + 1) * ROWS)
                p = prob_ref[TILES.index((g, i, j))]
                ds = low(wide(p) * (mm(values[at], do2) - delta2))
                dq = dq + mm(keys_t[:, at], ds)
                dk_ref[:, at] += mm(q2, ds, NT)
                dv_ref[:, at] += mm(do2, p, NT)
            cos, sin = cos_ref[:, here], sin_ref[:, here]
            dq = dq * 0.125
            for h in range(2):
                a, b = dq[:32, h * ROWS : (h + 1) * ROWS], dq[32:, h * ROWS : (h + 1) * ROWS]
                dqkv_ref[base + 64 * h : base + 64 * h + 32, here] = low(a * cos + b * sin)
                dqkv_ref[base + 64 * h + 32 : base + 64 * h + 64, here] = low(b * cos - a * sin)
        a, b = dk_ref[:32, :], dk_ref[32:, :]
        dqkv_ref[base + 128 : base + 160, :] = low(a * cos_ref[...] + b * sin_ref[...])
        dqkv_ref[base + 160 : base + 192, :] = low(b * cos_ref[...] - a * sin_ref[...])
        dqkv_ref[base + 192 : base + 256, :] = low(dv_ref[...])
        if g == 0:
            for copy in loads[1:6]:
                copy.wait()
        total = jnp.zeros((256, WIDTH), F32)
        for r in range(4):
            at = pl.ds(pl.multiple_of(lax.rem(at_ref[0] + r, 4) * ROWS, 128), ROWS)
            total = total + mm(dqkv_ref[base : base + 256, at], x_ref[r])
        put(g, 0, low(total))
    for copy in loads[6:]:
        copy.wait()
    for copy in moves:
        copy.start()
    for r, copy in enumerate(stores):
        at = pl.ds(pl.multiple_of(lax.rem(at_ref[0] + r, 4) * ROWS, 128), ROWS)
        part_ref[r] = low(mm(dqkv_ref[:256, at].T, wa_ref[...]) + mm(dqkv_ref[256:, at].T, wb_ref[...]))
        copy.start()
    for copy in stores + moves:
        copy.wait()


def attention_backward(at, d_blocks, x_blocks, qkv, o, probs, w_out, wa, wb, cos, sin, small, more):
    smem = pl.BlockSpec(memory_space=pltpu.SMEM)
    vmem = pl.BlockSpec(memory_space=pltpu.VMEM)
    anywhere = pl.BlockSpec(memory_space=pl.ANY)
    return pl.pallas_call(
        attention_backward_kernel,
        out_shape=(
            *[jax.ShapeDtypeStruct((HALF_ROWS, WIDTH), BF)] * 2,
            *[jax.ShapeDtypeStruct((n, WIDTH), BF) for n in (PIECE, PIECE, PIECE // 2, PIECE // 2, PIECE)],
        ),
        in_specs=[smem] + [vmem] * 8 + [anywhere] * 5 + [vmem] * 2 + [anywhere, vmem] + [anywhere] * 2 + [vmem] * 3 + [anywhere],
        out_specs=[vmem] * 2 + [anywhere] * 5,
        scratch_shapes=[
            pltpu.VMEM((256, SEQ), BF),
            pltpu.VMEM((8, SEQ), F32),
            pltpu.VMEM((64, SEQ), F32),
            pltpu.VMEM((64, SEQ), F32),
            pltpu.VMEM((512, SEQ), BF),
            pltpu.VMEM((4, ROWS, WIDTH), BF),
            pltpu.VMEM(probs.shape, BF),
            pltpu.VMEM(wa.shape, BF),
            pltpu.VMEM(wb.shape, BF),
            pltpu.VMEM((4, ROWS, WIDTH), BF),
            pltpu.SemaphoreType.DMA((8,)),
            pltpu.SemaphoreType.DMA((4,)),
            pltpu.SemaphoreType.DMA((5,)),
        ],
        compiler_params=pltpu.CompilerParams(vmem_limit_bytes=32 * MIB),
        cost_estimate=pl.CostEstimate(flops=20_000_000_000, bytes_accessed=15_000_000, transcendentals=3_000_000),
        name="attention_backward",
    )(at, *d_blocks, *x_blocks, qkv, o, probs, w_out, wa, wb, cos, sin, small, more)


def finish_kernel(core_ref, half, other, wa_ref, wb_ref, gq, gk, gv, go, rest):
    core = core_ref[0]

    def unpack(first, second):
        lines = jnp.zeros((1, WIDTH), F32)
        for g, (ref, w_ref) in enumerate(((first, wa_ref), (second, wb_ref))):
            grads = wide(ref[:256, :])
            lines = lines + (grads * wide(w_ref[...])).sum(axis=0, keepdims=True)
            gq[:, 128 * g : 128 * g + 128] = grads[:128].T
            turned = grads[128:].T
            gk[:, 64 * g : 64 * g + 64] = turned[:, :64]
            gv[:, 64 * g : 64 * g + 64] = turned[:, 64:]
            go[128 * g : 128 * g + 128, :] = wide(ref[256:384, :])
        rest[:32, :] = second[384:416, :]
        gains = wide(second[416:418, :]).sum(axis=0, keepdims=True)
        high, high2 = low(gains), low(lines)
        rows = [wide(high), gains - wide(high), wide(high2), lines - wide(high2), jnp.zeros((12, WIDTH), F32)]
        rest[32:, :] = low(jnp.concatenate(rows, axis=0))

    @pl.when(core == 0)
    def _():
        unpack(half, other)

    @pl.when(core != 0)
    def _():
        unpack(other, half)


def finish(core, half, other, wa, wb):
    smem = pl.BlockSpec(memory_space=pltpu.SMEM)
    vmem = pl.BlockSpec(memory_space=pltpu.VMEM)
    return pl.pallas_call(
        finish_kernel,
        out_shape=(
            jax.ShapeDtypeStruct((WIDTH, 256), F32),
            jax.ShapeDtypeStruct((WIDTH, 128), F32),
            jax.ShapeDtypeStruct((WIDTH, 128), F32),
            jax.ShapeDtypeStruct((256, WIDTH), F32),
            jax.ShapeDtypeStruct((48, WIDTH), BF),
        ),
        in_specs=[smem] + [vmem] * 4,
        out_specs=[vmem] * 5,
        compiler_params=pltpu.CompilerParams(vmem_limit_bytes=16 * MIB),
        cost_estimate=pl.CostEstimate(flops=3_000_000, bytes_accessed=6_000_000, transcendentals=0),
        name="finish",
    )(core, half, other, wa, wb)


def hidden_gradient_kernel(*refs):
    sources, (gain, named, w_ref, expert_ref, d_ref, first_ref, second_ref, small_ref), refs = refs[:9], refs[9:17], refs[17:]
    a0, a1, a2, b0, b1, b2, normed, hidden, cot = refs[:9]
    loads = [
        pltpu.make_async_copy(source, target, refs[9].at[k]) for k, (source, target) in enumerate(zip(sources, refs[:9]))
    ]
    for copy in loads:
        copy.start()
    for copy in loads:
        copy.wait()
    in_a = wide(a0[...]) + wide(a1[...]) + wide(a2[...])
    in_b = wide(b0[...]) + wide(b1[...]) + wide(b2[...])
    routed = in_a[ROWS:] + in_b[ROWS:]
    d_route = jnp.concatenate([routed[:, :ROWS], routed[:, ROWS:]], axis=0)
    picked = named[...] > 0.5
    logits = jnp.where(picked, mm(w_ref[...], normed[...], NT), -jnp.inf)
    powers = jnp.where(picked, jnp.exp(logits - logits.max(axis=0, keepdims=True)), 0.0)
    gates = powers / powers.sum(axis=0, keepdims=True)
    d_logits = low(gates * (d_route - (gates * d_route).sum(axis=0, keepdims=True)))
    d_normed = mm(d_logits, w_ref[...], TN) + jnp.concatenate([in_a[:ROWS], in_b[:ROWS]], axis=1)
    x = hidden[...]
    r = norm_scale(x)
    u = d_normed * gain[...]
    d = wide(cot[...]) + r * u - x * (r * r * r * jnp.mean(u * x, axis=1, keepdims=True))
    d_ref[...] = d
    first_ref[...] = low(d[: ROWS // 2])
    second_ref[...] = low(d[ROWS // 2 :])
    small_ref[:32, :] = low(mm(expert_ref[...], low(mm(d_logits, normed[...]))))
    gains = (d_normed * (x * r)).sum(axis=0, keepdims=True)
    high = wide(low(gains))
    small_ref[32:, :] = low(jnp.concatenate([high, gains - high, jnp.zeros((30, WIDTH), F32)], axis=0))


def hidden_gradient(*ins):
    vmem = pl.BlockSpec(memory_space=pltpu.VMEM)
    shapes = ((ROWS, WIDTH), (ROWS // 2, WIDTH), (ROWS // 2, WIDTH), (64, WIDTH))
    return pl.pallas_call(
        hidden_gradient_kernel,
        out_shape=tuple(jax.ShapeDtypeStruct(shape, F32 if k == 0 else BF) for k, shape in enumerate(shapes)),
        in_specs=[pl.BlockSpec(memory_space=pl.ANY)] * 9 + [vmem] * 4,
        out_specs=[vmem] * 4,
        scratch_shapes=[*[pltpu.VMEM(v.shape, v.dtype) for v in ins[:9]], pltpu.SemaphoreType.DMA((9,))],
        compiler_params=pltpu.CompilerParams(vmem_limit_bytes=20 * MIB),
        cost_estimate=pl.CostEstimate(flops=60_000_000, bytes_accessed=6_000_000, transcendentals=10_000),
        name="hidden_gradient",
    )(*ins)


def relay_rows_kernel(plus, minus, first, second, plus_out, minus_out):
    plus_out[...] = add_low(plus[...], first[...])
    minus_out[...] = add_low(minus[...], second[...])


def relay_rows(plus, minus, first, second):
    lower = pl.BlockSpec((PIECE // 2, WIDTH), lambda i: (0, 0))
    upper = pl.BlockSpec((PIECE // 2, WIDTH), lambda i: (1, 0))
    return pl.pallas_call(
        relay_rows_kernel,
        grid=(1,),
        out_shape=(jax.ShapeDtypeStruct((PIECE, WIDTH), BF),) * 2,
        in_specs=[lower, upper, lower, lower],
        out_specs=[lower, upper],
        input_output_aliases={0: 0, 1: 1},
        compiler_params=pltpu.CompilerParams(vmem_limit_bytes=10 * MIB),
        cost_estimate=pl.CostEstimate(flops=300_000, bytes_accessed=1_500_000, transcendentals=0),
        name="relay_rows",
    )(plus, minus, first, second)


SHARD = WIDTH + 512
PACK = 384
PIECE = ROWS + PACK


FAR_STEPS = (((2, 0), (2, 1), (2, 2), (2, 3)), ((0, 2), (1, 2), (3, 2)))
NEAR_STEPS = tuple(tuple((x, z) for z in (0, 1, 3)) for x in (0, 1, 3))
EARLY_STEPS, NEAR_STEPS = NEAR_STEPS[:1], NEAR_STEPS[1:]


def member(pieces, outer, inner):
    if outer == 2:
        return pieces[2 + inner // 2].at[inner % 2]
    return pieces[(0, 1, None, 4)[outer]].at[inner]


def expert_kernel(steps, kept, far, at_ref, *refs):
    ta, tb, (cot_ref, pos_ref, hot_ref, wr_ref), weights, refs = refs[:5], refs[5:10], refs[10:14], refs[14:16], refs[16:]
    refs = refs[kept:]
    stacks, (a0, a1, a4, b0, b1, b4, out_ref), refs = refs[:4], refs[4:11], refs[11:]
    (a2, a3, b2, b3), refs = (refs[:4], refs[4:]) if far else ((None,) * 4, refs)
    da, db = (a0, a1, a2, a3, a4), (b0, b1, b2, b3, b4)
    (tok_scr, cot_scr, wgu_scr, wd_scr, x_scr, dx_scr, act_scr, dgu_scr, g_scr, m_scr, y_scr, p_scr, out_scr), refs = (
        refs[:13], refs[13:],
    )
    w_sem, in_sem, stack_sem, out_sem = refs
    place = wide(lax.broadcasted_iota(jnp.int32, (CAP, ROWS), 0))
    z_of = [lax.rem(at_ref[2] + k, 4) for k in range(4)]
    x_of = [lax.rem(at_ref[3] + k, 4) for k in range(4)]
    chip = at_ref[2] * 4 + at_ref[3]
    first = lax.rem(at_ref[0], 2) == 0
    line = lax.broadcasted_iota(jnp.int32, (16, HALF), 0) == chip
    both = range(2)

    def weight_copies():
        copies = []
        for e, whole in enumerate(weights):
            for r in range(4):
                ref = whole.at[r]
                cols = pl.ds(128 * r, 128)
                moves = [
                    (ref.at[pl.ds(0, WIDTH), pl.ds(0, 128)], wgu_scr.at[e, :, cols]),
                    (ref.at[pl.ds(0, WIDTH), pl.ds(128, 128)], wgu_scr.at[e, :, pl.ds(FF + 128 * r, 128)]),
                ]
                for c in range(4):
                    moves.append((ref.at[pl.ds(WIDTH + 128 * c, 128), :], wd_scr.at[e, cols, pl.ds(256 * c, 256)]))
                for source, target in moves:
                    copies.append(pltpu.make_async_copy(source, target, w_sem.at[len(copies)]))
        return copies

    def in_copies(n):
        copies = []
        for k, (x, z) in enumerate(steps[n]):
            to = tok_scr.at[n % 2, k]
            for source, target in (
                (member(ta, x, z), to.at[:, pl.ds(0, HALF)]),
                (member(tb, z, x), to.at[:, pl.ds(HALF, HALF)]),
                (cot_ref.at[z_of[z], x_of[x], pl.ds(0, ROWS)], cot_scr.at[n % 2, k]),
            ):
                copies.append(pltpu.make_async_copy(source, target, in_sem.at[n % 2, len(copies)]))
        return copies

    def stack_copies(n):
        rows, base = len(steps[n]) * CAP, sum(len(step) for step in steps[:n]) * CAP
        return [
            pltpu.make_async_copy(
                scr.at[n % 2, :, pl.ds(0, rows)], ref.at[:, pl.ds(base, rows)], stack_sem.at[n % 2, i]
            )
            for i, (scr, ref) in enumerate(zip((x_scr, dx_scr, act_scr, dgu_scr), stacks))
        ]

    def out_copies(n):
        copies = []
        for k, (x, z) in enumerate(steps[n]):
            dense = out_scr.at[n % 2, k]
            for source, target in (
                (dense.at[pl.ds(0, EXTRA), pl.ds(0, HALF)], member(da, x, z)),
                (dense.at[pl.ds(0, EXTRA), pl.ds(HALF, HALF)], member(db, z, x)),
                (dense.at[pl.ds(EXTRA, ROWS)], out_ref.at[z_of[z], x_of[x]]),
            ):
                copies.append(pltpu.make_async_copy(source, target, out_sem.at[n % 2, len(copies)]))
        return copies

    for copy in in_copies(0) + weight_copies():
        copy.start()
    for n, step in enumerate(steps):
        slot, count = n % 2, len(step)
        rows = count * CAP
        lane = lax.broadcasted_iota(jnp.int32, (rows, SLOTS), 1)
        for copy in in_copies(n):
            copy.wait()
        if n + 1 < len(steps):
            for copy in in_copies(n + 1):
                copy.start()
        if n >= 2:
            for copy in stack_copies(n - 2) + out_copies(n - 2):
                copy.wait()
        for k, (x, z) in enumerate(step):
            pos = pos_ref[z_of[z], x_of[x]]
            pick = jnp.concatenate([low(wide(place == pos[e : e + 1, :])) for e in both], axis=0)
            p_scr[k] = pick
            xs, gs = low(mm(pick, tok_scr[slot, k])), low(mm(pick, cot_scr[slot, k]))
            ms = mm(pick, hot_ref[z_of[z], x_of[x]], NT)
            for e in both:
                at = slice(k * CAP, (k + 1) * CAP)
                x_scr[slot, e, at, :] = xs[e * CAP : (e + 1) * CAP]
                g_scr[e, at, :] = gs[e * CAP : (e + 1) * CAP]
                m_scr[e, at, :] = ms[e * CAP : (e + 1) * CAP]
        if n == 0:
            for copy in weight_copies():
                copy.wait()
        gu = [mm(x_scr[slot, e, :rows], wgu_scr[e]) for e in both]
        logits = [mm(x_scr[slot, e, :rows], wr_ref[...]) for e in both]
        sig = [jax.nn.sigmoid(gu[e][:, :FF]) for e in both]
        for e in both:
            act_scr[slot, e, :rows] = low(gu[e][:, :FF] * sig[e] * gu[e][:, FF:])
        out = [low(mm(act_scr[slot, e, :rows], wd_scr[e])) for e in both]
        gate = []
        for e in both:
            named = m_scr[e, :rows] > 0.5
            found = jnp.where(named, logits[e], -1e30)
            powers = jnp.where(named, jnp.exp(found - found.max(axis=1, keepdims=True)), 0.0)
            total = powers.sum(axis=1, keepdims=True)
            mine = jnp.where(lane == at_ref[e], powers, 0.0).sum(axis=1, keepdims=True)
            gate.append(mine / jnp.where(total > 0.0, total, 1.0))
            dx_scr[slot, e, :rows] = low(gate[e] * wide(g_scr[e, :rows]))
        d_act = [mm(dx_scr[slot, e, :rows], wd_scr[e], NT) for e in both]
        d_route = []
        for e in both:
            d_route.append((wide(out[e]) * wide(g_scr[e, :rows])).sum(axis=1, keepdims=True))
            y_scr[0, e, :rows] = low(gate[e] * wide(out[e]))
        for e in both:
            pre, up = gu[e][:, :FF], gu[e][:, FF:]
            dgu_scr[slot, e, :rows, :FF] = low(d_act[e] * up * sig[e] * (1.0 + pre * (1.0 - sig[e])))
            dgu_scr[slot, e, :rows, FF:] = low(d_act[e] * (pre * sig[e]))
        for copy in stack_copies(n):
            copy.start()
        for e in both:
            y_scr[1, e, :rows] = low(mm(dgu_scr[slot, e, :rows], wgu_scr[e], NT))
        for k in range(count):
            at = slice(k * CAP, (k + 1) * CAP)
            pick_t = p_scr[k].T
            dense = low(mm(pick_t, jnp.concatenate([y_scr[1, e, at, :] for e in both], axis=0)))
            out_scr[slot, k, :ROWS] = dense
            own, other = [
                (wide(p_scr[k, e * CAP : (e + 1) * CAP, :]) * d_route[e][at]).sum(axis=0, keepdims=True) for e in both
            ]
            pair = jnp.concatenate([jnp.where(first, own, other), jnp.where(first, other, own)], axis=1)
            high = wide(low(pair))
            out_scr[slot, k, ROWS:EXTRA, :HALF] = low(jnp.where(line, high, 0.0))
            out_scr[slot, k, ROWS:EXTRA, HALF:] = low(jnp.where(line, pair - high, 0.0))
            dense = low(mm(pick_t, jnp.concatenate([y_scr[0, e, at, :] for e in both], axis=0)))
            out_scr[slot, k, EXTRA:] = dense
        for copy in out_copies(n):
            copy.start()
    for n in range(max(0, len(steps) - 2), len(steps)):
        for copy in stack_copies(n) + out_copies(n):
            copy.wait()


def experts(steps, at, tok_a, tok_b, cot, pos, hot, w_router, weights, partial=()):
    far = any(2 in member for step in steps for member in step)
    smem = pl.BlockSpec(memory_space=pltpu.SMEM)
    vmem = pl.BlockSpec(memory_space=pltpu.VMEM)
    anywhere = pl.BlockSpec(memory_space=pl.ANY)
    rows, most = sum(len(step) for step in steps) * CAP, max(len(step) for step in steps)
    widths = (WIDTH, WIDTH, FF, 2 * FF)
    ins = (at, *tok_a, *tok_b, cot, pos, hot, w_router, *weights, *partial)
    return pl.pallas_call(
        functools.partial(expert_kernel, steps, len(partial), far),
        out_shape=(
            *[jax.ShapeDtypeStruct((2, rows, width), BF) for width in widths],
            *[jax.ShapeDtypeStruct((4, EXTRA, HALF), BF)] * 6,
            jax.ShapeDtypeStruct((4, 4, ROWS, WIDTH), BF),
            *[jax.ShapeDtypeStruct((2, EXTRA, HALF), BF)] * (4 * far),
        ),
        in_specs=[smem, *[anywhere] * 11, vmem, vmem, vmem, *[anywhere] * (2 + len(partial))],
        out_specs=[anywhere] * (11 + 4 * far),
        scratch_shapes=[
            pltpu.VMEM((2, most, ROWS, WIDTH), BF),
            pltpu.VMEM((2, most, ROWS, WIDTH), BF),
            pltpu.VMEM((2, WIDTH, 2 * FF), BF),
            pltpu.VMEM((2, FF, WIDTH), BF),
            *[pltpu.VMEM((2, 2, most * CAP, width), BF) for width in widths],
            pltpu.VMEM((2, most * CAP, WIDTH), BF),
            pltpu.VMEM((2, most * CAP, SLOTS), F32),
            pltpu.VMEM((2, 2, most * CAP, WIDTH), BF),
            pltpu.VMEM((most, 2 * CAP, ROWS), BF),
            pltpu.VMEM((2, most, EXTRA + ROWS, WIDTH), BF),
            pltpu.SemaphoreType.DMA((48,)),
            pltpu.SemaphoreType.DMA((2, 3 * most)),
            pltpu.SemaphoreType.DMA((2, 4)),
            pltpu.SemaphoreType.DMA((2, 3 * most)),
        ],
        input_output_aliases={17 + k: 4 + k for k in range(len(partial))},
        compiler_params=pltpu.CompilerParams(vmem_limit_bytes=VMEM),
        cost_estimate=pl.CostEstimate(flops=rows * 10_000_000, bytes_accessed=rows * 20_000, transcendentals=rows * 1_000),
        name="experts",
    )(*ins)


def expert_gradient_kernel(y_ref, *refs):
    (x, dx, act, dgu), outs = [
        jnp.concatenate([refs[4 * k + i][0] for k in range(3)], axis=0) for i in range(4)
    ], refs[12:]
    gu = low(mm(x.T, dgu))
    gd = low(mm(act, dx, TN))
    for i, ref in enumerate(outs):

        @pl.when(pl.program_id(0) == i)
        def _(ref=ref):
            for r in range(4):
                to = lax.rem(r - y_ref[0] + 4, 4)
                cols = slice(128 * r, 128 * r + 128)
                ref[to, :128, :] = gd[cols, :]
                for k in range(4):
                    part = slice(256 * k, 256 * k + 256)
                    ref[to, 128:, 256 * k : 256 * k + 128] = gu[part, cols]
                    ref[to, 128:, 256 * k + 128 : 256 * k + 256] = gu[part, FF + 128 * r : FF + 128 * r + 128]


def expert_gradients(y, *sets):
    stacks = [v for one in sets for v in one]
    whole = pl.BlockSpec((4, PACK, WIDTH), lambda i: (0, 0, 0))
    return pl.pallas_call(
        expert_gradient_kernel,
        grid=(2,),
        out_shape=(jax.ShapeDtypeStruct((4, PACK, WIDTH), BF),) * 2,
        in_specs=[
            pl.BlockSpec(memory_space=pltpu.SMEM),
            *[pl.BlockSpec((1, *v.shape[1:]), lambda i: (1 - i, 0, 0)) for v in stacks],
        ],
        out_specs=[whole, whole],
        compiler_params=pltpu.CompilerParams(vmem_limit_bytes=VMEM),
        cost_estimate=pl.CostEstimate(flops=18_000_000_000, bytes_accessed=28_000_000, transcendentals=0),
        name="expert_gradients",
    )(y, *stacks)


def merge_kernel(a_ref, b_ref, out):
    out[...] = add_low(a_ref[...], b_ref[...])


def merge(a, b):
    spec = pl.BlockSpec((1, PACK, WIDTH), lambda i: (i, 0, 0))
    return pl.pallas_call(
        merge_kernel,
        grid=(4,),
        out_shape=jax.ShapeDtypeStruct(a.shape, BF),
        in_specs=[spec] * 2,
        out_specs=spec,
        compiler_params=pltpu.CompilerParams(vmem_limit_bytes=10 * MIB),
        cost_estimate=pl.CostEstimate(flops=2_000_000, bytes_accessed=10_000_000, transcendentals=0),
        name="merge",
    )(a, b)


def token_gradient_kernel(own, plus, minus, tokens, gain, d_hidden, d_tokens, gate, up, down):
    def total(first, last):
        return wide(own[first:last]) + wide(plus[first:last]) + wide(minus[first:last])

    x = wide(tokens[...])
    r = norm_scale(x)
    u = total(0, ROWS) * gain[...]
    d_tokens[...] = d_hidden[...] + r * u - x * (r * r * r * jnp.mean(u * x, axis=1, keepdims=True))
    down[0] = total(ROWS, ROWS + 128)
    packed = total(ROWS + 128, PIECE)
    for k in range(4):
        gate[0, 256 * k : 256 * k + 256, :] = packed[:, 256 * k : 256 * k + 128]
        up[0, 256 * k : 256 * k + 256, :] = packed[:, 256 * k + 128 : 256 * k + 256]


def token_gradient(*ins):
    vmem = pl.BlockSpec(memory_space=pltpu.VMEM)
    return pl.pallas_call(
        token_gradient_kernel,
        out_shape=(
            jax.ShapeDtypeStruct((ROWS, WIDTH), F32),
            jax.ShapeDtypeStruct((1, WIDTH, 128), F32),
            jax.ShapeDtypeStruct((1, WIDTH, 128), F32),
            jax.ShapeDtypeStruct((1, 128, WIDTH), F32),
        ),
        in_specs=[vmem] * 6,
        out_specs=[vmem] * 4,
        compiler_params=pltpu.CompilerParams(vmem_limit_bytes=20 * MIB),
        cost_estimate=pl.CostEstimate(flops=6_000_000, bytes_accessed=9_000_000, transcendentals=0),
        name="token_gradient",
    )(*ins)


def after(value, *others):
    return lax.optimization_barrier((value, *others))[0]


def norm_scale(x):
    return lax.rsqrt(jnp.mean(x * x, axis=-1, keepdims=True) + NORM_EPS)


def shards(
    tokens, cotangent, gain_attn, w_query, w_key, w_value, w_out, gain_moe, w_router,
    w_gate, w_up, w_down, routes, owner_map,
):
    dp = lax.axis_index("dp")
    y = lax.axis_index("tensor").astype(jnp.int32).reshape(1)
    z_at, x_at, core = ring_position(dp)

    x_in = wide(tokens)
    scale_a = norm_scale(x_in)
    normed_a = low(x_in * scale_a * gain_attn)
    x_blocks = (normed_a, *gather_direct(normed_a, from_y))

    slot_ids = jnp.arange(SLOTS, dtype=jnp.int32)
    picks = routes[:, :, None] == slot_ids[None, None, :]
    route_slots = jnp.sum(jnp.where(picks, owner_map[None, None, :], 0), axis=-1)
    hot = low(jnp.any(route_slots.T[:, None, :] == slot_ids[None, :, None], axis=0))
    row_slots = jnp.concatenate([slot_ids[0::2], slot_ids[1::2]])
    named = wide(jnp.any(route_slots.T[:, None, :] == row_slots[None, :, None], axis=0))
    row_experts = low(row_slots[:, None] == owner_map[None, :])
    router_by_row = low(mm(row_experts, w_router, NT))

    sent = jnp.concatenate([cotangent, hot.reshape(8, WIDTH), jnp.zeros((8, WIDTH), BF)], axis=0)
    cot = lax.all_gather(sent, "dp", axis=0, axis_index_groups=PLANE).reshape(4, 4, EXTRA, WIDTH)

    half = HEAD // 2
    inv_freq = jnp.exp(jnp.arange(half).astype(F32) * (-2.0 * math.log(10000.0) / HEAD))
    angles = inv_freq[:, None] * jnp.arange(SEQ).astype(F32)[None, :]
    cos, sin = jnp.cos(angles), jnp.sin(angles)
    w_cat_t = jnp.concatenate([w_query, w_key, w_value], axis=1).T

    qkv, o_t, lse, *parts = attention_forward(y, x_blocks, w_cat_t, w_out, cos, sin)
    hidden = x_in + sum_direct(*parts, from_y)
    normed_m = low(hidden * norm_scale(hidden) * gain_moe)

    down = w_down[0].reshape(128, 4, 256).transpose(1, 0, 2).reshape(512, 256)
    shard = jnp.concatenate([jnp.concatenate([w_gate[0], w_up[0]], axis=1), down], axis=0)
    w_own = lax.all_gather(shard, "tensor", axis=0)
    tok_a, tok_b = plane_gather_first(normed_m)
    wa = jnp.concatenate([w_cat_t[:128], w_cat_t[256:320], w_cat_t[384:448]], axis=0)
    wb = jnp.concatenate([w_cat_t[128:256], w_cat_t[320:384], w_cat_t[448:]], axis=0)
    row_experts_t = row_experts.T
    tok_a, tok_b, cot, named, router_by_row, row_experts_t, wa, wb = lax.optimization_barrier(
        (tok_a, tok_b, cot, named, router_by_row, row_experts_t, wa, wb)
    )
    hot_all = cot[:, :, ROWS : ROWS + 8].reshape(4, 4, SLOTS, ROWS)
    at = jnp.stack([dp, dp + 1 - 2 * core, z_at, x_at]).astype(jnp.int32)
    mine = jnp.concatenate([lax.dynamic_slice_in_dim(hot_all, at[e], 1, 2) for e in range(2)], axis=2)
    before = low(jnp.arange(ROWS)[:, None] < jnp.arange(ROWS)[None, :])
    rank = jnp.dot(mine.reshape(-1, ROWS), before, preferred_element_type=F32).reshape(mine.shape)
    pos = jnp.where(mine > 0, rank, -1.0)
    by_slot = low(owner_map[:, None] == slot_ids[None, :])
    router_by_slot = low(jnp.dot(w_router, by_slot, preferred_element_type=F32))
    *near, hot_all, at, pos, router_by_slot = lax.optimization_barrier(
        (*plane_gather_second(tok_a, tok_b), hot_all, at, pos, router_by_slot)
    )
    pieces = split(*near)
    far = plane_gather_last(*pieces)
    w_own = after(w_own, *pieces)
    weights = w_own, from_core(w_own)
    table = (cot, pos, hot_all, router_by_slot, weights)
    feeds_early = (at, (tok_a, near[0], *pieces[:2], near[2]), (tok_b, near[1], *pieces[:2], near[3]), *table)
    feeds = (at, (tok_a, near[0], far[0], far[2], near[2]), (tok_b, near[1], far[1], far[3], near[3]), *table)
    early = experts(EARLY_STEPS, *feeds_early)
    outer = experts(FAR_STEPS, *feeds, early[4:])
    a2, a3, b2, b3 = outer[11:]
    far = first_sums((None, None, a2, a3), (None, None, b2, b3))
    near = experts(NEAR_STEPS, *feeds, outer[4:11])
    a0, a1, a4, b0, b1, b4, weighted = near[4:]
    di_a, di_b = (a0, a1, a2, a3, a4), (b0, b1, b2, b3, b4)
    *far, first_stack = lax.optimization_barrier((*far, near[0]))
    relayed = second_sums(di_a, di_b, far)
    other, own = expert_gradients(y, early[:4], outer[:4], (first_stack, *near[1:4]))
    *relayed, other, own = lax.optimization_barrier((*relayed, other, own))
    qa, qb, ra, rb = relayed
    terms = di_a[0], qa, ra, di_b[0], qb, rb
    a2, a3, b2, b3 = fold(1, *terms)
    far = from_z(a2, -1), from_x(b2, -1)
    minus = from_z(a3, 1), from_x(b3, 1)
    a0, a1, b0, b1 = fold(0, *terms)
    both = merge(own, from_core(other))
    *far, both = lax.optimization_barrier((*far, *minus, both))
    far, minus = far[:2], far[2:]
    last = from_z(add_low(a1, far[0]), -1), from_x(add_low(b1, far[1]), -1)
    terms = (a0, minus[0], last[0], b0, minus[1], last[1])
    d_hidden, d_first, d_second, small = hidden_gradient(
        *terms, normed_m, hidden, cotangent, gain_moe[None], named, router_by_row, row_experts_t
    )
    d_blocks = gather_halves(d_first, d_second)

    weighted = after(weighted, *last)
    returned = lax.psum_scatter(
        weighted.reshape(16 * ROWS, WIDTH), "dp", scatter_dimension=0, axis_index_groups=PLANE, tiled=True
    )

    core_at = core.astype(jnp.int32).reshape(1)
    probs = probabilities(after(qkv, d_first), lse)
    keep, send, *d_parts = attention_backward(
        jnp.concatenate([y, core_at]), d_blocks, x_blocks, qkv, o_t, probs, w_out, wa, wb, cos, sin, small, both
    )

    x_index = x_at.astype(jnp.int32).reshape(1)
    far = from_y(d_parts[2], -1), from_y(d_parts[3], 1)
    blocks = dp_spread(x_index, keep, from_core(send))
    s = wide(blocks[0]) + wide(from_x(blocks[2], 2)) + wide(from_x(blocks[1], -1)) + wide(from_x(blocks[3], 1))
    *far, s = lax.optimization_barrier((*far, low(s)))
    plus, minus = relay_rows(d_parts[1], d_parts[4], *far)
    plus, minus = from_y(plus, -1), from_y(minus, 1)
    s = plane_exchange(s)
    half_sum, (plus, minus) = dp_collect(x_index, s, (plus, minus))
    half_sum, returned = lax.optimization_barrier((half_sum, returned))
    g_query, g_key, g_value, g_out, rest = finish(core_at, half_sum, from_core(half_sum), wa, wb)
    plus, minus = lax.optimization_barrier((plus, minus, rest))[:2]
    grads = token_gradient(d_parts[0], plus, minus, tokens, gain_attn[None], d_hidden)
    rest = (rest, *[from_y(rest, d) for d in (1, 2, 3)])
    *rest, d_tokens, g_gate, g_up, g_down = lax.optimization_barrier((*rest, *grads))
    g_router, g_gain_moe, g_gain_attn = totals(*rest, gain_attn[None])
    mixed = low(hidden + wide(returned))
    return (
        mixed, d_tokens, g_gain_attn[0], g_query, g_key, g_value, g_out, g_gain_moe[0], g_router.T,
        g_gate, g_up, g_down,
    )


def solution(mesh):
    both = P(("dp", "tensor"), None)
    in_specs = (
        both, both, P(), P(None, "tensor"), P(None, "tensor"), P(None, "tensor"), P("tensor", None), P(), P(),
        P("dp", None, "tensor"), P("dp", None, "tensor"), P("dp", "tensor", None), both, P(),
    )
    out_specs = (
        both, both, P(), P(None, "tensor"), P(None, "tensor"), P(None, "tensor"), P("tensor", None), P(), P(),
        P("dp", None, "tensor"), P("dp", None, "tensor"), P("dp", "tensor", None),
    )
    return jax.shard_map(shards, mesh=mesh, in_specs=in_specs, out_specs=out_specs, check_vma=False)
```

```python
import functools
import math

import jax
import jax.numpy as jnp
from jax import lax
from jax.experimental import pallas as pl
from jax.experimental.pallas import tpu as pltpu
from jax.sharding import PartitionSpec as P

BF = jnp.bfloat16
F32 = jnp.float32
NORM_EPS = 1e-05
HEAD = 64
SEQ = 1024
ROWS = 256
WIDTH = 1024
HALF = 512
FF = 512
SLOTS = 32
CAP = 96
MIB = 1024 * 1024
VMEM = 58 * MIB

NN = (((1,), (0,)), ((), ()))
NT = (((1,), (1,)), ((), ()))
TN = (((0,), (0,)), ((), ()))


def mm(a, b, dims=NN):
    return lax.dot_general(a, b, dims, preferred_element_type=F32)


def _dp_pairs(dz, dx, dc):
    pairs = []
    for z in range(4):
        for x in range(4):
            for c in range(2):
                src = ((z + dz) % 4) * 8 + ((x + dx) % 4) * 2 + (c + dc) % 2
                pairs.append((src, z * 8 + x * 2 + c))
    return pairs


def from_z(v, d):
    return lax.ppermute(v, "dp", _dp_pairs(d, 0, 0))


def from_x(v, d):
    return lax.ppermute(v, "dp", _dp_pairs(0, d, 0))


def from_core(v):
    return lax.ppermute(v, "dp", _dp_pairs(0, 0, 1))


def from_y(v, d):
    return lax.ppermute(v, "tensor", [((i + d) % 4, i) for i in range(4)])


def low(v):
    return v.astype(BF)


def wide(v):
    return v.astype(F32)


PLANE = [[2 * chip + c for chip in range(16)] for c in range(2)]
EXTRA = ROWS + 16
PART = 112
HALF_ROWS = 4 * PART


def gather_direct(own, get, cut=None):
    cut = own.shape[0] // 2 if cut is None else cut
    return get(own, 1), get(own[:cut], 2), get(own[cut:], -2), get(own, -1)


def gather_halves(first, second):
    plus_first, minus_second = from_y(first, 1), from_y(second, -1)
    minus_first, plus_second = from_y(first, -1), from_y(second, 1)
    far = from_y(plus_first, 1), from_y(minus_second, -1)
    return first, second, plus_first, plus_second, *far, minus_first, minus_second


def sum_direct(own, plus, far_low, far_high, minus, get):
    far = jnp.concatenate([get(far_low, 2), get(far_high, -2)], axis=0)
    return wide(own) + wide(get(plus, -1)) + wide(get(minus, 1)) + wide(far)


def plane_gather_first(rows):
    a, b = rows[None, :, :HALF], rows[None, :, HALF:]
    ap, bp, am, bm = from_z(a, 1), from_x(b, 1), from_z(a, -1), from_x(b, -1)
    return jnp.concatenate([a, ap, from_z(ap, 1), am], axis=0), jnp.concatenate([b, bp, from_x(bp, 1), bm], axis=0)


def plane_gather_second(a, b):
    return from_x(a, 1), from_z(b, 1), from_x(a, -1), from_z(b, -1)


def split_kernel(ap, bp, am, bm, *outs):
    for ref, out in zip((ap, bp, am, bm), outs):
        out[...] = ref[...]


def split(a_plus, b_plus, a_minus, b_minus):
    first = pl.BlockSpec((1, ROWS, HALF), lambda i: (i, 0, 0))
    second = pl.BlockSpec((1, ROWS, HALF), lambda i: (2 + i, 0, 0))
    return pl.pallas_call(
        split_kernel,
        grid=(2,),
        out_shape=(jax.ShapeDtypeStruct((2, ROWS, HALF), BF),) * 4,
        in_specs=[first, first, second, second],
        out_specs=[first] * 4,
        compiler_params=pltpu.CompilerParams(vmem_limit_bytes=8 * MIB),
        cost_estimate=pl.CostEstimate(flops=0, bytes_accessed=4_000_000, transcendentals=0),
        name="split",
    )(a_plus, b_plus, a_minus, b_minus)


def plane_gather_last(a_low, b_low, a_high, b_high):
    return from_x(a_low, 1), from_z(b_low, 1), from_x(a_high, -1), from_z(b_high, -1)


def add_low(a, b):
    return low(wide(a) + wide(b))


def relay_kernel(a1, a3, b1, b3, al, ah, bl, bh, a1o, a3o, b1o, b3o):
    for own, got, out in ((a1, al, a1o), (a3, ah, a3o), (b1, bl, b1o), (b3, bh, b3o)):
        out[...] = add_low(own[...], got[...])


def relay(a1, a3, b1, b3, al, ah, bl, bh):
    first = pl.BlockSpec((1, EXTRA, HALF), lambda i: (i, 0, 0))
    second = pl.BlockSpec((1, EXTRA, HALF), lambda i: (2 + i, 0, 0))
    shape = jax.ShapeDtypeStruct(a1.shape, BF)
    return pl.pallas_call(
        relay_kernel,
        grid=(2,),
        out_shape=(shape,) * 4,
        in_specs=[first, second] * 2 + [first] * 4,
        out_specs=[first, second] * 2,
        input_output_aliases={k: k for k in range(4)},
        compiler_params=pltpu.CompilerParams(vmem_limit_bytes=12 * MIB),
        cost_estimate=pl.CostEstimate(flops=2_000_000, bytes_accessed=7_000_000, transcendentals=0),
        name="relay",
    )(a1, a3, b1, b3, al, ah, bl, bh)


def fold_kernel(a0, qa, ra, b0, qb, rb, *outs):
    for own, q, r, to in ((a0, qa, ra, outs[:2]), (b0, qb, rb, outs[2:])):
        for k in range(2):
            to[k][...] = low(wide(own[k]) + wide(q[k]) + wide(r[k]))


def fold(half, *terms):
    spec = pl.BlockSpec((2, EXTRA, HALF), lambda i: (half, 0, 0))
    return pl.pallas_call(
        fold_kernel,
        grid=(1,),
        out_shape=(jax.ShapeDtypeStruct((EXTRA, HALF), BF),) * 4,
        in_specs=[spec] * 6,
        out_specs=[pl.BlockSpec((EXTRA, HALF), lambda i: (0, 0))] * 4,
        compiler_params=pltpu.CompilerParams(vmem_limit_bytes=16 * MIB),
        cost_estimate=pl.CostEstimate(flops=1_500_000, bytes_accessed=4_500_000, transcendentals=0),
        name="fold",
    )(*terms)


def first_sums(a, b):
    return from_x(a[2], -1), from_z(b[2], -1), from_x(a[3], 1), from_z(b[3], 1)


def second_sums(a, b, far):
    al, bl, ah, bh = far
    a1, a3, b1, b3 = relay(a[1], a[4], b[1], b[4], al, ah, bl, bh)
    return from_x(a1, -1), from_z(b1, -1), from_x(a3, 1), from_z(b3, 1)


def ring_position(dp):
    return dp // 8, (dp // 2) % 4, dp % 2


def spread_kernel(x_ref, keep, got, *blocks):
    for r, ref in enumerate(blocks):
        at = pl.ds(pl.multiple_of(lax.rem(x_ref[0] + r, 4) * PART, 16), PART)
        ref[...] = low(wide(keep[at, :]) + wide(got[at, :]))


def collect_kernel(x_ref, *refs):
    for r, ref in enumerate(refs[:4]):
        at = pl.ds(pl.multiple_of(lax.rem(x_ref[0] + r, 4) * PART, 16), PART)
        refs[4][at, :] = ref[...]


def dp_spread(x, keep, got):
    vmem = pl.BlockSpec(memory_space=pltpu.VMEM)
    return pl.pallas_call(
        spread_kernel,
        out_shape=(jax.ShapeDtypeStruct((PART, WIDTH), BF),) * 4,
        in_specs=[pl.BlockSpec(memory_space=pltpu.SMEM), vmem, vmem],
        out_specs=[vmem] * 4,
        compiler_params=pltpu.CompilerParams(vmem_limit_bytes=8 * MIB),
        name="spread",
    )(x, keep, got)


def plane_exchange(s):
    return low(wide(s) + wide(from_z(s, 2)) + wide(from_z(s, 1)) + wide(from_z(s, -1)))


def dp_collect(x, s, others):
    vmem = pl.BlockSpec(memory_space=pltpu.VMEM)
    p, f, m, *others = lax.optimization_barrier((from_x(s, 1), from_x(s, 2), from_x(s, -1), *others))
    return pl.pallas_call(
        collect_kernel,
        out_shape=jax.ShapeDtypeStruct((HALF_ROWS, WIDTH), BF),
        in_specs=[pl.BlockSpec(memory_space=pltpu.SMEM)] + [vmem] * 4,
        out_specs=vmem,
        compiler_params=pltpu.CompilerParams(vmem_limit_bytes=8 * MIB),
        name="collect",
    )(x, s, p, f, m), others


def totals_kernel(a, b, c, d, gain, router, moe, attn):
    total = wide(a[...]) + wide(b[...]) + wide(c[...]) + wide(d[...])
    router[...] = total[:32]
    moe[...] = total[32:33] + total[33:34]
    attn[...] = (total[34:35] + total[35:36]) / gain[...]


def totals(*ins):
    vmem = pl.BlockSpec(memory_space=pltpu.VMEM)
    return pl.pallas_call(
        totals_kernel,
        out_shape=tuple(jax.ShapeDtypeStruct((n, WIDTH), F32) for n in (32, 1, 1)),
        in_specs=[vmem] * 5,
        out_specs=[vmem] * 3,
        compiler_params=pltpu.CompilerParams(vmem_limit_bytes=8 * MIB),
        cost_estimate=pl.CostEstimate(flops=1_000_000, bytes_accessed=1_000_000, transcendentals=0),
        name="totals",
    )(*ins)


def _block_starts(y):
    starts = []
    for r in range(4):
        off = lax.rem(y + r, 4) * ROWS
        if r == 2:
            starts += [off, off + ROWS // 2]
        else:
            starts.append(off)
    return [pl.multiple_of(s, 128) for s in starts]


def whole_blocks(y, halves):
    for r in range(4):
        at = pl.ds(pl.multiple_of(lax.rem(y + r, 4) * ROWS, 128), ROWS)
        yield at, jnp.concatenate([halves[2 * r][...], halves[2 * r + 1][...]], axis=0)


def attention_forward_kernel(
    y_ref, n0, n1, n2, n3, n4, w_ref, wo_ref, cos_ref, sin_ref,
    qkv_ref, o_ref, lse_ref, p0, p1, p2, p3, p4,
):
    starts = _block_starts(y_ref[0])
    for start, ref in zip(starts, (n0, n1, n2, n3, n4)):
        width = ref.shape[0]
        at = pl.ds(start, width)
        t = mm(w_ref[...], ref[...], NT)
        cos, sin = cos_ref[:, at], sin_ref[:, at]
        for h in range(6):
            a, b = t[64 * h : 64 * h + 32], t[64 * h + 32 : 64 * h + 64]
            ra, rb = a * cos - b * sin, b * cos + a * sin
            if h < 4:
                ra, rb = ra * 0.125, rb * 0.125
            qkv_ref[64 * h : 64 * h + 32, at] = low(ra)
            qkv_ref[64 * h + 32 : 64 * h + 64, at] = low(rb)
        qkv_ref[384:512, at] = low(t[384:])
    key_at = lax.broadcasted_iota(jnp.int32, (ROWS, 2 * ROWS), 0)
    query_at = lax.broadcasted_iota(jnp.int32, (ROWS, 2 * ROWS), 1)
    allowed = key_at <= jnp.bitwise_and(query_at, ROWS - 1)
    for g in range(2):
        keys = qkv_ref[256 + 64 * g : 320 + 64 * g, :].T
        values = qkv_ref[384 + 64 * g : 448 + 64 * g, :]
        for i in range(4):
            here = slice(i * ROWS, (i + 1) * ROWS)
            q2 = jnp.concatenate(
                [qkv_ref[128 * g : 128 * g + 64, here], qkv_ref[128 * g + 64 : 128 * g + 128, here]],
                axis=1,
            )
            tiles = []
            for j in range(i + 1):
                s = mm(keys[j * ROWS : (j + 1) * ROWS], q2)
                if j == i:
                    s = jnp.where(allowed, s, -jnp.inf)
                tiles.append(s)
            peak = tiles[0].max(axis=0, keepdims=True)
            for s in tiles[1:]:
                peak = jnp.maximum(peak, s.max(axis=0, keepdims=True))
            total = jnp.zeros_like(peak)
            mixed = jnp.zeros((HEAD, 2 * ROWS), F32)
            for j, s in enumerate(tiles):
                e = jnp.exp(s - peak)
                total = total + e.sum(axis=0, keepdims=True)
                mixed = mixed + mm(values[:, j * ROWS : (j + 1) * ROWS], low(e))
            mixed = mixed / total
            lse = peak + jnp.log(total)
            o_ref[128 * g : 128 * g + 64, here] = mixed[:, :ROWS]
            o_ref[128 * g + 64 : 128 * g + 128, here] = mixed[:, ROWS:]
            lse_ref[2 * g : 2 * g + 1, here] = lse[:, :ROWS]
            lse_ref[2 * g + 1 : 2 * g + 2, here] = lse[:, ROWS:]
    lse_ref[4:8, :] = jnp.zeros((4, SEQ), F32)
    for start, ref in zip(starts, (p0, p1, p2, p3, p4)):
        att = low(o_ref[:, pl.ds(start, ref.shape[0])])
        ref[...] = low(mm(att.T, wo_ref[...]))


PIECES = (ROWS, ROWS, ROWS // 2, ROWS // 2, ROWS)


def attention_forward(y, blocks, w_t, w_out, cos, sin):
    smem = pl.BlockSpec(memory_space=pltpu.SMEM)
    vmem = pl.BlockSpec(memory_space=pltpu.VMEM)
    return pl.pallas_call(
        attention_forward_kernel,
        out_shape=(
            jax.ShapeDtypeStruct((512, SEQ), BF),
            jax.ShapeDtypeStruct((256, SEQ), F32),
            jax.ShapeDtypeStruct((8, SEQ), F32),
            *[jax.ShapeDtypeStruct((w, WIDTH), BF) for w in PIECES],
        ),
        in_specs=[smem] + [vmem] * 9,
        out_specs=[vmem] * 8,
        compiler_params=pltpu.CompilerParams(vmem_limit_bytes=24 * MIB),
        cost_estimate=pl.CostEstimate(flops=8_000_000_000, bytes_accessed=10_000_000, transcendentals=3_000_000),
        name="attention_forward",
    )(y, *blocks, w_t, w_out, cos, sin)


TILES = tuple((g, i, j) for g in range(2) for i in range(4) for j in range(i + 1))


def probabilities_kernel(qkv_ref, lse_ref, out):
    key_at = lax.broadcasted_iota(jnp.int32, (ROWS, 2 * ROWS), 0)
    query_at = lax.broadcasted_iota(jnp.int32, (ROWS, 2 * ROWS), 1)
    allowed = key_at <= jnp.bitwise_and(query_at, ROWS - 1)
    for g in range(2):
        keys = qkv_ref[256 + 64 * g : 320 + 64 * g, :].T
        for i in range(4):
            here = slice(i * ROWS, (i + 1) * ROWS)
            q2 = jnp.concatenate(
                [qkv_ref[128 * g : 128 * g + 64, here], qkv_ref[128 * g + 64 : 128 * g + 128, here]], axis=1
            )
            lse2 = jnp.concatenate([lse_ref[2 * g : 2 * g + 1, here], lse_ref[2 * g + 1 : 2 * g + 2, here]], axis=1)
            for j in range(i + 1):
                p = jnp.exp(mm(keys[j * ROWS : (j + 1) * ROWS], q2) - lse2)
                out[TILES.index((g, i, j))] = low(jnp.where(allowed, p, 0.0) if j == i else p)


def probabilities(qkv, lse):
    vmem = pl.BlockSpec(memory_space=pltpu.VMEM)
    return pl.pallas_call(
        probabilities_kernel,
        out_shape=jax.ShapeDtypeStruct((len(TILES), ROWS, 2 * ROWS), BF),
        in_specs=[vmem] * 2,
        out_specs=vmem,
        compiler_params=pltpu.CompilerParams(vmem_limit_bytes=16 * MIB),
        cost_estimate=pl.CostEstimate(flops=5_000_000_000, bytes_accessed=7_000_000, transcendentals=3_000_000),
        name="probabilities",
    )(qkv, lse)


def attention_backward_kernel(
    at_ref, d0, d1, d2, d3, d4, d5, d6, d7, x0, x1, x2, x3, x4, qkv_ref, o_ref, prob_any, wo_ref, wa_any, wb_any, cos_ref, sin_ref,
    small_ref, more, keep_ref, send_ref, p0, p1, p2, p3, p4, do_ref, delta_ref, dk_ref, dv_ref, dqkv_ref,
    x_ref, prob_ref, wa_ref, wb_ref, part_ref, in_sem, out_sem, more_sem,
):
    sources = (prob_any, x0, x1, x2, x3, x4, wa_any, wb_any)
    x_parts = [x_ref.at[2, pl.ds(half * (ROWS // 2), ROWS // 2)] for half in range(2)]
    targets = (prob_ref, x_ref.at[0], x_ref.at[1], *x_parts, x_ref.at[3], wa_ref, wb_ref)
    loads = [
        pltpu.make_async_copy(source, target, in_sem.at[k]) for k, (source, target) in enumerate(zip(sources, targets))
    ]
    own = pl.ds(0, ROWS)
    stores = [
        pltpu.make_async_copy(part_ref.at[r], target.at[own], out_sem.at[r]) for r, target in enumerate((p0, p1, p2, p4))
    ]
    rest, cut = pl.ds(ROWS, PACK), PIECE // 2 - ROWS
    moves = [
        (more.at[0], p0.at[rest]), (more.at[1], p1.at[rest]), (more.at[3], p4.at[rest]),
        (more.at[2, pl.ds(0, cut)], p2.at[pl.ds(ROWS, cut)]), (more.at[2, pl.ds(cut, PACK - cut)], p3),
    ]
    moves = [pltpu.make_async_copy(source, target, more_sem.at[k]) for k, (source, target) in enumerate(moves)]
    for copy in loads:
        copy.start()
    core = at_ref[1]

    def put(half, first, value):
        rows = slice(first, first + value.shape[0])

        @pl.when(core == half)
        def _():
            keep_ref[rows, :] = value

        @pl.when(core != half)
        def _():
            send_ref[rows, :] = value

    total = jnp.zeros((256, WIDTH), F32)
    for at, d in whole_blocks(at_ref[0], (d0, d1, d2, d3, d4, d5, d6, d7)):
        do_ref[:, at] = low(mm(wo_ref[...], d, NT))
        total = total + mm(low(o_ref[:, at]), d)
    put(0, 256, low(total[:128]))
    put(1, 256, low(total[128:]))
    put(0, 384, jnp.zeros((64, WIDTH), BF))
    put(1, 384, small_ref[...])
    prod = o_ref[...] * wide(do_ref[...])
    for h in range(4):
        delta_ref[h : h + 1, :] = prod[64 * h : 64 * h + 64].sum(axis=0, keepdims=True)
    loads[0].wait()
    for g in range(2):
        keys_t = qkv_ref[256 + 64 * g : 320 + 64 * g, :]
        values = qkv_ref[384 + 64 * g : 448 + 64 * g, :].T
        dk_ref[...] = jnp.zeros_like(dk_ref)
        dv_ref[...] = jnp.zeros_like(dv_ref)
        base = 256 * g
        for i in range(4):
            here = slice(i * ROWS, (i + 1) * ROWS)

            def pair(ref, base, step):
                return jnp.concatenate(
                    [ref[base : base + step, here], ref[base + step : base + 2 * step, here]], axis=1
                )

            q2 = pair(qkv_ref, 128 * g, 64)
            do2 = pair(do_ref, 128 * g, 64)
            delta2 = pair(delta_ref, 2 * g, 1)
            dq = jnp.zeros((HEAD, 2 * ROWS), F32)
            for j in range(i + 1):
                at = slice(j * ROWS, (j + 1) * ROWS)
                p = prob_ref[TILES.index((g, i, j))]
                ds = low(wide(p) * (mm(values[at], do2) - delta2))
                dq = dq + mm(keys_t[:, at], ds)
                dk_ref[:, at] += mm(q2, ds, NT)
                dv_ref[:, at] += mm(do2, p, NT)
            cos, sin = cos_ref[:, here], sin_ref[:, here]
            dq = dq * 0.125
            for h in range(2):
                a, b = dq[:32, h * ROWS : (h + 1) * ROWS], dq[32:, h * ROWS : (h + 1) * ROWS]
                dqkv_ref[base + 64 * h : base + 64 * h + 32, here] = low(a * cos + b * sin)
                dqkv_ref[base + 64 * h + 32 : base + 64 * h + 64, here] = low(b * cos - a * sin)
        a, b = dk_ref[:32, :], dk_ref[32:, :]
        dqkv_ref[base + 128 : base + 160, :] = low(a * cos_ref[...] + b * sin_ref[...])
        dqkv_ref[base + 160 : base + 192, :] = low(b * cos_ref[...] - a * sin_ref[...])
        dqkv_ref[base + 192 : base + 256, :] = low(dv_ref[...])
        if g == 0:
            for copy in loads[1:6]:
                copy.wait()
        total = jnp.zeros((256, WIDTH), F32)
        for r in range(4):
            at = pl.ds(pl.multiple_of(lax.rem(at_ref[0] + r, 4) * ROWS, 128), ROWS)
            total = total + mm(dqkv_ref[base : base + 256, at], x_ref[r])
        put(g, 0, low(total))
    for copy in loads[6:]:
        copy.wait()
    for copy in moves:
        copy.start()
    for r, copy in enumerate(stores):
        at = pl.ds(pl.multiple_of(lax.rem(at_ref[0] + r, 4) * ROWS, 128), ROWS)
        part_ref[r] = low(mm(dqkv_ref[:256, at].T, wa_ref[...]) + mm(dqkv_ref[256:, at].T, wb_ref[...]))
        copy.start()
    for copy in stores + moves:
        copy.wait()


def attention_backward(at, d_blocks, x_blocks, qkv, o, probs, w_out, wa, wb, cos, sin, small, more):
    smem = pl.BlockSpec(memory_space=pltpu.SMEM)
    vmem = pl.BlockSpec(memory_space=pltpu.VMEM)
    anywhere = pl.BlockSpec(memory_space=pl.ANY)
    return pl.pallas_call(
        attention_backward_kernel,
        out_shape=(
            *[jax.ShapeDtypeStruct((HALF_ROWS, WIDTH), BF)] * 2,
            *[jax.ShapeDtypeStruct((n, WIDTH), BF) for n in (PIECE, PIECE, PIECE // 2, PIECE // 2, PIECE)],
        ),
        in_specs=[smem] + [vmem] * 8 + [anywhere] * 5 + [vmem] * 2 + [anywhere, vmem] + [anywhere] * 2 + [vmem] * 3 + [anywhere],
        out_specs=[vmem] * 2 + [anywhere] * 5,
        scratch_shapes=[
            pltpu.VMEM((256, SEQ), BF),
            pltpu.VMEM((8, SEQ), F32),
            pltpu.VMEM((64, SEQ), F32),
            pltpu.VMEM((64, SEQ), F32),
            pltpu.VMEM((512, SEQ), BF),
            pltpu.VMEM((4, ROWS, WIDTH), BF),
            pltpu.VMEM(probs.shape, BF),
            pltpu.VMEM(wa.shape, BF),
            pltpu.VMEM(wb.shape, BF),
            pltpu.VMEM((4, ROWS, WIDTH), BF),
            pltpu.SemaphoreType.DMA((8,)),
            pltpu.SemaphoreType.DMA((4,)),
            pltpu.SemaphoreType.DMA((5,)),
        ],
        compiler_params=pltpu.CompilerParams(vmem_limit_bytes=32 * MIB),
        cost_estimate=pl.CostEstimate(flops=20_000_000_000, bytes_accessed=15_000_000, transcendentals=3_000_000),
        name="attention_backward",
    )(at, *d_blocks, *x_blocks, qkv, o, probs, w_out, wa, wb, cos, sin, small, more)


def finish_kernel(core_ref, half, other, wa_ref, wb_ref, gq, gk, gv, go, rest):
    core = core_ref[0]

    def unpack(first, second):
        lines = jnp.zeros((1, WIDTH), F32)
        for g, (ref, w_ref) in enumerate(((first, wa_ref), (second, wb_ref))):
            grads = wide(ref[:256, :])
            lines = lines + (grads * wide(w_ref[...])).sum(axis=0, keepdims=True)
            gq[:, 128 * g : 128 * g + 128] = grads[:128].T
            turned = grads[128:].T
            gk[:, 64 * g : 64 * g + 64] = turned[:, :64]
            gv[:, 64 * g : 64 * g + 64] = turned[:, 64:]
            go[128 * g : 128 * g + 128, :] = wide(ref[256:384, :])
        rest[:32, :] = second[384:416, :]
        gains = wide(second[416:418, :]).sum(axis=0, keepdims=True)
        high, high2 = low(gains), low(lines)
        rows = [wide(high), gains - wide(high), wide(high2), lines - wide(high2), jnp.zeros((12, WIDTH), F32)]
        rest[32:, :] = low(jnp.concatenate(rows, axis=0))

    @pl.when(core == 0)
    def _():
        unpack(half, other)

    @pl.when(core != 0)
    def _():
        unpack(other, half)


def finish(core, half, other, wa, wb):
    smem = pl.BlockSpec(memory_space=pltpu.SMEM)
    vmem = pl.BlockSpec(memory_space=pltpu.VMEM)
    return pl.pallas_call(
        finish_kernel,
        out_shape=(
            jax.ShapeDtypeStruct((WIDTH, 256), F32),
            jax.ShapeDtypeStruct((WIDTH, 128), F32),
            jax.ShapeDtypeStruct((WIDTH, 128), F32),
            jax.ShapeDtypeStruct((256, WIDTH), F32),
            jax.ShapeDtypeStruct((48, WIDTH), BF),
        ),
        in_specs=[smem] + [vmem] * 4,
        out_specs=[vmem] * 5,
        compiler_params=pltpu.CompilerParams(vmem_limit_bytes=16 * MIB),
        cost_estimate=pl.CostEstimate(flops=3_000_000, bytes_accessed=6_000_000, transcendentals=0),
        name="finish",
    )(core, half, other, wa, wb)


def hidden_gradient_kernel(*refs):
    sources, (gain, named, w_ref, expert_ref, d_ref, first_ref, second_ref, small_ref), refs = refs[:9], refs[9:17], refs[17:]
    a0, a1, a2, b0, b1, b2, normed, hidden, cot = refs[:9]
    loads = [
        pltpu.make_async_copy(source, target, refs[9].at[k]) for k, (source, target) in enumerate(zip(sources, refs[:9]))
    ]
    for copy in loads:
        copy.start()
    for copy in loads:
        copy.wait()
    in_a = wide(a0[...]) + wide(a1[...]) + wide(a2[...])
    in_b = wide(b0[...]) + wide(b1[...]) + wide(b2[...])
    routed = in_a[ROWS:] + in_b[ROWS:]
    d_route = jnp.concatenate([routed[:, :ROWS], routed[:, ROWS:]], axis=0)
    picked = named[...] > 0.5
    logits = jnp.where(picked, mm(w_ref[...], normed[...], NT), -jnp.inf)
    powers = jnp.where(picked, jnp.exp(logits - logits.max(axis=0, keepdims=True)), 0.0)
    gates = powers / powers.sum(axis=0, keepdims=True)
    d_logits = low(gates * (d_route - (gates * d_route).sum(axis=0, keepdims=True)))
    d_normed = mm(d_logits, w_ref[...], TN) + jnp.concatenate([in_a[:ROWS], in_b[:ROWS]], axis=1)
    x = hidden[...]
    r = norm_scale(x)
    u = d_normed * gain[...]
    d = wide(cot[...]) + r * u - x * (r * r * r * jnp.mean(u * x, axis=1, keepdims=True))
    d_ref[...] = d
    first_ref[...] = low(d[: ROWS // 2])
    second_ref[...] = low(d[ROWS // 2 :])
    small_ref[:32, :] = low(mm(expert_ref[...], low(mm(d_logits, normed[...]))))
    gains = (d_normed * (x * r)).sum(axis=0, keepdims=True)
    high = wide(low(gains))
    small_ref[32:, :] = low(jnp.concatenate([high, gains - high, jnp.zeros((30, WIDTH), F32)], axis=0))


def hidden_gradient(*ins):
    vmem = pl.BlockSpec(memory_space=pltpu.VMEM)
    shapes = ((ROWS, WIDTH), (ROWS // 2, WIDTH), (ROWS // 2, WIDTH), (64, WIDTH))
    return pl.pallas_call(
        hidden_gradient_kernel,
        out_shape=tuple(jax.ShapeDtypeStruct(shape, F32 if k == 0 else BF) for k, shape in enumerate(shapes)),
        in_specs=[pl.BlockSpec(memory_space=pl.ANY)] * 9 + [vmem] * 4,
        out_specs=[vmem] * 4,
        scratch_shapes=[*[pltpu.VMEM(v.shape, v.dtype) for v in ins[:9]], pltpu.SemaphoreType.DMA((9,))],
        compiler_params=pltpu.CompilerParams(vmem_limit_bytes=20 * MIB),
        cost_estimate=pl.CostEstimate(flops=60_000_000, bytes_accessed=6_000_000, transcendentals=10_000),
        name="hidden_gradient",
    )(*ins)


def relay_rows_kernel(plus, minus, first, second, plus_out, minus_out):
    plus_out[...] = add_low(plus[...], first[...])
    minus_out[...] = add_low(minus[...], second[...])


def relay_rows(plus, minus, first, second):
    lower = pl.BlockSpec((PIECE // 2, WIDTH), lambda i: (0, 0))
    upper = pl.BlockSpec((PIECE // 2, WIDTH), lambda i: (1, 0))
    return pl.pallas_call(
        relay_rows_kernel,
        grid=(1,),
        out_shape=(jax.ShapeDtypeStruct((PIECE, WIDTH), BF),) * 2,
        in_specs=[lower, upper, lower, lower],
        out_specs=[lower, upper],
        input_output_aliases={0: 0, 1: 1},
        compiler_params=pltpu.CompilerParams(vmem_limit_bytes=10 * MIB),
        cost_estimate=pl.CostEstimate(flops=300_000, bytes_accessed=1_500_000, transcendentals=0),
        name="relay_rows",
    )(plus, minus, first, second)


SHARD = WIDTH + 512
PACK = 384
PIECE = ROWS + PACK


FAR_STEPS = (((2, 0), (2, 1), (2, 2), (2, 3)), ((0, 2), (1, 2), (3, 2)))
NEAR_STEPS = tuple(tuple((x, z) for z in (0, 1, 3)) for x in (0, 1, 3))
EARLY_STEPS, NEAR_STEPS = NEAR_STEPS[:1], NEAR_STEPS[1:]


def member(pieces, outer, inner):
    if outer == 2:
        return pieces[2 + inner // 2].at[inner % 2]
    return pieces[(0, 1, None, 4)[outer]].at[inner]


def expert_kernel(steps, kept, far, at_ref, *refs):
    ta, tb, (cot_ref, pos_ref, hot_ref, wr_ref), weights, refs = refs[:5], refs[5:10], refs[10:14], refs[14:16], refs[16:]
    refs = refs[kept:]
    stacks, (a0, a1, a4, b0, b1, b4, out_ref), refs = refs[:4], refs[4:11], refs[11:]
    (a2, a3, b2, b3), refs = (refs[:4], refs[4:]) if far else ((None,) * 4, refs)
    da, db = (a0, a1, a2, a3, a4), (b0, b1, b2, b3, b4)
    (tok_scr, cot_scr, wgu_scr, wd_scr, x_scr, dx_scr, act_scr, dgu_scr, g_scr, m_scr, y_scr, p_scr, out_scr), refs = (
        refs[:13], refs[13:],
    )
    w_sem, in_sem, stack_sem, out_sem = refs
    place = wide(lax.broadcasted_iota(jnp.int32, (CAP, ROWS), 0))
    z_of = [lax.rem(at_ref[2] + k, 4) for k in range(4)]
    x_of = [lax.rem(at_ref[3] + k, 4) for k in range(4)]
    chip = at_ref[2] * 4 + at_ref[3]
    first = lax.rem(at_ref[0], 2) == 0
    line = lax.broadcasted_iota(jnp.int32, (16, HALF), 0) == chip
    both = range(2)

    def weight_copies():
        copies = []
        for e, whole in enumerate(weights):
            for r in range(4):
                ref = whole.at[r]
                cols = pl.ds(128 * r, 128)
                moves = [
                    (ref.at[pl.ds(0, WIDTH), pl.ds(0, 128)], wgu_scr.at[e, :, cols]),
                    (ref.at[pl.ds(0, WIDTH), pl.ds(128, 128)], wgu_scr.at[e, :, pl.ds(FF + 128 * r, 128)]),
                ]
                for c in range(4):
                    moves.append((ref.at[pl.ds(WIDTH + 128 * c, 128), :], wd_scr.at[e, cols, pl.ds(256 * c, 256)]))
                for source, target in moves:
                    copies.append(pltpu.make_async_copy(source, target, w_sem.at[len(copies)]))
        return copies

    def in_copies(n):
        copies = []
        for k, (x, z) in enumerate(steps[n]):
            to = tok_scr.at[n % 2, k]
            for source, target in (
                (member(ta, x, z), to.at[:, pl.ds(0, HALF)]),
                (member(tb, z, x), to.at[:, pl.ds(HALF, HALF)]),
                (cot_ref.at[z_of[z], x_of[x], pl.ds(0, ROWS)], cot_scr.at[n % 2, k]),
            ):
                copies.append(pltpu.make_async_copy(source, target, in_sem.at[n % 2, len(copies)]))
        return copies

    def stack_copies(n):
        rows, base = len(steps[n]) * CAP, sum(len(step) for step in steps[:n]) * CAP
        return [
            pltpu.make_async_copy(
                scr.at[n % 2, :, pl.ds(0, rows)], ref.at[:, pl.ds(base, rows)], stack_sem.at[n % 2, i]
            )
            for i, (scr, ref) in enumerate(zip((x_scr, dx_scr, act_scr, dgu_scr), stacks))
        ]

    def out_copies(n):
        copies = []
        for k, (x, z) in enumerate(steps[n]):
            dense = out_scr.at[n % 2, k]
            for source, target in (
                (dense.at[pl.ds(0, EXTRA), pl.ds(0, HALF)], member(da, x, z)),
                (dense.at[pl.ds(0, EXTRA), pl.ds(HALF, HALF)], member(db, z, x)),
                (dense.at[pl.ds(EXTRA, ROWS)], out_ref.at[z_of[z], x_of[x]]),
            ):
                copies.append(pltpu.make_async_copy(source, target, out_sem.at[n % 2, len(copies)]))
        return copies

    for copy in in_copies(0) + weight_copies():
        copy.start()
    for n, step in enumerate(steps):
        slot, count = n % 2, len(step)
        rows = count * CAP
        lane = lax.broadcasted_iota(jnp.int32, (rows, SLOTS), 1)
        for copy in in_copies(n):
            copy.wait()
        if n + 1 < len(steps):
            for copy in in_copies(n + 1):
                copy.start()
        if n >= 2:
            for copy in stack_copies(n - 2) + out_copies(n - 2):
                copy.wait()
        for k, (x, z) in enumerate(step):
            pos = pos_ref[z_of[z], x_of[x]]
            pick = jnp.concatenate([low(wide(place == pos[e : e + 1, :])) for e in both], axis=0)
            p_scr[k] = pick
            xs, gs = low(mm(pick, tok_scr[slot, k])), low(mm(pick, cot_scr[slot, k]))
            ms = mm(pick, hot_ref[z_of[z], x_of[x]], NT)
            for e in both:
                at = slice(k * CAP, (k + 1) * CAP)
                x_scr[slot, e, at, :] = xs[e * CAP : (e + 1) * CAP]
                g_scr[e, at, :] = gs[e * CAP : (e + 1) * CAP]
                m_scr[e, at, :] = ms[e * CAP : (e + 1) * CAP]
        if n == 0:
            for copy in weight_copies():
                copy.wait()
        gu = [mm(x_scr[slot, e, :rows], wgu_scr[e]) for e in both]
        logits = [mm(x_scr[slot, e, :rows], wr_ref[...]) for e in both]
        sig = [jax.nn.sigmoid(gu[e][:, :FF]) for e in both]
        for e in both:
            act_scr[slot, e, :rows] = low(gu[e][:, :FF] * sig[e] * gu[e][:, FF:])
        out = [low(mm(act_scr[slot, e, :rows], wd_scr[e])) for e in both]
        gate = []
        for e in both:
            named = m_scr[e, :rows] > 0.5
            found = jnp.where(named, logits[e], -1e30)
            powers = jnp.where(named, jnp.exp(found - found.max(axis=1, keepdims=True)), 0.0)
            total = powers.sum(axis=1, keepdims=True)
            mine = jnp.where(lane == at_ref[e], powers, 0.0).sum(axis=1, keepdims=True)
            gate.append(mine / jnp.where(total > 0.0, total, 1.0))
            dx_scr[slot, e, :rows] = low(gate[e] * wide(g_scr[e, :rows]))
        d_act = [mm(dx_scr[slot, e, :rows], wd_scr[e], NT) for e in both]
        d_route = []
        for e in both:
            d_route.append((wide(out[e]) * wide(g_scr[e, :rows])).sum(axis=1, keepdims=True))
            y_scr[0, e, :rows] = low(gate[e] * wide(out[e]))
        for e in both:
            pre, up = gu[e][:, :FF], gu[e][:, FF:]
            dgu_scr[slot, e, :rows, :FF] = low(d_act[e] * up * sig[e] * (1.0 + pre * (1.0 - sig[e])))
            dgu_scr[slot, e, :rows, FF:] = low(d_act[e] * (pre * sig[e]))
        for copy in stack_copies(n):
            copy.start()
        for e in both:
            y_scr[1, e, :rows] = low(mm(dgu_scr[slot, e, :rows], wgu_scr[e], NT))
        for k in range(count):
            at = slice(k * CAP, (k + 1) * CAP)
            pick_t = p_scr[k].T
            dense = low(mm(pick_t, jnp.concatenate([y_scr[1, e, at, :] for e in both], axis=0)))
            out_scr[slot, k, :ROWS] = dense
            own, other = [
                (wide(p_scr[k, e * CAP : (e + 1) * CAP, :]) * d_route[e][at]).sum(axis=0, keepdims=True) for e in both
            ]
            pair = jnp.concatenate([jnp.where(first, own, other), jnp.where(first, other, own)], axis=1)
            high = wide(low(pair))
            out_scr[slot, k, ROWS:EXTRA, :HALF] = low(jnp.where(line, high, 0.0))
            out_scr[slot, k, ROWS:EXTRA, HALF:] = low(jnp.where(line, pair - high, 0.0))
            dense = low(mm(pick_t, jnp.concatenate([y_scr[0, e, at, :] for e in both], axis=0)))
            out_scr[slot, k, EXTRA:] = dense
        for copy in out_copies(n):
            copy.start()
    for n in range(max(0, len(steps) - 2), len(steps)):
        for copy in stack_copies(n) + out_copies(n):
            copy.wait()


def experts(steps, at, tok_a, tok_b, cot, pos, hot, w_router, weights, partial=()):
    far = any(2 in member for step in steps for member in step)
    smem = pl.BlockSpec(memory_space=pltpu.SMEM)
    vmem = pl.BlockSpec(memory_space=pltpu.VMEM)
    anywhere = pl.BlockSpec(memory_space=pl.ANY)
    rows, most = sum(len(step) for step in steps) * CAP, max(len(step) for step in steps)
    widths = (WIDTH, WIDTH, FF, 2 * FF)
    ins = (at, *tok_a, *tok_b, cot, pos, hot, w_router, *weights, *partial)
    return pl.pallas_call(
        functools.partial(expert_kernel, steps, len(partial), far),
        out_shape=(
            *[jax.ShapeDtypeStruct((2, rows, width), BF) for width in widths],
            *[jax.ShapeDtypeStruct((4, EXTRA, HALF), BF)] * 6,
            jax.ShapeDtypeStruct((4, 4, ROWS, WIDTH), BF),
            *[jax.ShapeDtypeStruct((2, EXTRA, HALF), BF)] * (4 * far),
        ),
        in_specs=[smem, *[anywhere] * 11, vmem, vmem, vmem, *[anywhere] * (2 + len(partial))],
        out_specs=[anywhere] * (11 + 4 * far),
        scratch_shapes=[
            pltpu.VMEM((2, most, ROWS, WIDTH), BF),
            pltpu.VMEM((2, most, ROWS, WIDTH), BF),
            pltpu.VMEM((2, WIDTH, 2 * FF), BF),
            pltpu.VMEM((2, FF, WIDTH), BF),
            *[pltpu.VMEM((2, 2, most * CAP, width), BF) for width in widths],
            pltpu.VMEM((2, most * CAP, WIDTH), BF),
            pltpu.VMEM((2, most * CAP, SLOTS), F32),
            pltpu.VMEM((2, 2, most * CAP, WIDTH), BF),
            pltpu.VMEM((most, 2 * CAP, ROWS), BF),
            pltpu.VMEM((2, most, EXTRA + ROWS, WIDTH), BF),
            pltpu.SemaphoreType.DMA((48,)),
            pltpu.SemaphoreType.DMA((2, 3 * most)),
            pltpu.SemaphoreType.DMA((2, 4)),
            pltpu.SemaphoreType.DMA((2, 3 * most)),
        ],
        input_output_aliases={17 + k: 4 + k for k in range(len(partial))},
        compiler_params=pltpu.CompilerParams(vmem_limit_bytes=54 * MIB),
        cost_estimate=pl.CostEstimate(flops=rows * 10_000_000, bytes_accessed=rows * 20_000, transcendentals=rows * 1_000),
        name="experts",
    )(*ins)


def expert_gradient_kernel(y_ref, *refs):
    (x, dx, act, dgu), outs = [
        jnp.concatenate([refs[4 * k + i][0] for k in range(3)], axis=0) for i in range(4)
    ], refs[12:]
    gu = low(mm(x.T, dgu))
    gd = low(mm(act, dx, TN))
    for i, ref in enumerate(outs):

        @pl.when(pl.program_id(0) == i)
        def _(ref=ref):
            for r in range(4):
                to = lax.rem(r - y_ref[0] + 4, 4)
                cols = slice(128 * r, 128 * r + 128)
                ref[to, :128, :] = gd[cols, :]
                for k in range(4):
                    part = slice(256 * k, 256 * k + 256)
                    ref[to, 128:, 256 * k : 256 * k + 128] = gu[part, cols]
                    ref[to, 128:, 256 * k + 128 : 256 * k + 256] = gu[part, FF + 128 * r : FF + 128 * r + 128]


def expert_gradients(y, *sets):
    stacks = [v for one in sets for v in one]
    whole = pl.BlockSpec((4, PACK, WIDTH), lambda i: (0, 0, 0))
    return pl.pallas_call(
        expert_gradient_kernel,
        grid=(2,),
        out_shape=(jax.ShapeDtypeStruct((4, PACK, WIDTH), BF),) * 2,
        in_specs=[
            pl.BlockSpec(memory_space=pltpu.SMEM),
            *[pl.BlockSpec((1, *v.shape[1:]), lambda i: (1 - i, 0, 0)) for v in stacks],
        ],
        out_specs=[whole, whole],
        compiler_params=pltpu.CompilerParams(vmem_limit_bytes=VMEM),
        cost_estimate=pl.CostEstimate(flops=18_000_000_000, bytes_accessed=28_000_000, transcendentals=0),
        name="expert_gradients",
    )(y, *stacks)


def merge_kernel(a_ref, b_ref, out):
    out[...] = add_low(a_ref[...], b_ref[...])


def merge(a, b):
    spec = pl.BlockSpec((1, PACK, WIDTH), lambda i: (i, 0, 0))
    return pl.pallas_call(
        merge_kernel,
        grid=(4,),
        out_shape=jax.ShapeDtypeStruct(a.shape, BF),
        in_specs=[spec] * 2,
        out_specs=spec,
        compiler_params=pltpu.CompilerParams(vmem_limit_bytes=10 * MIB),
        cost_estimate=pl.CostEstimate(flops=2_000_000, bytes_accessed=10_000_000, transcendentals=0),
        name="merge",
    )(a, b)


def token_gradient_kernel(own, plus, minus, tokens, gain, d_hidden, d_tokens, gate, up, down):
    def total(first, last):
        return wide(own[first:last]) + wide(plus[first:last]) + wide(minus[first:last])

    x = wide(tokens[...])
    r = norm_scale(x)
    u = total(0, ROWS) * gain[...]
    d_tokens[...] = d_hidden[...] + r * u - x * (r * r * r * jnp.mean(u * x, axis=1, keepdims=True))
    down[0] = total(ROWS, ROWS + 128)
    packed = total(ROWS + 128, PIECE)
    for k in range(4):
        gate[0, 256 * k : 256 * k + 256, :] = packed[:, 256 * k : 256 * k + 128]
        up[0, 256 * k : 256 * k + 256, :] = packed[:, 256 * k + 128 : 256 * k + 256]


def token_gradient(*ins):
    vmem = pl.BlockSpec(memory_space=pltpu.VMEM)
    return pl.pallas_call(
        token_gradient_kernel,
        out_shape=(
            jax.ShapeDtypeStruct((ROWS, WIDTH), F32),
            jax.ShapeDtypeStruct((1, WIDTH, 128), F32),
            jax.ShapeDtypeStruct((1, WIDTH, 128), F32),
            jax.ShapeDtypeStruct((1, 128, WIDTH), F32),
        ),
        in_specs=[vmem] * 6,
        out_specs=[vmem] * 4,
        compiler_params=pltpu.CompilerParams(vmem_limit_bytes=20 * MIB),
        cost_estimate=pl.CostEstimate(flops=6_000_000, bytes_accessed=9_000_000, transcendentals=0),
        name="token_gradient",
    )(*ins)


def after(value, *others):
    return lax.optimization_barrier((value, *others))[0]


def norm_scale(x):
    return lax.rsqrt(jnp.mean(x * x, axis=-1, keepdims=True) + NORM_EPS)


def shards(
    tokens, cotangent, gain_attn, w_query, w_key, w_value, w_out, gain_moe, w_router,
    w_gate, w_up, w_down, routes, owner_map,
):
    dp = lax.axis_index("dp")
    y = lax.axis_index("tensor").astype(jnp.int32).reshape(1)
    z_at, x_at, core = ring_position(dp)

    x_in = wide(tokens)
    scale_a = norm_scale(x_in)
    normed_a = low(x_in * scale_a * gain_attn)
    x_blocks = (normed_a, *gather_direct(normed_a, from_y))

    slot_ids = jnp.arange(SLOTS, dtype=jnp.int32)
    picks = routes[:, :, None] == slot_ids[None, None, :]
    route_slots = jnp.sum(jnp.where(picks, owner_map[None, None, :], 0), axis=-1)
    hot = low(jnp.any(route_slots.T[:, None, :] == slot_ids[None, :, None], axis=0))
    row_slots = jnp.concatenate([slot_ids[0::2], slot_ids[1::2]])
    named = wide(jnp.any(route_slots.T[:, None, :] == row_slots[None, :, None], axis=0))
    row_experts = low(row_slots[:, None] == owner_map[None, :])
    router_by_row = low(mm(row_experts, w_router, NT))

    sent = jnp.concatenate([cotangent, hot.reshape(8, WIDTH), jnp.zeros((8, WIDTH), BF)], axis=0)
    cot = lax.all_gather(sent, "dp", axis=0, axis_index_groups=PLANE).reshape(4, 4, EXTRA, WIDTH)

    half = HEAD // 2
    inv_freq = jnp.exp(jnp.arange(half).astype(F32) * (-2.0 * math.log(10000.0) / HEAD))
    angles = inv_freq[:, None] * jnp.arange(SEQ).astype(F32)[None, :]
    cos, sin = jnp.cos(angles), jnp.sin(angles)
    w_cat_t = jnp.concatenate([w_query, w_key, w_value], axis=1).T

    qkv, o_t, lse, *parts = attention_forward(y, x_blocks, w_cat_t, w_out, cos, sin)
    hidden = x_in + sum_direct(*parts, from_y)
    normed_m = low(hidden * norm_scale(hidden) * gain_moe)

    down = w_down[0].reshape(128, 4, 256).transpose(1, 0, 2).reshape(512, 256)
    shard = jnp.concatenate([jnp.concatenate([w_gate[0], w_up[0]], axis=1), down], axis=0)
    w_own = lax.all_gather(shard, "tensor", axis=0)
    tok_a, tok_b = plane_gather_first(normed_m)
    wa = jnp.concatenate([w_cat_t[:128], w_cat_t[256:320], w_cat_t[384:448]], axis=0)
    wb = jnp.concatenate([w_cat_t[128:256], w_cat_t[320:384], w_cat_t[448:]], axis=0)
    row_experts_t = row_experts.T
    tok_a, tok_b, cot, named, router_by_row, row_experts_t, wa, wb = lax.optimization_barrier(
        (tok_a, tok_b, cot, named, router_by_row, row_experts_t, wa, wb)
    )
    hot_all = cot[:, :, ROWS : ROWS + 8].reshape(4, 4, SLOTS, ROWS)
    at = jnp.stack([dp, dp + 1 - 2 * core, z_at, x_at]).astype(jnp.int32)
    mine = jnp.concatenate([lax.dynamic_slice_in_dim(hot_all, at[e], 1, 2) for e in range(2)], axis=2)
    before = low(jnp.arange(ROWS)[:, None] < jnp.arange(ROWS)[None, :])
    rank = jnp.dot(mine.reshape(-1, ROWS), before, preferred_element_type=F32).reshape(mine.shape)
    pos = jnp.where(mine > 0, rank, -1.0)
    by_slot = low(owner_map[:, None] == slot_ids[None, :])
    router_by_slot = low(jnp.dot(w_router, by_slot, preferred_element_type=F32))
    *near, hot_all, at, pos, router_by_slot = lax.optimization_barrier(
        (*plane_gather_second(tok_a, tok_b), hot_all, at, pos, router_by_slot)
    )
    pieces = split(*near)
    far = plane_gather_last(*pieces)
    w_own = after(w_own, *pieces)
    weights = w_own, from_core(w_own)
    table = (cot, pos, hot_all, router_by_slot, weights)
    feeds_early = (at, (tok_a, near[0], *pieces[:2], near[2]), (tok_b, near[1], *pieces[:2], near[3]), *table)
    feeds = (at, (tok_a, near[0], far[0], far[2], near[2]), (tok_b, near[1], far[1], far[3], near[3]), *table)
    early = experts(EARLY_STEPS, *feeds_early)
    outer = experts(FAR_STEPS, *feeds, early[4:])
    a2, a3, b2, b3 = outer[11:]
    far = first_sums((None, None, a2, a3), (None, None, b2, b3))
    near = experts(NEAR_STEPS, *feeds, outer[4:11])
    a0, a1, a4, b0, b1, b4, weighted = near[4:]
    di_a, di_b = (a0, a1, a2, a3, a4), (b0, b1, b2, b3, b4)
    *far, first_stack = lax.optimization_barrier((*far, near[0]))
    relayed = second_sums(di_a, di_b, far)
    other, own = expert_gradients(y, early[:4], outer[:4], (first_stack, *near[1:4]))
    *relayed, other, own = lax.optimization_barrier((*relayed, other, own))
    qa, qb, ra, rb = relayed
    terms = di_a[0], qa, ra, di_b[0], qb, rb
    a2, a3, b2, b3 = fold(1, *terms)
    far = from_z(a2, -1), from_x(b2, -1)
    minus = from_z(a3, 1), from_x(b3, 1)
    a0, a1, b0, b1 = fold(0, *terms)
    both = merge(own, from_core(other))
    *far, both = lax.optimization_barrier((*far, *minus, both))
    far, minus = far[:2], far[2:]
    last = from_z(add_low(a1, far[0]), -1), from_x(add_low(b1, far[1]), -1)
    terms = (a0, minus[0], last[0], b0, minus[1], last[1])
    d_hidden, d_first, d_second, small = hidden_gradient(
        *terms, normed_m, hidden, cotangent, gain_moe[None], named, router_by_row, row_experts_t
    )
    d_blocks = gather_halves(d_first, d_second)

    weighted = after(weighted, *last)
    returned = lax.psum_scatter(
        weighted.reshape(16 * ROWS, WIDTH), "dp", scatter_dimension=0, axis_index_groups=PLANE, tiled=True
    )

    core_at = core.astype(jnp.int32).reshape(1)
    probs = probabilities(after(qkv, d_first), lse)
    keep, send, *d_parts = attention_backward(
        jnp.concatenate([y, core_at]), d_blocks, x_blocks, qkv, o_t, probs, w_out, wa, wb, cos, sin, small, both
    )

    x_index = x_at.astype(jnp.int32).reshape(1)
    far = from_y(d_parts[2], -1), from_y(d_parts[3], 1)
    blocks = dp_spread(x_index, keep, from_core(send))
    s = wide(blocks[0]) + wide(from_x(blocks[2], 2)) + wide(from_x(blocks[1], -1)) + wide(from_x(blocks[3], 1))
    *far, s = lax.optimization_barrier((*far, low(s)))
    plus, minus = relay_rows(d_parts[1], d_parts[4], *far)
    plus, minus = from_y(plus, -1), from_y(minus, 1)
    s = plane_exchange(s)
    half_sum, (plus, minus) = dp_collect(x_index, s, (plus, minus))
    half_sum, returned = lax.optimization_barrier((half_sum, returned))
    g_query, g_key, g_value, g_out, rest = finish(core_at, half_sum, from_core(half_sum), wa, wb)
    plus, minus = lax.optimization_barrier((plus, minus, rest))[:2]
    grads = token_gradient(d_parts[0], plus, minus, tokens, gain_attn[None], d_hidden)
    rest = (rest, *[from_y(rest, d) for d in (1, 2, 3)])
    *rest, d_tokens, g_gate, g_up, g_down = lax.optimization_barrier((*rest, *grads))
    g_router, g_gain_moe, g_gain_attn = totals(*rest, gain_attn[None])
    mixed = low(hidden + wide(returned))
    return (
        mixed, d_tokens, g_gain_attn[0], g_query, g_key, g_value, g_out, g_gain_moe[0], g_router.T,
        g_gate, g_up, g_down,
    )


def solution(mesh):
    both = P(("dp", "tensor"), None)
    in_specs = (
        both, both, P(), P(None, "tensor"), P(None, "tensor"), P(None, "tensor"), P("tensor", None), P(), P(),
        P("dp", None, "tensor"), P("dp", None, "tensor"), P("dp", "tensor", None), both, P(),
    )
    out_specs = (
        both, both, P(), P(None, "tensor"), P(None, "tensor"), P(None, "tensor"), P("tensor", None), P(), P(),
        P("dp", None, "tensor"), P("dp", None, "tensor"), P("dp", "tensor", None),
    )
    return jax.shard_map(shards, mesh=mesh, in_specs=in_specs, out_specs=out_specs, check_vma=False)
```
